32 devices in a mesh: dp: 8 (over z, x), vocab: 4 (over y, core).
Axes of the slice: x: 2, y: 2, z: 4, core: 2. Of those that a mesh axis runs over, the one named last changes fastest.
Arguments:
- token_ids: int32 [64, 2, 64], P('dp'), may hold values from 0 to 31999
- lengths: int32 [64, 2], P('dp'), may hold values from 32 to 64
- comp_mask: int32 [64, 2, 16], P('dp'), may hold values 0 or 1
- ref_logp: float32 [64, 2], P('dp'), may hold values from -240 to 240
- owner: int32 [32], replicated, may hold values from 0 to 31, as said below
- blocks: float32 [32, 768, 384], P('dp', 'vocab')
- left_stat: float32 [32, 768, 768], P('dp'), as said below
- right_stat: float32 [32, 384, 384], P('dp'), as said below
- left_root: float32 [32, 768, 768], P('dp')
- right_root: float32 [32, 384, 384], P('dp')
- tables: float32 [2, 32000, 768], P(None, ('vocab', 'dp'))
- table_moment: float32 [2, 32000, 768], P(None, ('vocab', 'dp')), may hold values from -0.00096 to 0.00096
- table_second: float32 [2, 32000, 768], P(None, ('vocab', 'dp')), may hold values from 2.56e-09 to 1.024e-08
- gains: float32 [3, 768], replicated, may hold values from 0.5 to 1.5
- gain_moment: float32 [3, 768], replicated, may hold values from -0.0384 to 0.0384
- gain_second: float32 [3, 768], replicated, may hold values from 4.096e-06 to 1.6384e-05
Outputs:
- new_blocks: float32 [32, 768, 384], P('dp', 'vocab')
- block_grads: float32 [32, 768, 384], P('dp', 'vocab')
- new_left: float32 [32, 768, 768], P('dp')
- new_right: float32 [32, 384, 384], P('dp')
- new_tables: float32 [2, 32000, 768], P(None, ('vocab', 'dp'))
- new_table_moment: float32 [2, 32000, 768], P(None, ('vocab', 'dp'))
- new_table_second: float32 [2, 32000, 768], P(None, ('vocab', 'dp'))
- new_gains: float32 [3, 768], replicated
- new_gain_moment: float32 [3, 768], replicated
- new_gain_second: float32 [3, 768], replicated
- loss_sum: float32 [], replicated
The draws below stay inside these ranges and needn't reach their ends.
Inputs may be any that keep to these rules, and one draw needn't show every extreme that they name: `owner`: each slot number appears once. `left_stat`: symmetric positive definite. `right_stat`: symmetric positive definite.
All inputs are finite; a program needn't handle non-finite values. No bound on the sum of `comp_mask` on one device may be relied on, other than what follows from the above.
Results may differ from the reference program's by a relative error of at most 0.02.
Values may be sent and summed in bfloat16 or wider, within the bound.
No kernel may reach another device: no remote copies, remote signals or barrier semaphores. Data moves between devices by JAX's collectives and lax.ppermute only.
A program may use at most 320 MiB of HBM per device.

```python
import math
import jax
import jax.numpy as jnp
import numpy as np
from jax import lax

D = 768
HEADS = 12
HDIM = 64
FF = 3072
VOCAB = 32000
SLOT = 64
CMP = 16
STEP = 10
BC = 384
NBLK = 32
PAIRS = 64


def dealing(key):
    return jax.random.permutation(jax.random.fold_in(key, 7), NBLK).astype(jnp.int32)


def draw_owner(key, part):
    return dealing(key)


def draw_blocks(key, part):
    slots = dealing(key)
    key = jax.random.fold_in(key, 11)
    col_blocks = D // BC
    ff_blocks = FF // BC
    number = jnp.arange(NBLK)
    narrow = D ** (-0.5)
    scale = jnp.where(number < 3 * col_blocks, narrow, jnp.where(number < 4 * col_blocks, (SLOT / 4.0) ** 0.5 * narrow, jnp.where(number < 4 * col_blocks + 2 * ff_blocks, narrow, FF ** (-0.5))))
    slot_scale = jnp.zeros((NBLK,), jnp.float32).at[slots].set(scale.astype(jnp.float32))
    return jax.random.normal(key, (NBLK, D, BC), jnp.float32) * slot_scale[:, None, None]


def symmetric(key, width, level, low_end, high_end):
    diag_key, noise_key = jax.random.split(key)
    diagonal = level * jnp.exp(jax.random.uniform(diag_key, (NBLK, width), jnp.float32, math.log(low_end), math.log(high_end)))
    noise = jax.random.normal(noise_key, (NBLK, width, width), jnp.float32) * (0.3 * level / width ** 0.5)
    noise = (noise + jnp.swapaxes(noise, 1, 2)) * 0.7071
    return noise + diagonal[:, :, None] * jnp.eye(width, dtype=jnp.float32)[None]


def grad_level():
    return 0.002 * (PAIRS * CMP) ** 0.5


def draw_left_stat(key, part):
    key = jax.random.fold_in(key, 21)
    return symmetric(key, D, BC * grad_level() ** 2, 1.0, 4.0)


def draw_right_stat(key, part):
    key = jax.random.fold_in(key, 22)
    return symmetric(key, BC, D * grad_level() ** 2, 1.0, 4.0)


def draw_left_root(key, part):
    key = jax.random.fold_in(key, 23)
    return symmetric(key, D, (BC * grad_level() ** 2) ** (-0.25), 0.7, 1.4)


def draw_right_root(key, part):
    key = jax.random.fold_in(key, 24)
    return symmetric(key, BC, (D * grad_level() ** 2) ** (-0.25), 0.7, 1.4)


def draw_tables(key, part):
    key = jax.random.fold_in(key, 31)
    embed_key, head_key = jax.random.split(key)
    rising = 1.0 + 2.0 * jnp.arange(VOCAB).astype(jnp.float32) / VOCAB
    embed_rows = jax.random.normal(embed_key, (VOCAB, D), jnp.float32)
    head_rows = jax.random.normal(head_key, (VOCAB, D), jnp.float32)
    head_rows = head_rows * D ** (-0.5) * rising[:, None]
    return jnp.stack([embed_rows, head_rows])


def draw_lengths(key, part):
    key = jax.random.fold_in(key, 41)
    values = jax.random.randint(key, (PAIRS, 2), SLOT // 2, SLOT + 1)
    return values.at[0, 0].set(SLOT).at[0, 1].set(SLOT // 2).astype(jnp.int32)


def touch_ends(entries, key, least, top_value):
    longest = entries.shape.index(max(entries.shape))
    spots = []
    for shift in (0, 1):
        where = [jax.random.randint(jax.random.fold_in(key, axis), (), 0, length) for axis, length in enumerate(entries.shape)]
        where[longest] = (where[longest] + shift) % entries.shape[longest]
        spots.append(tuple(where))
    return entries.at[spots[0]].set(least).at[spots[1]].set(top_value)


def steps_of(own_key, dims, cuts, low, top_value):
    def one(axis_at, shards_of):
        draws = jax.random.uniform(jax.random.fold_in(jax.random.fold_in(own_key, 6), axis_at), (shards_of,), jnp.float32, low / len(cuts), top_value / len(cuts))
        return jnp.repeat(jnp.exp(draws), dims[axis_at] // shards_of).reshape((-1,) + (1,) * (len(dims) - axis_at - 1))

    level = one(*cuts[0])
    for cut in cuts[1:]:
        level = level * one(*cut)
    return level


def cumulative_ranks(number_of, skew):
    portions = [(1 << 20) // math.isqrt(rank ** skew) + 1 for rank in range(1, number_of + 1)]
    spread = 1 + sum(portions) // (1 << 30)
    return np.cumsum(np.array([max(1, weight // spread) for weight in portions]))


def ranked(stream_key, shape, count, slope):
    table = cumulative_ranks(count, slope)
    ticket = jax.random.randint(jax.random.fold_in(stream_key, 1), shape, 0, int(table[count - 1]))
    rank = jnp.searchsorted(jnp.asarray(table, jnp.int32), ticket, side="right")
    return jax.random.permutation(jax.random.fold_in(stream_key, 2), count)[rank].astype(jnp.int32)


def gaussian(stream_key, shape, spread, limit, shards=(), kind=jnp.bfloat16):
    level = steps_of(stream_key, shape, shards, -0.22, 0.18) if shards else 1.0
    result = jax.random.normal(stream_key, shape, jnp.float32) * spread * level
    return jnp.minimum(jnp.maximum(result, -limit), limit).astype(kind)


def setup_inputs(seed: int = 0) -> dict:
    streams_of = jax.random.split(jax.random.key(seed), 17)
    return {
        "token_ids": touch_ends(ranked(streams_of[0], (PAIRS, 2, SLOT), VOCAB, 2), jax.random.fold_in(streams_of[0], 3), 0, VOCAB - 1).astype(jnp.int32),
        "lengths": draw_lengths(jax.random.fold_in(streams_of[16], 71), 0),
        "comp_mask": touch_ends((jax.random.randint(streams_of[2], (PAIRS, 2, CMP), 0, 4) < 3).astype(jnp.int32), jax.random.fold_in(streams_of[2], 1), 0, 1),
        "ref_logp": gaussian(streams_of[3], (PAIRS, 2), 40.0, 240.0, ((0, 8),), jnp.float32),
        "owner": draw_owner(jax.random.fold_in(streams_of[16], 71), 0),
        "blocks": draw_blocks(jax.random.fold_in(streams_of[16], 71), 0),
        "left_stat": draw_left_stat(jax.random.fold_in(streams_of[16], 71), 0),
        "right_stat": draw_right_stat(jax.random.fold_in(streams_of[16], 71), 0),
        "left_root": draw_left_root(jax.random.fold_in(streams_of[16], 71), 0),
        "right_root": draw_right_root(jax.random.fold_in(streams_of[16], 71), 0),
        "tables": draw_tables(jax.random.fold_in(streams_of[16], 71), 0),
        "table_moment": gaussian(streams_of[11], (2, VOCAB, D), (2e-5 * PAIRS ** 0.5), 0.00096, ((1, 32),), jnp.float32),
        "table_second": jnp.clip(jnp.exp(math.log(1.023999995908298e-08) - 1.3862944 * jax.random.uniform(streams_of[12], (2, VOCAB, D), jnp.float32) ** steps_of(streams_of[12], (2, VOCAB, D), ((1, 32),), -0.2, 0.2)), 2.559999989770745e-09, 1.023999995908298e-08),
        "gains": jnp.clip(1.0 + 0.1 * jax.random.normal(streams_of[13], (3, D), jnp.float32), 0.5, 1.5),
        "gain_moment": gaussian(streams_of[14], (3, D), (1e-4 * (PAIRS * SLOT) ** 0.5), 0.0384, (), jnp.float32),
        "gain_second": jnp.clip(jnp.exp(jax.random.uniform(streams_of[15], (3, D), jnp.float32, math.log(4.095999884157209e-06), math.log(1.6383999536628835e-05))), 4.095999884157209e-06, 1.6383999536628835e-05),
    }


@jax.custom_vjp
def low(v):
    return lax.optimization_barrier(v.astype(jnp.bfloat16)).astype(jnp.float32)

@jax.custom_vjp
def low_back(v):
    return v

def low_keep(v):
    return (low(v), None)

def low_pass(kept, grad):
    return (grad,)

def back_keep(v):
    return (v, None)

def back_low(kept, grad):
    return (low(grad),)
low.defvjp(low_keep, low_pass)
low_back.defvjp(back_keep, back_low)
NORM_EPS = 1e-05
DPO_BETA = 0.02
ROPE_BASE = 10000.0
ADAM_ONE = 0.9
ADAM_TWO = 0.999
ADAM_EPS = 1e-08
WEIGHT_DECAY = 0.01
GAIN_RATE = 0.3
STAT_DECAY = 0.5
SHAMPOO_RATE = 0.5
MASKED = -1e+30

def matmul_hi(left, right):
    return jnp.matmul(left, right, precision=lax.Precision.HIGHEST)

def rms_norm(values, gain):
    return values * lax.rsqrt(lax.optimization_barrier(jnp.mean(values * values, axis=-1, keepdims=True)) + NORM_EPS) * gain

def angles():
    inv_freq = ROPE_BASE ** (-jnp.arange(HDIM // 2).astype(jnp.float32) * 2.0 / HDIM)
    phase_grid = jnp.arange(SLOT).astype(jnp.float32)[:, None] * inv_freq[None, :]
    return (jnp.cos(phase_grid), jnp.sin(phase_grid))

def rotate(values, cosine, sine):
    half_dim = HDIM // 2
    lead_half = values[..., :half_dim]
    tail_half = values[..., half_dim:]
    cos_grid = cosine[None, :, None, :]
    sin_grid = sine[None, :, None, :]
    return jnp.concatenate([lead_half * cos_grid - tail_half * sin_grid, tail_half * cos_grid + lead_half * sin_grid], axis=-1)

def matrices(weights):
    col_blocks = D // BC
    ff_blocks = FF // BC

    def joined(start_at, number):
        return jnp.concatenate([weights[start_at + j] for j in range(number)], axis=1)
    w_query = joined(0, col_blocks)
    w_key = joined(col_blocks, col_blocks)
    w_value = joined(2 * col_blocks, col_blocks)
    w_out = joined(3 * col_blocks, col_blocks)
    w_gate = joined(4 * col_blocks, ff_blocks)
    w_up = joined(4 * col_blocks + ff_blocks, ff_blocks)
    base_down = 4 * col_blocks + 2 * ff_blocks
    w_down = jnp.concatenate([joined(base_down + r * col_blocks, col_blocks) for r in range(FF // D)], axis=0)
    return (w_query, w_key, w_value, w_out, w_gate, w_up, w_down)

def group_loss(params, group_ids, group_lens, group_mask, group_ref):
    tables, gains, real_blocks = params
    table_low = low(tables)
    w_query, w_key, w_value, w_out, w_gate, w_up, w_down = matrices(low(real_blocks))
    seq_count = group_ids.shape[0] * 2
    flat_ids = group_ids.reshape(seq_count, SLOT)
    inputs = jnp.take(table_low[0], flat_ids.reshape(-1), axis=0).reshape(seq_count, SLOT, D)
    cosine, sine = angles()

    def to_heads(values):
        return values.reshape(seq_count, SLOT, HEADS, HDIM)
    normed = low(rms_norm(inputs, gains[0]))
    q_rot = low(rotate(to_heads(low_back(matmul_hi(normed, w_query))), cosine, sine))
    k_rot = low(rotate(to_heads(low_back(matmul_hi(normed, w_key))), cosine, sine))
    v_heads = low(to_heads(low_back(matmul_hi(normed, w_value))))
    scores = jnp.einsum('nqhd,nkhd->nhqk', q_rot, k_rot, precision=lax.Precision.HIGHEST) / math.sqrt(HDIM)
    scores = low_back(scores)
    len_vec = group_lens.reshape(seq_count)
    places = jnp.arange(SLOT)
    valid = (places[None, :] <= places[:, None])[None, None] & (places[None, None, None, :] < len_vec[:, None, None, None])
    scores = jnp.where(valid, scores, MASKED)
    p_low = low(jax.nn.softmax(scores, axis=-1))
    att_out = jnp.einsum('nhqk,nkhd->nqhd', p_low, v_heads, precision=lax.Precision.HIGHEST).reshape(seq_count, SLOT, D)
    att_out = low(low_back(att_out))
    h_mid = inputs + low_back(matmul_hi(att_out, w_out))
    b_low = low(rms_norm(h_mid, gains[1]))
    gate_pre = low_back(matmul_hi(b_low, w_gate))
    up_pre = low_back(matmul_hi(b_low, w_up))
    mix_low = low(jax.nn.silu(gate_pre) * up_pre)
    h_out = h_mid + low_back(matmul_hi(mix_low, w_down))
    positions = len_vec[:, None] - 1 - CMP + jnp.arange(CMP)[None, :]
    picked_rows = jnp.take_along_axis(h_out, positions[:, :, None], axis=1)
    target = jnp.take_along_axis(flat_ids, positions + 1, axis=1)
    c_low = low(rms_norm(picked_rows, gains[2]))
    logits = low_back(matmul_hi(c_low, table_low[1].T))
    log_total = jax.nn.logsumexp(logits, axis=-1)
    picked = jnp.take_along_axis(logits, target[:, :, None], axis=2)[:, :, 0]
    weights_mask = group_mask.reshape(seq_count, CMP).astype(jnp.float32)
    seq_logp = lax.optimization_barrier(jnp.sum((picked - log_total) * weights_mask, axis=1)).reshape(-1, 2)
    margin = DPO_BETA * (seq_logp[:, 0] - group_ref[:, 0] - (seq_logp[:, 1] - group_ref[:, 1]))
    return jnp.sum(jax.nn.softplus(-margin))

def adam_step(weight, grad, moment, second, rate):
    moment = ADAM_ONE * moment + (1.0 - ADAM_ONE) * grad
    second = ADAM_TWO * second + (1.0 - ADAM_TWO) * grad * grad
    ratio = moment / (1.0 - ADAM_ONE ** STEP) / (jnp.sqrt(second / (1.0 - ADAM_TWO ** STEP)) + ADAM_EPS)
    return (weight - rate * (ratio + WEIGHT_DECAY * weight), moment, second)

def reference(token_ids, lengths, comp_mask, ref_logp, owner, blocks, left_stat, right_stat, left_root, right_root, tables, table_moment, table_second, gains, gain_moment, gain_second):
    real_blocks = jnp.take(blocks, owner, axis=0)
    params = (tables, gains, real_blocks)
    group = math.gcd(PAIRS, max(1, 4096 // (2 * SLOT)))
    rounds = PAIRS // group

    def split(values):
        return values.reshape((rounds, group) + values.shape[1:])

    def group_step(carry, item):
        group_ids, group_lens, group_mask, group_ref = item
        value, pull = jax.vjp(lambda params_in: group_loss(params_in, group_ids, group_lens, group_mask, group_ref), params)
        grads = pull(jnp.ones((), value.dtype))[0]
        return ((carry[0] + value, jax.tree.map(jnp.add, carry[1], grads)), None)
    start = (jnp.zeros((), tables.dtype), jax.tree.map(jnp.zeros_like, params))
    (loss_sum, (grad_tables, grad_gains, grad_real)), _ = lax.scan(group_step, start, (split(token_ids), split(lengths), split(comp_mask), split(ref_logp)))
    block_grads = jnp.zeros_like(blocks).at[owner].set(grad_real)
    highest = lax.Precision.HIGHEST
    new_left = STAT_DECAY * left_stat + (1.0 - STAT_DECAY) * jnp.einsum('bij,bkj->bik', block_grads, block_grads, precision=highest)
    new_right = STAT_DECAY * right_stat + (1.0 - STAT_DECAY) * jnp.einsum('bji,bjk->bik', block_grads, block_grads, precision=highest)
    direction = jnp.einsum('bij,bjk->bik', left_root, block_grads, precision=highest)
    direction = jnp.einsum('bij,bjk->bik', direction, right_root, precision=highest)
    new_blocks = blocks - SHAMPOO_RATE * direction
    rates = jnp.array([0.3, 0.02], tables.dtype)[:, None, None]
    new_tables, new_table_moment, new_table_second = adam_step(tables, grad_tables, table_moment, table_second, rates)
    new_gains, new_gain_moment, new_gain_second = adam_step(gains, grad_gains, gain_moment, gain_second, GAIN_RATE)
    return (new_blocks, block_grads, new_left, new_right, new_tables, new_table_moment, new_table_second, new_gains, new_gain_moment, new_gain_second, loss_sum)
```

```python
import functools
import math

import jax
import jax.numpy as jnp
from jax import lax
from jax.experimental import pallas as pl
from jax.experimental.pallas import tpu as pltpu
from jax.sharding import Mesh
from jax.sharding import PartitionSpec as P

D = 768
HEADS = 12
HDIM = 64
FF = 3072
SLOT = 64
MB = 2
CMP = 16
STEP = 10
BC = 384
NBLK = 32


NORM_EPS = 1e-05
DPO_BETA = 0.02
ROPE_BASE = 10000.0
ADAM_ONE = 0.9
ADAM_TWO = 0.999
ADAM_EPS = 1e-08
WEIGHT_DECAY = 0.01
GAIN_RATE = 0.3
STAT_DECAY = 0.5
SHAMPOO_RATE = 0.5
MASKED = -1e30


def joined(value, axis, join):
    pieces = jax.tree.map(lambda part: lax.all_gather(part, axis), value)
    head = jax.tree.map(lambda part: part[0], pieces)
    tail = jax.tree.map(lambda part: part[1:], pieces)
    so_far, _ = lax.scan(lambda so_far, section: (join(so_far, section), None), head, tail)
    return so_far


def mult(left, right):
    return jnp.dot(left, right, preferred_element_type=jnp.float32)


def mult_t(left, right):
    return lax.dot_general(
        left, right, (((0,), (0,)), ((), ())), preferred_element_type=jnp.float32
    )


def mult_nt(left, right):
    return lax.dot_general(
        left, right, (((1,), (1,)), ((), ())), preferred_element_type=jnp.float32
    )


def project(rows, group):
    product = jnp.einsum("td,ndk->tnk", rows, group, preferred_element_type=jnp.float32)
    return product.reshape(rows.shape[0], group.shape[0] * BC)


def project_back(grad, group):
    return jnp.einsum(
        "tnk,ndk->td",
        grad.reshape(grad.shape[0], group.shape[0], BC),
        group,
        preferred_element_type=jnp.float32,
    )


def block_grad(rows, grad, number):
    return jnp.einsum(
        "td,tnk->ndk",
        rows,
        grad.reshape(grad.shape[0], number, BC),
        preferred_element_type=jnp.float32,
    )


def down_forward(mix, down):
    row_total = mix.shape[0]
    product = jnp.einsum(
        "trd,rjdk->tjk",
        mix.reshape(row_total, FF // D, D),
        down.reshape(FF // D, D // BC, D, BC),
        preferred_element_type=jnp.float32,
    )
    return product.reshape(row_total, D)


def down_back(grad, down):
    row_total = grad.shape[0]
    product = jnp.einsum(
        "tjk,rjdk->trd",
        grad.reshape(row_total, D // BC, BC),
        down.reshape(FF // D, D // BC, D, BC),
        preferred_element_type=jnp.float32,
    )
    return product.reshape(row_total, FF)


def down_grad(mix, grad):
    row_total = mix.shape[0]
    product = jnp.einsum(
        "trd,tjk->rjdk",
        mix.reshape(row_total, FF // D, D),
        grad.reshape(row_total, D // BC, BC),
        preferred_element_type=jnp.float32,
    )
    return product.reshape(-1, D, BC)


def groups(weights):
    col_blocks = D // BC
    ff_blocks = FF // BC
    base_gate = 4 * col_blocks
    return (
        weights[0:col_blocks],
        weights[col_blocks : 2 * col_blocks],
        weights[2 * col_blocks : 3 * col_blocks],
        weights[3 * col_blocks : base_gate],
        weights[base_gate : base_gate + ff_blocks],
        weights[base_gate + ff_blocks : base_gate + 2 * ff_blocks],
        weights[base_gate + 2 * ff_blocks :],
    )


def rms_forward(values, gain):
    return values * lax.rsqrt(jnp.mean(values * values, axis=-1, keepdims=True) + NORM_EPS) * gain


def rms_backward(values, gain, grad):
    scale = lax.rsqrt(jnp.mean(values * values, axis=-1, keepdims=True) + NORM_EPS)
    inner = jnp.mean(values * gain * grad, axis=-1, keepdims=True)
    back = scale * gain * grad - values * scale**3 * inner
    return (back, jnp.sum(grad * values * scale, axis=0))


def angles():
    inv_freq = ROPE_BASE ** (-jnp.arange(HDIM // 2).astype(jnp.float32) * 2.0 / HDIM)
    phase_grid = jnp.arange(SLOT).astype(jnp.float32)[:, None] * inv_freq[None, :]
    return (jnp.cos(phase_grid), jnp.sin(phase_grid))


def rotate(values, cosine, sine, direction):
    half_dim = HDIM // 2
    lead_half = values[..., :half_dim]
    tail_half = values[..., half_dim:]
    cos_grid = cosine[None, :, None, :]
    sin_grid = direction * sine[None, :, None, :]
    return jnp.concatenate(
        [lead_half * cos_grid - tail_half * sin_grid, tail_half * cos_grid + lead_half * sin_grid],
        axis=-1,
    )


def attend_scores(q_rot, k_rot, len_vec):
    raw = jnp.einsum(
        "nqhd,nkhd->nhqk", q_rot, k_rot, preferred_element_type=jnp.float32
    ) / math.sqrt(HDIM)
    places = jnp.arange(SLOT)
    valid = (places[None, :] <= places[:, None])[None, None] & (
        places[None, None, None, :] < len_vec[:, None, None, None]
    )
    return jnp.where(valid, raw, MASKED)


def layer_forward(inputs, len_vec, gains, mats, cosine, sine):
    w_query, w_key, w_value, w_out, w_gate, w_up, w_down = mats
    seq_count = inputs.shape[0] // SLOT

    def to_heads(values):
        return values.reshape(seq_count, SLOT, HEADS, HDIM)

    a_low = rms_forward(inputs, gains[0]).astype(jnp.bfloat16)
    q_rot = rotate(to_heads(project(a_low, w_query)), cosine, sine, 1.0).astype(jnp.bfloat16)
    k_rot = rotate(to_heads(project(a_low, w_key)), cosine, sine, 1.0).astype(jnp.bfloat16)
    v_heads = to_heads(project(a_low, w_value)).astype(jnp.bfloat16)
    scores = attend_scores(q_rot, k_rot, len_vec)
    row_max = jnp.max(scores, axis=-1, keepdims=True)
    log_total = jnp.log(jnp.sum(jnp.exp(scores - row_max), axis=-1, keepdims=True)) + row_max
    p_low = jnp.exp(scores - log_total).astype(jnp.bfloat16)
    att_out = jnp.einsum("nhqk,nkhd->nqhd", p_low, v_heads, preferred_element_type=jnp.float32)
    att_out = att_out.reshape(seq_count * SLOT, D).astype(jnp.bfloat16)
    h_mid = inputs + project(att_out, w_out)
    b_low = rms_forward(h_mid, gains[1]).astype(jnp.bfloat16)
    gate_pre = project(b_low, w_gate)
    up_pre = project(b_low, w_up)
    mix_low = (jax.nn.silu(gate_pre) * up_pre).astype(jnp.bfloat16)
    h_out = h_mid + down_forward(mix_low, w_down)
    return (
        h_out,
        (a_low, q_rot, k_rot, v_heads, log_total, att_out, h_mid, b_low, gate_pre, up_pre, mix_low),
    )


def layer_backward(inputs, len_vec, gains, mats, cosine, sine, saved, grad_out):
    w_query, w_key, w_value, w_out, w_gate, w_up, w_down = mats
    a_low, q_rot, k_rot, v_heads, log_total, att_out, h_mid, b_low, gate_pre, up_pre, mix_low = (
        saved
    )
    seq_count = inputs.shape[0] // SLOT
    grad_branch = grad_out.astype(jnp.bfloat16)
    grad_mix = down_back(grad_branch, w_down)
    sigmoid_gate = jax.nn.sigmoid(gate_pre)
    grad_gate = (grad_mix * up_pre * sigmoid_gate * (1.0 + gate_pre * (1.0 - sigmoid_gate))).astype(
        jnp.bfloat16
    )
    grad_up = (grad_mix * gate_pre * sigmoid_gate).astype(jnp.bfloat16)
    grad_b = project_back(grad_gate, w_gate) + project_back(grad_up, w_up)
    back_mid, gain_mid = rms_backward(h_mid, gains[1], grad_b)
    grad_mid = grad_out + back_mid
    grad_attn = grad_mid.astype(jnp.bfloat16)
    grad_att = (
        project_back(grad_attn, w_out).astype(jnp.bfloat16).reshape(seq_count, SLOT, HEADS, HDIM)
    )
    p_full = jnp.exp(attend_scores(q_rot, k_rot, len_vec) - log_total)
    grad_p = jnp.einsum("nqhd,nkhd->nhqk", grad_att, v_heads, preferred_element_type=jnp.float32)
    grad_s = (p_full * (grad_p - jnp.sum(p_full * grad_p, axis=-1, keepdims=True))).astype(
        jnp.bfloat16
    )
    grad_q = jnp.einsum(
        "nhqk,nkhd->nqhd", grad_s, k_rot, preferred_element_type=jnp.float32
    ) / math.sqrt(HDIM)
    grad_k = jnp.einsum(
        "nhqk,nqhd->nkhd", grad_s, q_rot, preferred_element_type=jnp.float32
    ) / math.sqrt(HDIM)
    grad_v = jnp.einsum(
        "nhqk,nqhd->nkhd", p_full.astype(jnp.bfloat16), grad_att, preferred_element_type=jnp.float32
    )
    row_total = seq_count * SLOT
    grad_q = rotate(grad_q, cosine, sine, -1.0).reshape(row_total, D).astype(jnp.bfloat16)
    grad_k = rotate(grad_k, cosine, sine, -1.0).reshape(row_total, D).astype(jnp.bfloat16)
    grad_v = grad_v.reshape(row_total, D).astype(jnp.bfloat16)
    grad_a = (
        project_back(grad_q, w_query) + project_back(grad_k, w_key) + project_back(grad_v, w_value)
    )
    back_in, gain_in = rms_backward(inputs, gains[0], grad_a)
    operands = (
        a_low,
        grad_q,
        grad_k,
        grad_v,
        att_out,
        grad_attn,
        b_low,
        grad_gate,
        grad_up,
        mix_low,
        grad_branch,
    )
    return (grad_mid + back_in, operands, jnp.stack([gain_in, gain_mid]))


def weight_grads(operands):
    (
        a_low,
        grad_q,
        grad_k,
        grad_v,
        att_out,
        grad_attn,
        b_low,
        grad_gate,
        grad_up,
        mix_low,
        grad_branch,
    ) = operands
    col_blocks = D // BC
    ff_blocks = FF // BC
    return jnp.concatenate(
        [
            block_grad(a_low, grad_q, col_blocks),
            block_grad(a_low, grad_k, col_blocks),
            block_grad(a_low, grad_v, col_blocks),
            block_grad(att_out, grad_attn, col_blocks),
            block_grad(b_low, grad_gate, ff_blocks),
            block_grad(b_low, grad_up, ff_blocks),
            down_grad(mix_low, grad_branch),
        ],
        axis=0,
    )


def combine_parts(earlier, later):
    max_one, sum_one, pick_one = earlier
    max_two, sum_two, pick_two = later
    joint_max = jnp.maximum(max_one, max_two)
    joint_sum = sum_one * jnp.exp(max_one - joint_max) + sum_two * jnp.exp(max_two - joint_max)
    return (joint_max, joint_sum, pick_one + pick_two)


def adam_step(weight, grad, moment, second, rate):
    moment = ADAM_ONE * moment + (1.0 - ADAM_ONE) * grad
    second = ADAM_TWO * second + (1.0 - ADAM_TWO) * grad * grad
    ratio = moment / (1.0 - ADAM_ONE**STEP) / (jnp.sqrt(second / (1.0 - ADAM_TWO**STEP)) + ADAM_EPS)
    return (weight - rate * (ratio + WEIGHT_DECAY * weight), moment, second)


def per_device(
    token_ids,
    lengths,
    comp_mask,
    ref_logp,
    owner,
    blocks,
    left_stat,
    right_stat,
    left_root,
    right_root,
    tables,
    table_moment,
    table_second,
    gains,
    gain_moment,
    gain_second,
):
    vocab_count = lax.axis_size("vocab")
    vocab_index = lax.axis_index("vocab")
    row_share = blocks.shape[1]
    cosine, sine = angles()
    tables_low = lax.all_gather(tables.astype(jnp.bfloat16), "dp", axis=1, tiled=True)
    vocab_rows = tables_low.shape[1]
    local_ids = token_ids.reshape(-1) - vocab_index * vocab_rows
    inside = (local_ids >= 0) & (local_ids < vocab_rows)
    safe_ids = jnp.clip(local_ids, 0, vocab_rows - 1)
    looked = jnp.where(inside[:, None], jnp.take(tables_low[0], safe_ids, axis=0), 0).astype(
        jnp.float32
    )
    embedded = lax.psum_scatter(
        looked.astype(jnp.bfloat16), "vocab", scatter_dimension=0, tiled=True
    ).astype(jnp.float32)
    rows_all = lax.all_gather(blocks.astype(jnp.bfloat16), "vocab", axis=1, tiled=True)
    slots_all = lax.all_gather(rows_all, "dp", axis=0, tiled=True)
    kept_mats = groups(jnp.take(slots_all, owner, axis=0))
    gain_total = jnp.zeros((3, D), jnp.float32)
    loss_own = jnp.zeros((), jnp.float32)
    grad_inputs = []
    operand_list = []
    logit_grads = []
    head_inputs = []
    for micro in range(MB):
        own_pair = vocab_index * MB + micro
        rows_in = embedded[micro * 2 * SLOT : (micro + 1) * 2 * SLOT]
        len_own = lax.dynamic_index_in_dim(lengths, own_pair, 0, keepdims=False)
        h_out, saved = layer_forward(rows_in, len_own, gains, kept_mats, cosine, sine)
        pos_own = len_own[:, None] - 1 - CMP + jnp.arange(CMP)[None, :]
        picked_rows = jnp.take_along_axis(
            h_out.reshape(2, SLOT, D), pos_own[:, :, None], axis=1
        ).reshape(2 * CMP, D)
        c_low = rms_forward(picked_rows, gains[2]).astype(jnp.bfloat16)
        all_rows = lax.all_gather(c_low, "vocab", axis=0, tiled=True)
        ids_sel = token_ids[micro::MB]
        lens_sel = lengths[micro::MB]
        mask_sel = comp_mask[micro::MB].astype(jnp.float32)
        ref_sel = ref_logp[micro::MB]
        pos_sel = lens_sel[:, :, None] - 1 - CMP + jnp.arange(CMP)[None, None, :]
        target = (
            jnp.take_along_axis(ids_sel, pos_sel + 1, axis=2).reshape(-1) - vocab_index * vocab_rows
        )
        logits = mult_nt(all_rows, tables_low[1])
        one_hot = jnp.arange(vocab_rows)[None, :] == target[:, None]
        row_max = jnp.max(logits, axis=1)
        row_sum = jnp.sum(jnp.exp(logits - row_max[:, None]), axis=1)
        row_pick = jnp.sum(jnp.where(one_hot, logits, 0.0), axis=1)
        full_max, full_sum, full_pick = joined((row_max, row_sum, row_pick), "vocab", combine_parts)
        log_norm = full_max + jnp.log(full_sum)
        seq_logp = jnp.sum((full_pick - log_norm).reshape(vocab_count, 2, CMP) * mask_sel, axis=2)
        margin = DPO_BETA * (seq_logp[:, 0] - ref_sel[:, 0] - (seq_logp[:, 1] - ref_sel[:, 1]))
        loss_own = loss_own + jnp.take(jax.nn.softplus(-margin), vocab_index)
        pair_weight = -DPO_BETA * jax.nn.sigmoid(-margin)
        grad_tok = (jnp.stack([pair_weight, -pair_weight], axis=1)[:, :, None] * mask_sel).reshape(
            -1
        )
        grad_logits = (
            grad_tok[:, None] * (one_hot.astype(jnp.float32) - jnp.exp(logits - log_norm[:, None]))
        ).astype(jnp.bfloat16)
        logit_grads.append(grad_logits)
        head_inputs.append(all_rows)
        grad_c = lax.psum_scatter(
            mult(grad_logits, tables_low[1]), "vocab", scatter_dimension=0, tiled=True
        )
        back_rows, gain_head = rms_backward(picked_rows, gains[2], grad_c)
        seq_index = jnp.arange(2)[:, None]
        grad_top = (
            jnp.zeros((2, SLOT, D), jnp.float32)
            .at[seq_index, pos_own]
            .add(back_rows.reshape(2, CMP, D))
        )
        grad_in, operands, gains_now = layer_backward(
            rows_in, len_own, gains, kept_mats, cosine, sine, saved, grad_top.reshape(2 * SLOT, D)
        )
        operand_list.append(operands)
        gain_total = gain_total + jnp.concatenate([gains_now, gain_head[None]], axis=0)
        grad_inputs.append(grad_in)
    joined_ops = tuple(
        (
            jnp.concatenate([ops[i] for ops in operand_list], axis=0)
            for i in range(len(operand_list[0]))
        )
    )
    block_order = weight_grads(joined_ops)
    grad_head = mult_t(jnp.concatenate(logit_grads, axis=0), jnp.concatenate(head_inputs, axis=0))
    grad_rows = lax.all_gather(
        jnp.concatenate(grad_inputs, axis=0).astype(jnp.bfloat16), "vocab", axis=0, tiled=True
    ).astype(jnp.float32)
    grad_embed = (
        jnp.zeros((vocab_rows, D), jnp.float32)
        .at[safe_ids]
        .add(jnp.where(inside[:, None], grad_rows, 0.0))
    )
    table_grad = lax.psum_scatter(
        jnp.stack([grad_embed, grad_head]).astype(jnp.bfloat16),
        "dp",
        scatter_dimension=1,
        tiled=True,
    ).astype(jnp.float32)
    inverse = jnp.zeros((NBLK,), jnp.int32).at[owner].set(jnp.arange(NBLK, dtype=jnp.int32))
    slotted = jnp.take(block_order, inverse, axis=0)
    summed = lax.psum_scatter(slotted.astype(jnp.bfloat16), "dp", scatter_dimension=0, tiled=True)
    share_part = lax.psum_scatter(summed, "vocab", scatter_dimension=1, tiled=True).astype(
        jnp.float32
    )
    whole = lax.all_gather(share_part.astype(jnp.bfloat16), "vocab", axis=1, tiled=True).astype(
        share_part.dtype
    )
    highest = lax.Precision.HIGHEST
    new_left = STAT_DECAY * left_stat + (1.0 - STAT_DECAY) * jnp.einsum(
        "bij,bkj->bik", whole, whole, precision=highest
    )
    new_right = STAT_DECAY * right_stat + (1.0 - STAT_DECAY) * jnp.einsum(
        "bji,bjk->bik", whole, whole, precision=highest
    )
    direction = jnp.einsum("bij,bjk->bik", left_root, whole, precision=highest)
    direction = jnp.einsum("bij,bjk->bik", direction, right_root, precision=highest)
    new_blocks = blocks - SHAMPOO_RATE * lax.dynamic_slice_in_dim(
        direction, vocab_index * row_share, row_share, 1
    )
    loss_sum, gain_grad = lax.psum((loss_own, gain_total), ("dp", "vocab"))
    rates = jnp.array([0.3, 0.02], jnp.float32)[:, None, None]
    new_tables, new_table_moment, new_table_second = adam_step(
        tables, table_grad, table_moment, table_second, rates
    )
    new_gains, new_gain_moment, new_gain_second = adam_step(
        gains, gain_grad, gain_moment, gain_second, GAIN_RATE
    )
    return (
        new_blocks,
        share_part,
        new_left,
        new_right,
        new_tables,
        new_table_moment,
        new_table_second,
        new_gains,
        new_gain_moment,
        new_gain_second,
        loss_sum,
    )


PAIR_ROWS = MB * 2 * CMP
TOKENS = MB * 2 * SLOT
CAP = 24
MSG = 32
EXT = D + 128
AXES = ("z", "x", "y", "core")
SHARD_AXES = ("y", "core", "z", "x")
VMEM_LIMIT = 60 * 1024 * 1024

AT_A = 0
AT_DK = AT_A + TOKENS
AT_DV = AT_DK + TOKENS
AT_AP = AT_DV + TOKENS
AT_DQ = AT_AP + PAIR_ROWS
AT_O = AT_DQ + PAIR_ROWS
AT_DO = AT_O + PAIR_ROWS
AT_B = AT_DO + PAIR_ROWS
AT_Z = AT_B + PAIR_ROWS
AT_DGATE = AT_Z + (FF // D) * PAIR_ROWS
AT_DUP = AT_DGATE + (FF // D) * PAIR_ROWS
AT_DH = AT_DUP + (FF // D) * PAIR_ROWS
ACT_ROWS = AT_DH + PAIR_ROWS


def flat_of(z, x, y, c):
    return ((z * 2 + x) * 2 + y) * 2 + c


def moves(target):
    pairs = []
    for z in range(4):
        for x in range(2):
            for y in range(2):
                for c in range(2):
                    pairs.append((flat_of(z, x, y, c), flat_of(*target(z, x, y, c))))
    return pairs


def hop_one(value):
    return lax.ppermute(
        value,
        AXES,
        moves(lambda z, x, y, c: (z, 1 - x, y, c) if c == 0 else (z, x, 1 - y, c)),
    )


def hop_two(value):
    return lax.ppermute(
        value,
        AXES,
        moves(lambda z, x, y, c: (z, x, 1 - y, c) if c == 0 else (z, 1 - x, y, c)),
    )


def hop_core(value):
    return lax.ppermute(value, AXES, moves(lambda z, x, y, c: (z, x, y, 1 - c)))


def hop_y(value):
    return lax.ppermute(value, AXES, moves(lambda z, x, y, c: (z, x, 1 - y, c)))


def ring(value, step):
    return lax.ppermute(value, AXES, moves(lambda z, x, y, c: ((z + step) % 4, x, y, c)))


def spread(chunk):
    line = jnp.stack([chunk] + [ring(chunk, step) for step in range(1, 4)])
    one = hop_one(line)
    two = hop_two(line)
    both = hop_two(one)
    plane = jnp.stack([line, one, two, both])
    return plane, hop_core(plane)


def dot_nn(left, right):
    return lax.dot_general(left, right, (((1,), (0,)), ((), ())), preferred_element_type=jnp.float32)


def dot_nt(left, right):
    return lax.dot_general(left, right, (((1,), (1,)), ((), ())), preferred_element_type=jnp.float32)


def dot_tn(left, right):
    return lax.dot_general(left, right, (((0,), (0,)), ((), ())), preferred_element_type=jnp.float32)


def low(value):
    return value.astype(jnp.bfloat16)


def high(value):
    return value.astype(jnp.float32)


def source_of(coord, other_core, rel, back):
    core = coord[3] + other_core * (1 - 2 * coord[3])
    first = rel & 1
    second = rel >> 1
    x_flip = first + core * (second - first)
    y_flip = second + core * (first - second)
    z = (coord[0] + 4 - back) & 3
    x = coord[1] + x_flip * (1 - 2 * coord[1])
    y = coord[2] + y_flip * (1 - 2 * coord[2])
    return z, x, y, core


def start_weights(coord, parts, held, sem):
    for index in range(8):
        slot_low, other_core = index // 2, index % 2

        def one(i, carry):
            rel, back = i >> 2, i & 3
            z, x, y, core = source_of(coord, other_core, rel, back)
            slot = 8 * z + 4 * x + slot_low
            row = pl.multiple_of(192 * (2 * y + core), 64)
            pltpu.make_async_copy(
                parts[index].at[rel, back], held.at[slot, pl.ds(row, 192)], sem
            ).start()
            return carry

        lax.fori_loop(0, 16, one, 0)


def wait_weights(held, sem):
    pltpu.make_async_copy(held, held, sem).wait()


def iota(shape, axis):
    return lax.broadcasted_iota(jnp.int32, shape, axis)


def pick_rows(lens):
    row = iota((PAIR_ROWS, 1), 0)
    seq = row >> 4
    length = jnp.where(
        seq == 0, lens[0], jnp.where(seq == 1, lens[1], jnp.where(seq == 2, lens[2], lens[3]))
    )
    return seq, length - 1 - CMP + (row & 15)


def masks(lens):
    seq, pos = pick_rows(lens)
    col = iota((PAIR_ROWS, TOKENS), 1)
    same = (col >> 6) == seq
    key = col & 63
    return same & (key <= pos), same & (key == pos)


def turn(chunk, cosine, sine, sign):
    lane = iota(chunk.shape, 1)
    swapped = jnp.where((lane & 63) < 32, pltpu.roll(chunk, 96, 1), pltpu.roll(chunk, 32, 1))
    return chunk * cosine + swapped * (sine * sign)


def scale_of(values):
    return lax.rsqrt(jnp.mean(values * values, axis=-1, keepdims=True) + NORM_EPS)


def rms_back(values, gain, grad):
    scale = scale_of(values)
    inner = jnp.mean(values * gain * grad, axis=-1, keepdims=True)
    back = scale * gain * grad - values * (scale * scale * scale) * inner
    return back, jnp.sum(grad * values * scale, axis=0, keepdims=True)


def forward_kernel(owner, coord, lens, x, gains, cos_q, sin_q, cos_k, sin_k, *rest):
    parts, rest = rest[:8], rest[8:]
    a_out, ap_out, q_out, k_out, v_out, o_out, h1_out, b_out, gate_out, up_out, z_out, h2_out, c_out = rest[:13]
    held, sem = rest[13:]
    start_weights(coord, parts, held, sem)
    values = high(x[...])
    a_low = low(values * scale_of(values) * gains[0:1, :])
    a_out[...] = a_low
    valid, chosen = masks(lens)
    select = jnp.where(chosen, 1.0, 0.0).astype(jnp.bfloat16)
    a_pick = low(dot_nn(select, a_low))
    ap_out[...] = a_pick
    x_pick = dot_nn(select, x[...])
    wait_weights(held, sem)
    for j in range(2):
        q = dot_nn(a_pick, held[owner[j]])
        k = dot_nn(a_low, held[owner[2 + j]])
        v_out[:, j * BC : (j + 1) * BC] = low(dot_nn(a_low, held[owner[4 + j]]))
        for i in range(3):
            at = slice(j * BC + i * 128, j * BC + (i + 1) * 128)
            q_out[:, at] = low(turn(q[:, i * 128 : (i + 1) * 128], cos_q[...], sin_q[...], 1.0))
            k_out[:, at] = low(turn(k[:, i * 128 : (i + 1) * 128], cos_k[...], sin_k[...], 1.0))
    lane = iota((TOKENS, 128), 1)
    zero = jnp.zeros((TOKENS, 128), jnp.bfloat16)
    for p in range(HEADS // 2):
        at = slice(p * 128, (p + 1) * 128)
        total = jnp.zeros((PAIR_ROWS, 128), jnp.float32)
        for h in range(2):
            mine = (lane >> 6) == h
            s = dot_nt(q_out[:, at], jnp.where(mine, k_out[:, at], zero)) * (1.0 / math.sqrt(HDIM))
            s = jnp.where(valid, s, MASKED)
            e = jnp.exp(s - jnp.max(s, axis=-1, keepdims=True))
            prob = low(e / jnp.sum(e, axis=-1, keepdims=True))
            total = total + dot_nn(prob, jnp.where(mine, v_out[:, at], zero))
        o_out[:, at] = low(total)
    for j in range(2):
        at = slice(j * BC, (j + 1) * BC)
        h1_out[:, at] = x_pick[:, at] + dot_nn(o_out[...], held[owner[6 + j]])
    h1 = h1_out[...]
    b_low = low(h1 * scale_of(h1) * gains[1:2, :])
    b_out[...] = b_low
    for j in range(FF // BC):
        at = slice(j * BC, (j + 1) * BC)
        gate = dot_nn(b_low, held[owner[8 + j]])
        up = dot_nn(b_low, held[owner[16 + j]])
        gate_out[:, at] = gate
        up_out[:, at] = up
        z_out[:, at] = low(gate * jax.nn.sigmoid(gate) * up)
    for j in range(2):
        total = h1[:, j * BC : (j + 1) * BC]
        for r in range(FF // D):
            total = total + dot_nn(z_out[:, r * D : (r + 1) * D], held[owner[24 + 2 * r + j]])
        h2_out[:, j * BC : (j + 1) * BC] = total
    h2 = h2_out[...]
    c_out[...] = low(h2 * scale_of(h2) * gains[2:3, :])


def vmem(number):
    return [pl.BlockSpec(memory_space=pltpu.VMEM)] * number


def smem(number):
    return [pl.BlockSpec(memory_space=pltpu.SMEM)] * number


def anywhere(number):
    return [pl.BlockSpec(memory_space=pl.ANY)] * number


def forward_call(owner, coord, lens, x, gains, turns, parts):
    def made(rows, columns, kind):
        return jax.ShapeDtypeStruct((rows, columns), kind)

    return pl.pallas_call(
        forward_kernel,
        out_shape=(
            made(TOKENS, D, jnp.bfloat16),
            made(PAIR_ROWS, D, jnp.bfloat16),
            made(PAIR_ROWS, D, jnp.bfloat16),
            made(TOKENS, D, jnp.bfloat16),
            made(TOKENS, D, jnp.bfloat16),
            made(PAIR_ROWS, D, jnp.bfloat16),
            made(PAIR_ROWS, D, jnp.float32),
            made(PAIR_ROWS, D, jnp.bfloat16),
            made(PAIR_ROWS, FF, jnp.float32),
            made(PAIR_ROWS, FF, jnp.float32),
            made(PAIR_ROWS, FF, jnp.bfloat16),
            made(PAIR_ROWS, D, jnp.float32),
            made(PAIR_ROWS, D, jnp.bfloat16),
        ),
        in_specs=smem(3) + vmem(6) + anywhere(8),
        out_specs=tuple(vmem(13)),
        scratch_shapes=[
            pltpu.VMEM((NBLK, D, BC), jnp.bfloat16),
            pltpu.SemaphoreType.DMA,
        ],
        compiler_params=pltpu.CompilerParams(vmem_limit_bytes=VMEM_LIMIT),
        name="layer_forward",
    )(owner, coord, lens, x, gains, *turns, *parts)


def unpack(ext):
    stat = high(ext[:, D:EXT])
    top = (stat[:, 0:1] + stat[:, 1:2]) + stat[:, 2:3]
    total = (stat[:, 3:4] + stat[:, 4:5]) + stat[:, 5:6]
    return top, total, high(ext[:, :D])


def pack_stat(top, total):
    lane = iota((top.shape[0], 128), 1)
    out = jnp.zeros((top.shape[0], 128), jnp.float32)
    for first, value in ((0, top), (3, total)):
        for i in range(3):
            piece = high(low(value))
            out = jnp.where(lane == first + i, piece, out)
            value = value - piece
    return low(out)


def merge(items):
    top = items[0][0]
    for item in items[1:]:
        top = jnp.maximum(top, item[0])
    total = 0.0
    mixed = 0.0
    for item_top, item_total, item_mixed in items:
        factor = jnp.exp(item_top - top)
        total = total + item_total * factor
        mixed = mixed + item_mixed * factor
    return top, total, mixed


def merge_kernel(*refs):
    out = refs[-1]
    top, total, mixed = merge([unpack(ref[...]) for ref in refs[:-1]])
    out[:, :D] = low(mixed)
    out[:, D:EXT] = pack_stat(top, total)


def merge_call(*parts):
    rows = parts[0].shape[0]
    block = min(rows, 256)
    spec = pl.BlockSpec((block, EXT), lambda i: (i, 0))
    return pl.pallas_call(
        merge_kernel,
        grid=(rows // block,),
        out_shape=jax.ShapeDtypeStruct((rows, EXT), jnp.bfloat16),
        in_specs=[spec] * len(parts),
        out_specs=spec,
        compiler_params=pltpu.CompilerParams(vmem_limit_bytes=VMEM_LIMIT),
        name="merge_parts",
    )(*parts)


def head_kernel(real, rows, head, ext, kept, stat):
    logits = dot_nt(rows[...], head[...])
    col = iota(logits.shape, 1)
    logits = jnp.where(col < real, logits, MASKED)
    top = jnp.max(logits, axis=-1, keepdims=True)
    e = jnp.exp(logits - top)
    total = jnp.sum(e, axis=-1, keepdims=True)
    e_low = low(e)
    kept[...] = e_low
    ext[:, :D] = low(dot_nn(e_low, head[...]))
    ext[:, D:EXT] = pack_stat(top, total)
    stat[...] = jnp.broadcast_to(top, stat.shape)


def head_call(rows, head, real):
    number, wide = rows.shape[0], head.shape[0]
    return pl.pallas_call(
        functools.partial(head_kernel, real),
        grid=(number // 256,),
        out_shape=(
            jax.ShapeDtypeStruct((number, EXT), jnp.bfloat16),
            jax.ShapeDtypeStruct((number, wide), jnp.bfloat16),
            jax.ShapeDtypeStruct((number, 128), jnp.float32),
        ),
        in_specs=[
            pl.BlockSpec((256, D), lambda i: (i, 0)),
            pl.BlockSpec((wide, D), lambda i: (0, 0)),
        ],
        out_specs=(
            pl.BlockSpec((256, EXT), lambda i: (i, 0)),
            pl.BlockSpec((256, wide), lambda i: (i, 0)),
            pl.BlockSpec((256, 128), lambda i: (i, 0)),
        ),
        compiler_params=pltpu.CompilerParams(vmem_limit_bytes=VMEM_LIMIT),
        name="head_forward",
    )(rows, head)


def head_grad_kernel(rows, kept, stat, info, out):
    weight = info[:, 0:1]
    factor = weight * jnp.exp(stat[:, 0:1] - info[:, 1:2])
    col = iota(kept.shape, 1)
    hit = col == info[:, 2:3].astype(jnp.int32)
    grad = low(jnp.where(hit, weight, 0.0) - high(kept[...]) * factor)

    @pl.when(pl.program_id(0) == 0)
    def _():
        out[...] = jnp.zeros(out.shape, jnp.float32)

    out[...] += dot_tn(grad, rows[...])


def head_grad_call(rows, kept, stat, info):
    number, wide = kept.shape
    return pl.pallas_call(
        head_grad_kernel,
        grid=(number // 256,),
        out_shape=jax.ShapeDtypeStruct((wide, D), jnp.float32),
        in_specs=[
            pl.BlockSpec((256, D), lambda i: (i, 0)),
            pl.BlockSpec((256, wide), lambda i: (i, 0)),
            pl.BlockSpec((256, 128), lambda i: (i, 0)),
            pl.BlockSpec((256, 128), lambda i: (i, 0)),
        ],
        out_specs=pl.BlockSpec((wide, D), lambda i: (0, 0)),
        compiler_params=pltpu.CompilerParams(vmem_limit_bytes=VMEM_LIMIT),
        name="head_grad",
    )(rows, kept, stat, info)


def backward_kernel(owner, coord, lens, refs, x, gains, cos_q, sin_q, cos_k, sin_k, *rest):
    a, ap, q, k, v, o, h1, b, gate, up, z, h2, c = rest[:13]
    truth, wanted, u0, u1, u2, u3 = rest[13:19]
    parts = rest[19:27]
    act, dx_out, gain_out, info_out, loss_out = rest[27:32]
    held, sem, dk_acc = rest[32:]
    start_weights(coord, parts, held, sem)
    valid, chosen = masks(lens)
    select = jnp.where(chosen, 1.0, 0.0).astype(jnp.bfloat16)
    act[AT_A:AT_DK] = a[...]
    act[AT_AP:AT_DQ] = ap[...]
    act[AT_O:AT_DO] = o[...]
    act[AT_B:AT_Z] = b[...]
    for r in range(FF // D):
        act[AT_Z + r * PAIR_ROWS : AT_Z + (r + 1) * PAIR_ROWS] = z[:, r * D : (r + 1) * D]
    top, total, mixed = merge([unpack(part[...]) for part in (u0, u1, u2, u3)])
    norm = top + jnp.log(total)
    target = high(truth[...])
    picked = jnp.sum(high(c[...]) * target, axis=-1, keepdims=True)
    scored = wanted[:, 0:1]
    terms = (picked - norm) * scored
    seq = iota((PAIR_ROWS, 1), 0) >> 4
    logp = [jnp.sum(jnp.where(seq == n, terms, 0.0), axis=0, keepdims=True) for n in range(2 * MB)]
    weight = jnp.zeros((PAIR_ROWS, 1), jnp.float32)
    loss = jnp.zeros((1, 1), jnp.float32)
    for n in range(MB):
        margin = DPO_BETA * ((logp[2 * n] - refs[2 * n]) - (logp[2 * n + 1] - refs[2 * n + 1]))
        loss = loss + jnp.maximum(-margin, 0.0) + jnp.log1p(jnp.exp(-jnp.abs(margin)))
        slope = -DPO_BETA * jax.nn.sigmoid(-margin)
        weight = jnp.where(seq == 2 * n, slope, jnp.where(seq == 2 * n + 1, -slope, weight))
    weight = weight * scored
    loss_out[...] = jnp.broadcast_to(loss, loss_out.shape)
    lane = iota((PAIR_ROWS, 128), 1)
    info_out[...] = jnp.where(
        lane == 0, weight, jnp.where(lane == 1, norm, jnp.where(lane == 2, wanted[:, 1:2], 0.0))
    )
    grad_c = weight * (target - mixed / total)
    d2, gain_top = rms_back(h2[...], gains[2:3, :], grad_c)
    gain_out[2:3, :] = gain_top
    d2_low = low(d2)
    act[AT_DH:ACT_ROWS] = d2_low
    wait_weights(held, sem)
    grad_b = jnp.zeros((PAIR_ROWS, D), jnp.float32)
    for r in range(FF // D):
        grad_mix = dot_nt(d2_low[:, :BC], held[owner[24 + 2 * r]]) + dot_nt(
            d2_low[:, BC:], held[owner[25 + 2 * r]]
        )
        at = slice(r * D, (r + 1) * D)
        gate_pre = gate[:, at]
        sig = jax.nn.sigmoid(gate_pre)
        d_gate = low(grad_mix * up[:, at] * sig * (1.0 + gate_pre * (1.0 - sig)))
        d_up = low(grad_mix * gate_pre * sig)
        act[AT_DGATE + r * PAIR_ROWS : AT_DGATE + (r + 1) * PAIR_ROWS] = d_gate
        act[AT_DUP + r * PAIR_ROWS : AT_DUP + (r + 1) * PAIR_ROWS] = d_up
        for j in range(2):
            cut = slice(j * BC, (j + 1) * BC)
            grad_b = grad_b + dot_nt(d_gate[:, cut], held[owner[8 + 2 * r + j]])
            grad_b = grad_b + dot_nt(d_up[:, cut], held[owner[16 + 2 * r + j]])
    back, gain_mid = rms_back(h1[...], gains[1:2, :], grad_b)
    gain_out[1:2, :] = gain_mid
    d1 = d2 + back
    d1_low = low(d1)
    act[AT_DO:AT_B] = d1_low
    d_att = low(
        dot_nt(d1_low[:, :BC], held[owner[6]]) + dot_nt(d1_low[:, BC:], held[owner[7]])
    )
    lane_k = iota((TOKENS, 128), 1)
    zero_k = jnp.zeros((TOKENS, 128), jnp.bfloat16)
    zero_q = jnp.zeros((PAIR_ROWS, 128), jnp.bfloat16)
    root = 1.0 / math.sqrt(HDIM)
    for p in range(HEADS // 2):
        at = slice(p * 128, (p + 1) * 128)
        d_q = jnp.zeros((PAIR_ROWS, 128), jnp.float32)
        d_k = jnp.zeros((TOKENS, 128), jnp.float32)
        d_v = jnp.zeros((TOKENS, 128), jnp.float32)
        for h in range(2):
            mine_k = (lane_k >> 6) == h
            mine_q = (lane >> 6) == h
            k_one = jnp.where(mine_k, k[:, at], zero_k)
            q_one = jnp.where(mine_q, q[:, at], zero_q)
            do_one = jnp.where(mine_q, d_att[:, at], zero_q)
            s = dot_nt(q_one, k_one) * root
            s = jnp.where(valid, s, MASKED)
            e = jnp.exp(s - jnp.max(s, axis=-1, keepdims=True))
            prob = e / jnp.sum(e, axis=-1, keepdims=True)
            d_p = dot_nt(do_one, v[:, at])
            d_s = low(prob * (d_p - jnp.sum(prob * d_p, axis=-1, keepdims=True)))
            d_q = d_q + dot_nn(d_s, k_one)
            d_k = d_k + dot_tn(d_s, q_one)
            d_v = d_v + dot_tn(low(prob), do_one)
        act[AT_DQ:AT_O, at] = low(turn(d_q * root, cos_q[...], sin_q[...], -1.0))
        act[AT_DK:AT_DV, at] = low(turn(d_k * root, cos_k[...], sin_k[...], -1.0))
        act[AT_DV:AT_AP, at] = low(d_v)
    d_q_all = low(dot_tn(select, act[AT_DQ:AT_O]))
    grad_a = jnp.zeros((TOKENS, D), jnp.float32)
    for j in range(2):
        cut = slice(j * BC, (j + 1) * BC)
        grad_a = grad_a + dot_nt(d_q_all[:, cut], held[owner[j]])
        grad_a = grad_a + dot_nt(act[AT_DK:AT_DV, cut], held[owner[2 + j]])
        grad_a = grad_a + dot_nt(act[AT_DV:AT_AP, cut], held[owner[4 + j]])
    back_in, gain_in = rms_back(high(x[...]), gains[0:1, :], grad_a)
    gain_out[0:1, :] = gain_in
    rest_low = low(d1 - high(d1_low))
    dx_out[...] = low(back_in + dot_tn(select, d1_low) + dot_tn(select, rest_low))


def backward_call(owner, coord, lens, refs, x, gains, turns, saved, truth, wanted, parts_u, parts):
    return pl.pallas_call(
        backward_kernel,
        out_shape=(
            jax.ShapeDtypeStruct((ACT_ROWS, D), jnp.bfloat16),
            jax.ShapeDtypeStruct((TOKENS, D), jnp.bfloat16),
            jax.ShapeDtypeStruct((3, D), jnp.float32),
            jax.ShapeDtypeStruct((PAIR_ROWS, 128), jnp.float32),
            jax.ShapeDtypeStruct((1, 128), jnp.float32),
        ),
        in_specs=smem(4) + vmem(6 + 13 + 2 + 4) + anywhere(8),
        out_specs=tuple(vmem(5)),
        scratch_shapes=[
            pltpu.VMEM((NBLK, D, BC), jnp.bfloat16),
            pltpu.SemaphoreType.DMA,
            pltpu.VMEM((8, 128), jnp.float32),
        ],
        compiler_params=pltpu.CompilerParams(vmem_limit_bytes=VMEM_LIMIT),
        name="layer_backward",
    )(owner, coord, lens, refs, x, gains, *turns, *saved, truth, wanted, *parts_u, *parts)


def weight_grad_kernel(block_of, x_at, y_at, coord, mine, theirs, *outs):
    core = coord[3]
    for k in range(4):
        own, one, two, both = outs[4 * k : 4 * k + 4]
        for x_flip in range(2):

            def step(back, carry):
                z = (coord[0] + 4 - back) & 3
                x = coord[1] + x_flip * (1 - 2 * coord[1])
                slot = 8 * z + 4 * x + k
                block = block_of[slot]
                cut = pl.ds(pl.multiple_of((block & 1) * BC, 128), BC)
                x_row = pl.multiple_of(x_at[slot], 64)
                y_row = pl.multiple_of(y_at[slot], 64)

                def put(grad):
                    grad_low = low(grad)
                    quarter = [grad_low[192 * n : 192 * (n + 1)] for n in range(4)]
                    even = coord[2] == 0
                    first = core == 0
                    near = jnp.where(
                        even,
                        jnp.where(first, quarter[0], quarter[1]),
                        jnp.where(first, quarter[2], quarter[3]),
                    )
                    far = jnp.where(
                        even,
                        jnp.where(first, quarter[2], quarter[3]),
                        jnp.where(first, quarter[0], quarter[1]),
                    )
                    if x_flip == 0:
                        own[back] = near

                        @pl.when(first)
                        def _():
                            two[back] = far

                        @pl.when(jnp.logical_not(first))
                        def _():
                            one[back] = far
                    else:
                        both[back] = far

                        @pl.when(first)
                        def _():
                            one[back] = near

                        @pl.when(jnp.logical_not(first))
                        def _():
                            two[back] = near

                wide = (block >= 2) & (block < 6)

                @pl.when(wide)
                def _():
                    left = jnp.concatenate(
                        [mine[pl.ds(x_row, TOKENS), :], theirs[pl.ds(x_row, TOKENS), :]], axis=0
                    )
                    right = jnp.concatenate(
                        [mine[pl.ds(y_row, TOKENS), cut], theirs[pl.ds(y_row, TOKENS), cut]], axis=0
                    )
                    put(dot_tn(left, right))

                @pl.when(jnp.logical_not(wide))
                def _():
                    left = jnp.concatenate(
                        [mine[pl.ds(x_row, PAIR_ROWS), :], theirs[pl.ds(x_row, PAIR_ROWS), :]],
                        axis=0,
                    )
                    right = jnp.concatenate(
                        [mine[pl.ds(y_row, PAIR_ROWS), cut], theirs[pl.ds(y_row, PAIR_ROWS), cut]],
                        axis=0,
                    )
                    put(dot_tn(left, right))

                return carry

            lax.fori_loop(0, 4, step, 0)


def weight_grad_call(block_of, x_at, y_at, coord, mine, theirs):
    return pl.pallas_call(
        weight_grad_kernel,
        out_shape=tuple([jax.ShapeDtypeStruct((4, 192, BC), jnp.bfloat16)] * 16),
        in_specs=smem(4) + vmem(2),
        out_specs=tuple(vmem(16)),
        compiler_params=pltpu.CompilerParams(vmem_limit_bytes=VMEM_LIMIT),
        name="weight_grads",
    )(block_of, x_at, y_at, coord, mine, theirs)


def shampoo_kernel(coord, own, by_y, by_core, by_both, lstat, rstat, lroot, rroot, blk, new_l, new_r, new_b, whole):
    y, core = coord[2], coord[3]
    for piece, y_at, core_at in (
        (own, y, core),
        (by_y, 1 - y, core),
        (by_core, y, 1 - core),
        (by_both, 1 - y, 1 - core),
    ):
        row = pl.multiple_of(192 * (2 * y_at + core_at), 64)
        whole[pl.ds(row, 192), :] = piece[0]
    grad = whole[...]
    new_l[0] = STAT_DECAY * lstat[0] + (1.0 - STAT_DECAY) * dot_nt(grad, grad)
    new_r[0] = STAT_DECAY * rstat[0] + (1.0 - STAT_DECAY) * dot_tn(grad, grad)
    turned = dot_nn(low(lroot[0]), grad)
    new_b[0] = blk[0] - SHAMPOO_RATE * dot_nn(low(turned), low(rroot[0]))


def shampoo_call(coord, pieces, lstat, rstat, lroot, rroot, blk):
    slots = lstat.shape[0]

    def one(rows, columns):
        return pl.BlockSpec((1, rows, columns), lambda i, coord: (i, 0, 0))

    return pl.pallas_call(
        shampoo_kernel,
        grid_spec=pltpu.PrefetchScalarGridSpec(
            num_scalar_prefetch=1,
            grid=(slots,),
            in_specs=[one(192, BC)] * 4
            + [
                one(D, D),
                one(BC, BC),
                pl.BlockSpec((1, 192, D), lambda i, coord: (i, 2 * coord[2] + coord[3], 0)),
                one(BC, BC),
                one(192, BC),
            ],
            out_specs=(one(D, D), one(BC, BC), one(192, BC)),
            scratch_shapes=[pltpu.VMEM((D, BC), jnp.bfloat16)],
        ),
        out_shape=(
            jax.ShapeDtypeStruct(lstat.shape, jnp.float32),
            jax.ShapeDtypeStruct(rstat.shape, jnp.float32),
            jax.ShapeDtypeStruct(blk.shape, jnp.float32),
        ),
        compiler_params=pltpu.CompilerParams(vmem_limit_bytes=VMEM_LIMIT),
        name="shampoo",
    )(coord, *pieces, lstat, rstat, lroot, rroot, blk)


def block_rows():
    x_at, y_at = [], []
    for b in range(NBLK):
        if b < 2:
            x_at.append(AT_AP), y_at.append(AT_DQ)
        elif b < 4:
            x_at.append(AT_A), y_at.append(AT_DK)
        elif b < 6:
            x_at.append(AT_A), y_at.append(AT_DV)
        elif b < 8:
            x_at.append(AT_O), y_at.append(AT_DO)
        elif b < 16:
            x_at.append(AT_B), y_at.append(AT_DGATE + (b - 8) // 2 * PAIR_ROWS)
        elif b < 24:
            x_at.append(AT_B), y_at.append(AT_DUP + (b - 16) // 2 * PAIR_ROWS)
        else:
            x_at.append(AT_Z + (b - 24) // 2 * PAIR_ROWS), y_at.append(AT_DH)
    return jnp.array(x_at, jnp.int32), jnp.array(y_at, jnp.int32)


def per_core(
    token_ids,
    lengths,
    comp_mask,
    ref_logp,
    owner,
    blocks,
    left_stat,
    right_stat,
    left_root,
    right_root,
    tables,
    table_moment,
    table_second,
    gains,
    gain_moment,
    gain_second,
):
    zi, xi, yi, ci = (lax.axis_index(name) for name in AXES)
    coord = jnp.stack([zi, xi, yi, ci]).astype(jnp.int32)
    vocab_index = 2 * yi + ci
    shard = vocab_index * 8 + 2 * zi + xi
    table_rows = tables.shape[1]
    vocab = table_rows * 32
    seqs = 2 * MB
    shares = blocks.astype(jnp.bfloat16)
    parts = []
    for slot in range(4):
        parts.extend(spread(shares[slot]))
    first_pair = vocab_index * MB
    ids = lax.dynamic_slice_in_dim(token_ids, first_pair, MB, 0).reshape(seqs, SLOT)
    lens = lax.dynamic_slice_in_dim(lengths, first_pair, MB, 0).reshape(seqs)
    wanted = lax.dynamic_slice_in_dim(comp_mask, first_pair, MB, 0).reshape(PAIR_ROWS)
    refs = lax.dynamic_slice_in_dim(ref_logp, first_pair, MB, 0).reshape(seqs)
    places = jnp.arange(SLOT)
    pos = (lens[:, None] - 1 - CMP + jnp.arange(CMP)[None, :]).astype(jnp.int32)
    targets = jnp.sum(
        jnp.where(places[None, None, :] == (pos + 1)[:, :, None], ids[:, None, :], 0), axis=-1
    ).reshape(PAIR_ROWS)
    asked = jnp.concatenate([ids.reshape(TOKENS), targets + vocab])
    used = jnp.concatenate(
        [(places[None, :] < lens[:, None]).reshape(TOKENS), jnp.ones((PAIR_ROWS,), bool)]
    )
    number = jnp.where(asked >= vocab, asked - vocab, asked)
    holder = number // table_rows
    local_row = number - holder * table_rows + jnp.where(asked >= vocab, table_rows, 0)
    total = asked.shape[0]
    earlier = jnp.arange(total)[None, :] < jnp.arange(total)[:, None]
    same = (asked[:, None] == asked[None, :]) & used[:, None] & used[None, :]
    first = used & jnp.logical_not(jnp.any(same & earlier, axis=1))
    rank = jnp.sum(
        ((holder[:, None] == holder[None, :]) & earlier & first[None, :]).astype(jnp.int32), axis=1
    )
    spill = jnp.any(first & (rank >= CAP))
    seat_first = jnp.where(first & (rank < CAP), holder * CAP + rank, -1)
    seat = jnp.sum(jnp.where(same & first[None, :], seat_first[None, :] + 1, 0), axis=1) - 1
    seats = jnp.arange(32 * CAP)
    request = jnp.sum(
        jnp.where(seat_first[:, None] == seats[None, :], local_row[:, None], 0), axis=0
    )
    message = jnp.concatenate(
        [
            request.reshape(32, CAP),
            jnp.broadcast_to(spill.astype(jnp.int32), (32, MSG - CAP)),
        ],
        axis=1,
    )
    message = lax.all_to_all(message, SHARD_AXES, 0, 0, tiled=True)
    any_spill = jnp.max(message[:, MSG - 1]) > 0
    asked_rows = message[:, :CAP].reshape(32 * CAP)
    table_low = tables.astype(jnp.bfloat16).reshape(2 * table_rows, D)
    give = (asked_rows[:, None] == jnp.arange(2 * table_rows)[None, :]).astype(jnp.bfloat16)
    given = low(dot_nn(give, table_low))
    got = lax.all_to_all(given, SHARD_AXES, 0, 0, tiled=True)
    place = (seat[:, None] == seats[None, :]).astype(jnp.bfloat16)
    quick = low(dot_nn(place, got))
    all_targets = jnp.sum(
        jnp.where(
            places[None, None, None, :]
            == (lengths[:, :, None] - CMP + jnp.arange(CMP)[None, None, :])[:, :, :, None],
            token_ids[:, :, None, :],
            0,
        ),
        axis=-1,
    )

    def rows_slow():
        gathered = lax.all_gather(table_low.reshape(2, table_rows, D), ("z", "x"), axis=1, tiled=True)
        held_rows = gathered.shape[1]

        def find(table, wanted_ids):
            local = wanted_ids - vocab_index * held_rows
            inside = (local >= 0) & (local < held_rows)
            rows = jnp.take(table, jnp.clip(local, 0, held_rows - 1), axis=0)
            return jnp.where(inside[:, None], rows, 0)

        found = jnp.concatenate(
            [
                find(gathered[0], token_ids.reshape(-1)).reshape(-1, TOKENS, D),
                find(gathered[1], all_targets.reshape(-1)).reshape(-1, PAIR_ROWS, D),
            ],
            axis=1,
        )
        summed = lax.psum(found.astype(jnp.float32), ("y", "core")).astype(jnp.bfloat16)
        return lax.dynamic_index_in_dim(summed, vocab_index, 0, keepdims=False)

    rows = lax.cond(any_spill, rows_slow, lambda: quick)
    x, truth = rows[:TOKENS], rows[TOKENS:]
    inv_freq = ROPE_BASE ** (-jnp.arange(HDIM // 2).astype(jnp.float32) * 2.0 / HDIM)
    phase = places.astype(jnp.float32)[:, None] * inv_freq[None, :]
    phase_pick = pos.reshape(PAIR_ROWS).astype(jnp.float32)[:, None] * inv_freq[None, :]

    def turning(angle, repeat):
        cosine, sine = jnp.cos(angle), jnp.sin(angle)
        return (
            jnp.tile(jnp.concatenate([cosine] * 4, axis=1), (repeat, 1)),
            jnp.tile(jnp.concatenate([-sine, sine, -sine, sine], axis=1), (repeat, 1)),
        )

    turns = turning(phase_pick, 1) + turning(phase, seqs)
    saved = forward_call(owner, coord, lens, x, gains, turns, parts)
    plane, other = spread(saved[-1])
    head_rows = jnp.concatenate([plane, other]).reshape(-1, D)
    wide = -(-table_rows // 128) * 128
    head_low = jnp.pad(table_low[table_rows:], ((0, wide - table_rows), (0, 0)))
    ext, kept, stat = head_call(head_rows, head_low, table_rows)
    half = ext.shape[0] // 2
    ext = merge_call(ext[:half], hop_core(ext[half:])).reshape(4, 4 * PAIR_ROWS, EXT)
    one = merge_call(ext[1], hop_two(ext[3]))
    ext = merge_call(ext[0], hop_one(one), hop_two(ext[2])).reshape(4, PAIR_ROWS, EXT)
    parts_u = [ext[0]] + [ring(ext[step], -step) for step in range(1, 4)]
    marks = jnp.stack([wanted.astype(jnp.float32), targets.astype(jnp.float32)], axis=1)
    marks = jnp.pad(marks, ((0, 0), (0, 126)))
    act, dx, gain_part, info, loss_part = backward_call(
        owner, coord, lens, refs, x, gains, turns, saved, truth, marks, parts_u, parts
    )
    inverse = jnp.sum(
        jnp.where(
            owner[None, :] == jnp.arange(NBLK)[:, None], jnp.arange(NBLK, dtype=jnp.int32)[None, :], 0
        ),
        axis=1,
    )
    x_at, y_at = block_rows()
    chosen = (inverse[:, None] == jnp.arange(NBLK)[None, :]).astype(jnp.int32)
    grads = weight_grad_call(
        inverse,
        jnp.sum(chosen * x_at[None, :], axis=1),
        jnp.sum(chosen * y_at[None, :], axis=1),
        coord,
        act,
        hop_core(act),
    )
    share_list, wholes = [], []
    for slot in range(4):
        own, one, two, both = grads[4 * slot : 4 * slot + 4]
        one = low(high(one) + high(hop_two(both)))
        one = hop_one(one)
        two = hop_two(two)
        line = [low(high(own[n]) + high(one[n]) + high(two[n])) for n in range(4)]
        share = high(line[0])
        for step in range(1, 4):
            share = share + high(ring(line[step], -step))
        share_list.append(share)
    block_grads = jnp.stack(share_list)
    near = block_grads.astype(jnp.bfloat16)
    by_y = hop_y(near)
    pair = hop_core(jnp.stack([near, by_y]))
    new_left, new_right, new_blocks = shampoo_call(
        coord, (near, by_y, pair[0], pair[1]), left_stat, right_stat, left_root, right_root, blocks
    )
    told = jnp.concatenate(
        [
            info[:, :3].reshape(-1),
            gain_part.reshape(-1),
            loss_part[0, :1],
            jnp.zeros((63,), jnp.float32),
        ]
    )
    heard = lax.all_to_all(
        jnp.broadcast_to(told[None], (32, told.shape[0])), AXES, 0, 0, tiled=True
    )
    summed = jnp.sum(heard[:, 3 * PAIR_ROWS :], axis=0)
    gain_grad = summed[: 3 * D].reshape(3, D)
    loss_sum = summed[3 * D]
    sources = []
    for other_core in range(2):
        for rel in range(4):
            for back in range(4):
                sources.append(flat_of(*source_of((zi, xi, yi, ci), other_core, rel, back)))
    sources = jnp.stack(sources)
    infos = jnp.sum(
        jnp.where(
            (sources[:, None] == jnp.arange(32)[None, :])[:, :, None],
            heard[None, :, : 3 * PAIR_ROWS],
            0.0,
        ),
        axis=1,
    ).reshape(-1, 3)
    infos = jnp.concatenate(
        [infos[:, :2], infos[:, 2:3] - (shard * table_rows).astype(jnp.float32)], axis=1
    )
    infos = jnp.pad(infos, ((0, 0), (0, 125)))
    grad_head = head_grad_call(head_rows, kept, stat, infos)[:table_rows]
    place_x = place[:TOKENS]
    sent = low(dot_tn(place_x, dx))
    back_rows = lax.all_to_all(sent, SHARD_AXES, 0, 0, tiled=True)
    take_back = (asked_rows[None, :] == jnp.arange(table_rows)[:, None]).astype(jnp.bfloat16)

    def embed_slow():
        all_dx = lax.all_gather(dx, ("y", "core"), axis=0, tiled=True).astype(jnp.float32)
        held_rows = table_rows * 8
        local = token_ids.reshape(-1) - vocab_index * held_rows
        inside = (local >= 0) & (local < held_rows)
        grad = (
            jnp.zeros((held_rows, D), jnp.float32)
            .at[jnp.clip(local, 0, held_rows - 1)]
            .add(jnp.where(inside[:, None], all_dx, 0.0))
        )
        return lax.psum_scatter(grad, ("z", "x"), scatter_dimension=0, tiled=True)

    grad_embed = lax.cond(any_spill, embed_slow, lambda: dot_nn(take_back, back_rows))
    new_embed = adam_step(tables[0], grad_embed, table_moment[0], table_second[0], 0.3)
    new_head = adam_step(tables[1], grad_head, table_moment[1], table_second[1], 0.02)
    new_tables, new_table_moment, new_table_second = (
        jnp.stack([e, h]) for e, h in zip(new_embed, new_head)
    )
    new_gains, new_gain_moment, new_gain_second = adam_step(
        gains, gain_grad, gain_moment, gain_second, GAIN_RATE
    )
    return (
        new_blocks,
        block_grads,
        new_left,
        new_right,
        new_tables,
        new_table_moment,
        new_table_second,
        new_gains,
        new_gain_moment,
        new_gain_second,
        loss_sum,
    )


def solution(mesh):
    tuned = mesh.shape["dp"] == 8 and mesh.shape["vocab"] == 4
    if tuned:
        dp, vocab = ("z", "x"), ("y", "core")
        where = Mesh(mesh.devices.reshape(4, 2, 2, 2), AXES)
        body = per_core
    else:
        dp, vocab = ("dp",), ("vocab",)
        where = mesh
        body = per_device
    placed = (
        P(dp, None, None),
        P(dp, None),
        P(dp, None, None),
        P(dp, None),
        P(),
        P(dp, vocab, None),
        P(dp, None, None),
        P(dp, None, None),
        P(dp, None, None),
        P(dp, None, None),
        P(None, vocab + dp, None),
        P(None, vocab + dp, None),
        P(None, vocab + dp, None),
        P(),
        P(),
        P(),
    )
    return jax.shard_map(
        body,
        mesh=where,
        in_specs=placed,
        out_specs=(
            P(dp, vocab, None),
            P(dp, vocab, None),
            P(dp, None, None),
            P(dp, None, None),
            P(None, vocab + dp, None),
            P(None, vocab + dp, None),
            P(None, vocab + dp, None),
            P(),
            P(),
            P(),
            P(),
        ),
        check_vma=False,
    )
```

```python
import functools
import math

import jax
import jax.numpy as jnp
from jax import lax
from jax.experimental import pallas as pl
from jax.experimental.layout import Layout, with_layout_constraint
from jax.experimental.pallas import tpu as pltpu
from jax.sharding import Mesh
from jax.sharding import PartitionSpec as P

D = 768
HEADS = 12
HDIM = 64
FF = 3072
SLOT = 64
MB = 2
CMP = 16
STEP = 10
BC = 384
NBLK = 32


NORM_EPS = 1e-05
DPO_BETA = 0.02
ROPE_BASE = 10000.0
ADAM_ONE = 0.9
ADAM_TWO = 0.999
ADAM_EPS = 1e-08
WEIGHT_DECAY = 0.01
GAIN_RATE = 0.3
STAT_DECAY = 0.5
SHAMPOO_RATE = 0.5
MASKED = -1e30


def joined(value, axis, join):
    pieces = jax.tree.map(lambda part: lax.all_gather(part, axis), value)
    head = jax.tree.map(lambda part: part[0], pieces)
    tail = jax.tree.map(lambda part: part[1:], pieces)
    so_far, _ = lax.scan(lambda so_far, section: (join(so_far, section), None), head, tail)
    return so_far


def mult(left, right):
    return jnp.dot(left, right, preferred_element_type=jnp.float32)


def mult_t(left, right):
    return lax.dot_general(
        left, right, (((0,), (0,)), ((), ())), preferred_element_type=jnp.float32
    )


def mult_nt(left, right):
    return lax.dot_general(
        left, right, (((1,), (1,)), ((), ())), preferred_element_type=jnp.float32
    )


def project(rows, group):
    product = jnp.einsum("td,ndk->tnk", rows, group, preferred_element_type=jnp.float32)
    return product.reshape(rows.shape[0], group.shape[0] * BC)


def project_back(grad, group):
    return jnp.einsum(
        "tnk,ndk->td",
        grad.reshape(grad.shape[0], group.shape[0], BC),
        group,
        preferred_element_type=jnp.float32,
    )


def block_grad(rows, grad, number):
    return jnp.einsum(
        "td,tnk->ndk",
        rows,
        grad.reshape(grad.shape[0], number, BC),
        preferred_element_type=jnp.float32,
    )


def down_forward(mix, down):
    row_total = mix.shape[0]
    product = jnp.einsum(
        "trd,rjdk->tjk",
        mix.reshape(row_total, FF // D, D),
        down.reshape(FF // D, D // BC, D, BC),
        preferred_element_type=jnp.float32,
    )
    return product.reshape(row_total, D)


def down_back(grad, down):
    row_total = grad.shape[0]
    product = jnp.einsum(
        "tjk,rjdk->trd",
        grad.reshape(row_total, D // BC, BC),
        down.reshape(FF // D, D // BC, D, BC),
        preferred_element_type=jnp.float32,
    )
    return product.reshape(row_total, FF)


def down_grad(mix, grad):
    row_total = mix.shape[0]
    product = jnp.einsum(
        "trd,tjk->rjdk",
        mix.reshape(row_total, FF // D, D),
        grad.reshape(row_total, D // BC, BC),
        preferred_element_type=jnp.float32,
    )
    return product.reshape(-1, D, BC)


def groups(weights):
    col_blocks = D // BC
    ff_blocks = FF // BC
    base_gate = 4 * col_blocks
    return (
        weights[0:col_blocks],
        weights[col_blocks : 2 * col_blocks],
        weights[2 * col_blocks : 3 * col_blocks],
        weights[3 * col_blocks : base_gate],
        weights[base_gate : base_gate + ff_blocks],
        weights[base_gate + ff_blocks : base_gate + 2 * ff_blocks],
        weights[base_gate + 2 * ff_blocks :],
    )


def rms_forward(values, gain):
    return values * lax.rsqrt(jnp.mean(values * values, axis=-1, keepdims=True) + NORM_EPS) * gain


def rms_backward(values, gain, grad):
    scale = lax.rsqrt(jnp.mean(values * values, axis=-1, keepdims=True) + NORM_EPS)
    inner = jnp.mean(values * gain * grad, axis=-1, keepdims=True)
    back = scale * gain * grad - values * scale**3 * inner
    return (back, jnp.sum(grad * values * scale, axis=0))


def angles():
    inv_freq = ROPE_BASE ** (-jnp.arange(HDIM // 2).astype(jnp.float32) * 2.0 / HDIM)
    phase_grid = jnp.arange(SLOT).astype(jnp.float32)[:, None] * inv_freq[None, :]
    return (jnp.cos(phase_grid), jnp.sin(phase_grid))


def rotate(values, cosine, sine, direction):
    half_dim = HDIM // 2
    lead_half = values[..., :half_dim]
    tail_half = values[..., half_dim:]
    cos_grid = cosine[None, :, None, :]
    sin_grid = direction * sine[None, :, None, :]
    return jnp.concatenate(
        [lead_half * cos_grid - tail_half * sin_grid, tail_half * cos_grid + lead_half * sin_grid],
        axis=-1,
    )


def attend_scores(q_rot, k_rot, len_vec):
    raw = jnp.einsum(
        "nqhd,nkhd->nhqk", q_rot, k_rot, preferred_element_type=jnp.float32
    ) / math.sqrt(HDIM)
    places = jnp.arange(SLOT)
    valid = (places[None, :] <= places[:, None])[None, None] & (
        places[None, None, None, :] < len_vec[:, None, None, None]
    )
    return jnp.where(valid, raw, MASKED)


def layer_forward(inputs, len_vec, gains, mats, cosine, sine):
    w_query, w_key, w_value, w_out, w_gate, w_up, w_down = mats
    seq_count = inputs.shape[0] // SLOT

    def to_heads(values):
        return values.reshape(seq_count, SLOT, HEADS, HDIM)

    a_low = rms_forward(inputs, gains[0]).astype(jnp.bfloat16)
    q_rot = rotate(to_heads(project(a_low, w_query)), cosine, sine, 1.0).astype(jnp.bfloat16)
    k_rot = rotate(to_heads(project(a_low, w_key)), cosine, sine, 1.0).astype(jnp.bfloat16)
    v_heads = to_heads(project(a_low, w_value)).astype(jnp.bfloat16)
    scores = attend_scores(q_rot, k_rot, len_vec)
    row_max = jnp.max(scores, axis=-1, keepdims=True)
    log_total = jnp.log(jnp.sum(jnp.exp(scores - row_max), axis=-1, keepdims=True)) + row_max
    p_low = jnp.exp(scores - log_total).astype(jnp.bfloat16)
    att_out = jnp.einsum("nhqk,nkhd->nqhd", p_low, v_heads, preferred_element_type=jnp.float32)
    att_out = att_out.reshape(seq_count * SLOT, D).astype(jnp.bfloat16)
    h_mid = inputs + project(att_out, w_out)
    b_low = rms_forward(h_mid, gains[1]).astype(jnp.bfloat16)
    gate_pre = project(b_low, w_gate)
    up_pre = project(b_low, w_up)
    mix_low = (jax.nn.silu(gate_pre) * up_pre).astype(jnp.bfloat16)
    h_out = h_mid + down_forward(mix_low, w_down)
    return (
        h_out,
        (a_low, q_rot, k_rot, v_heads, log_total, att_out, h_mid, b_low, gate_pre, up_pre, mix_low),
    )


def layer_backward(inputs, len_vec, gains, mats, cosine, sine, saved, grad_out):
    w_query, w_key, w_value, w_out, w_gate, w_up, w_down = mats
    a_low, q_rot, k_rot, v_heads, log_total, att_out, h_mid, b_low, gate_pre, up_pre, mix_low = (
        saved
    )
    seq_count = inputs.shape[0] // SLOT
    grad_branch = grad_out.astype(jnp.bfloat16)
    grad_mix = down_back(grad_branch, w_down)
    sigmoid_gate = jax.nn.sigmoid(gate_pre)
    grad_gate = (grad_mix * up_pre * sigmoid_gate * (1.0 + gate_pre * (1.0 - sigmoid_gate))).astype(
        jnp.bfloat16
    )
    grad_up = (grad_mix * gate_pre * sigmoid_gate).astype(jnp.bfloat16)
    grad_b = project_back(grad_gate, w_gate) + project_back(grad_up, w_up)
    back_mid, gain_mid = rms_backward(h_mid, gains[1], grad_b)
    grad_mid = grad_out + back_mid
    grad_attn = grad_mid.astype(jnp.bfloat16)
    grad_att = (
        project_back(grad_attn, w_out).astype(jnp.bfloat16).reshape(seq_count, SLOT, HEADS, HDIM)
    )
    p_full = jnp.exp(attend_scores(q_rot, k_rot, len_vec) - log_total)
    grad_p = jnp.einsum("nqhd,nkhd->nhqk", grad_att, v_heads, preferred_element_type=jnp.float32)
    grad_s = (p_full * (grad_p - jnp.sum(p_full * grad_p, axis=-1, keepdims=True))).astype(
        jnp.bfloat16
    )
    grad_q = jnp.einsum(
        "nhqk,nkhd->nqhd", grad_s, k_rot, preferred_element_type=jnp.float32
    ) / math.sqrt(HDIM)
    grad_k = jnp.einsum(
        "nhqk,nqhd->nkhd", grad_s, q_rot, preferred_element_type=jnp.float32
    ) / math.sqrt(HDIM)
    grad_v = jnp.einsum(
        "nhqk,nqhd->nkhd", p_full.astype(jnp.bfloat16), grad_att, preferred_element_type=jnp.float32
    )
    row_total = seq_count * SLOT
    grad_q = rotate(grad_q, cosine, sine, -1.0).reshape(row_total, D).astype(jnp.bfloat16)
    grad_k = rotate(grad_k, cosine, sine, -1.0).reshape(row_total, D).astype(jnp.bfloat16)
    grad_v = grad_v.reshape(row_total, D).astype(jnp.bfloat16)
    grad_a = (
        project_back(grad_q, w_query) + project_back(grad_k, w_key) + project_back(grad_v, w_value)
    )
    back_in, gain_in = rms_backward(inputs, gains[0], grad_a)
    operands = (
        a_low,
        grad_q,
        grad_k,
        grad_v,
        att_out,
        grad_attn,
        b_low,
        grad_gate,
        grad_up,
        mix_low,
        grad_branch,
    )
    return (grad_mid + back_in, operands, jnp.stack([gain_in, gain_mid]))


def weight_grads(operands):
    (
        a_low,
        grad_q,
        grad_k,
        grad_v,
        att_out,
        grad_attn,
        b_low,
        grad_gate,
        grad_up,
        mix_low,
        grad_branch,
    ) = operands
    col_blocks = D // BC
    ff_blocks = FF // BC
    return jnp.concatenate(
        [
            block_grad(a_low, grad_q, col_blocks),
            block_grad(a_low, grad_k, col_blocks),
            block_grad(a_low, grad_v, col_blocks),
            block_grad(att_out, grad_attn, col_blocks),
            block_grad(b_low, grad_gate, ff_blocks),
            block_grad(b_low, grad_up, ff_blocks),
            down_grad(mix_low, grad_branch),
        ],
        axis=0,
    )


def combine_parts(earlier, later):
    max_one, sum_one, pick_one = earlier
    max_two, sum_two, pick_two = later
    joint_max = jnp.maximum(max_one, max_two)
    joint_sum = sum_one * jnp.exp(max_one - joint_max) + sum_two * jnp.exp(max_two - joint_max)
    return (joint_max, joint_sum, pick_one + pick_two)


def adam_step(weight, grad, moment, second, rate):
    moment = ADAM_ONE * moment + (1.0 - ADAM_ONE) * grad
    second = ADAM_TWO * second + (1.0 - ADAM_TWO) * grad * grad
    ratio = moment / (1.0 - ADAM_ONE**STEP) / (jnp.sqrt(second / (1.0 - ADAM_TWO**STEP)) + ADAM_EPS)
    return (weight - rate * (ratio + WEIGHT_DECAY * weight), moment, second)


def per_device(
    dp,
    vocab,
    token_ids,
    lengths,
    comp_mask,
    ref_logp,
    owner,
    blocks,
    left_stat,
    right_stat,
    left_root,
    right_root,
    tables,
    table_moment,
    table_second,
    gains,
    gain_moment,
    gain_second,
):
    vocab_count = lax.axis_size(vocab)
    vocab_index = lax.axis_index(vocab)
    row_share = blocks.shape[1]
    cosine, sine = angles()
    tables_low = lax.all_gather(tables.astype(jnp.bfloat16), dp, axis=1, tiled=True)
    vocab_rows = tables_low.shape[1]
    local_ids = token_ids.reshape(-1) - vocab_index * vocab_rows
    inside = (local_ids >= 0) & (local_ids < vocab_rows)
    safe_ids = jnp.clip(local_ids, 0, vocab_rows - 1)
    looked = jnp.where(inside[:, None], jnp.take(tables_low[0], safe_ids, axis=0), 0).astype(
        jnp.float32
    )
    embedded = lax.psum_scatter(
        looked.astype(jnp.bfloat16), vocab, scatter_dimension=0, tiled=True
    ).astype(jnp.float32)
    rows_all = lax.all_gather(blocks.astype(jnp.bfloat16), vocab, axis=1, tiled=True)
    slots_all = lax.all_gather(rows_all, dp, axis=0, tiled=True)
    kept_mats = groups(jnp.take(slots_all, owner, axis=0))
    gain_total = jnp.zeros((3, D), jnp.float32)
    loss_own = jnp.zeros((), jnp.float32)
    grad_inputs = []
    operand_list = []
    logit_grads = []
    head_inputs = []
    for micro in range(MB):
        own_pair = vocab_index * MB + micro
        rows_in = embedded[micro * 2 * SLOT : (micro + 1) * 2 * SLOT]
        len_own = lax.dynamic_index_in_dim(lengths, own_pair, 0, keepdims=False)
        h_out, saved = layer_forward(rows_in, len_own, gains, kept_mats, cosine, sine)
        pos_own = len_own[:, None] - 1 - CMP + jnp.arange(CMP)[None, :]
        picked_rows = jnp.take_along_axis(
            h_out.reshape(2, SLOT, D), pos_own[:, :, None], axis=1
        ).reshape(2 * CMP, D)
        c_low = rms_forward(picked_rows, gains[2]).astype(jnp.bfloat16)
        all_rows = lax.all_gather(c_low, vocab, axis=0, tiled=True)
        ids_sel = token_ids[micro::MB]
        lens_sel = lengths[micro::MB]
        mask_sel = comp_mask[micro::MB].astype(jnp.float32)
        ref_sel = ref_logp[micro::MB]
        pos_sel = lens_sel[:, :, None] - 1 - CMP + jnp.arange(CMP)[None, None, :]
        target = (
            jnp.take_along_axis(ids_sel, pos_sel + 1, axis=2).reshape(-1) - vocab_index * vocab_rows
        )
        logits = mult_nt(all_rows, tables_low[1])
        one_hot = jnp.arange(vocab_rows)[None, :] == target[:, None]
        row_max = jnp.max(logits, axis=1)
        row_sum = jnp.sum(jnp.exp(logits - row_max[:, None]), axis=1)
        row_pick = jnp.sum(jnp.where(one_hot, logits, 0.0), axis=1)
        full_max, full_sum, full_pick = joined((row_max, row_sum, row_pick), vocab, combine_parts)
        log_norm = full_max + jnp.log(full_sum)
        seq_logp = jnp.sum((full_pick - log_norm).reshape(vocab_count, 2, CMP) * mask_sel, axis=2)
        margin = DPO_BETA * (seq_logp[:, 0] - ref_sel[:, 0] - (seq_logp[:, 1] - ref_sel[:, 1]))
        loss_own = loss_own + jnp.take(jax.nn.softplus(-margin), vocab_index)
        pair_weight = -DPO_BETA * jax.nn.sigmoid(-margin)
        grad_tok = (jnp.stack([pair_weight, -pair_weight], axis=1)[:, :, None] * mask_sel).reshape(
            -1
        )
        grad_logits = (
            grad_tok[:, None] * (one_hot.astype(jnp.float32) - jnp.exp(logits - log_norm[:, None]))
        ).astype(jnp.bfloat16)
        logit_grads.append(grad_logits)
        head_inputs.append(all_rows)
        grad_c = lax.psum_scatter(
            mult(grad_logits, tables_low[1]), vocab, scatter_dimension=0, tiled=True
        )
        back_rows, gain_head = rms_backward(picked_rows, gains[2], grad_c)
        seq_index = jnp.arange(2)[:, None]
        grad_top = (
            jnp.zeros((2, SLOT, D), jnp.float32)
            .at[seq_index, pos_own]
            .add(back_rows.reshape(2, CMP, D))
        )
        grad_in, operands, gains_now = layer_backward(
            rows_in, len_own, gains, kept_mats, cosine, sine, saved, grad_top.reshape(2 * SLOT, D)
        )
        operand_list.append(operands)
        gain_total = gain_total + jnp.concatenate([gains_now, gain_head[None]], axis=0)
        grad_inputs.append(grad_in)
    joined_ops = tuple(
        (
            jnp.concatenate([ops[i] for ops in operand_list], axis=0)
            for i in range(len(operand_list[0]))
        )
    )
    block_order = weight_grads(joined_ops)
    grad_head = mult_t(jnp.concatenate(logit_grads, axis=0), jnp.concatenate(head_inputs, axis=0))
    grad_rows = lax.all_gather(
        jnp.concatenate(grad_inputs, axis=0).astype(jnp.bfloat16), vocab, axis=0, tiled=True
    ).astype(jnp.float32)
    grad_embed = (
        jnp.zeros((vocab_rows, D), jnp.float32)
        .at[safe_ids]
        .add(jnp.where(inside[:, None], grad_rows, 0.0))
    )
    table_grad = lax.psum_scatter(
        jnp.stack([grad_embed, grad_head]).astype(jnp.bfloat16),
        dp,
        scatter_dimension=1,
        tiled=True,
    ).astype(jnp.float32)
    inverse = jnp.zeros((NBLK,), jnp.int32).at[owner].set(jnp.arange(NBLK, dtype=jnp.int32))
    slotted = jnp.take(block_order, inverse, axis=0)
    summed = lax.psum_scatter(slotted.astype(jnp.bfloat16), dp, scatter_dimension=0, tiled=True)
    share_part = lax.psum_scatter(summed, vocab, scatter_dimension=1, tiled=True).astype(
        jnp.float32
    )
    whole = lax.all_gather(share_part.astype(jnp.bfloat16), vocab, axis=1, tiled=True).astype(
        share_part.dtype
    )
    highest = lax.Precision.HIGHEST
    new_left = STAT_DECAY * left_stat + (1.0 - STAT_DECAY) * jnp.einsum(
        "bij,bkj->bik", whole, whole, precision=highest
    )
    new_right = STAT_DECAY * right_stat + (1.0 - STAT_DECAY) * jnp.einsum(
        "bji,bjk->bik", whole, whole, precision=highest
    )
    direction = jnp.einsum("bij,bjk->bik", left_root, whole, precision=highest)
    direction = jnp.einsum("bij,bjk->bik", direction, right_root, precision=highest)
    new_blocks = blocks - SHAMPOO_RATE * lax.dynamic_slice_in_dim(
        direction, vocab_index * row_share, row_share, 1
    )
    loss_sum, gain_grad = lax.psum((loss_own, gain_total), dp + vocab)
    rates = jnp.array([0.3, 0.02], jnp.float32)[:, None, None]
    new_tables, new_table_moment, new_table_second = adam_step(
        tables, table_grad, table_moment, table_second, rates
    )
    new_gains, new_gain_moment, new_gain_second = adam_step(
        gains, gain_grad, gain_moment, gain_second, GAIN_RATE
    )
    return (
        new_blocks,
        share_part,
        new_left,
        new_right,
        new_tables,
        new_table_moment,
        new_table_second,
        new_gains,
        new_gain_moment,
        new_gain_second,
        loss_sum,
    )


PAIR_ROWS = MB * 2 * CMP
TOKENS = MB * 2 * SLOT
CAP = 24
MSG = 32
EXT = D + 128
AXES = ("z", "x", "y", "core")
SHARD_AXES = ("y", "core", "z", "x")
VMEM_LIMIT = 60 * 1024 * 1024

AT_A = 0
AT_AP = AT_A + TOKENS
AT_O = AT_AP + PAIR_ROWS
AT_B = AT_O + PAIR_ROWS
AT_Z = AT_B + PAIR_ROWS
LEFT_ROWS = AT_Z + (FF // D) * PAIR_ROWS
LEFT_KINDS = (LEFT_ROWS - AT_AP) // PAIR_ROWS
AT_DK = 0
AT_DV = AT_DK + TOKENS
AT_DQ = AT_DV + TOKENS
AT_DO = AT_DQ + PAIR_ROWS
AT_DGATE = AT_DO + PAIR_ROWS
AT_DUP = AT_DGATE + (FF // D) * PAIR_ROWS
AT_DH = AT_DUP + (FF // D) * PAIR_ROWS
RIGHT_ROWS = AT_DH + PAIR_ROWS


def flat_of(z, x, y, c):
    return ((z * 2 + x) * 2 + y) * 2 + c


def moves(target):
    pairs = []
    for z in range(4):
        for x in range(2):
            for y in range(2):
                for c in range(2):
                    pairs.append((flat_of(z, x, y, c), flat_of(*target(z, x, y, c))))
    return pairs


def hop_one(value):
    return lax.ppermute(
        value,
        AXES,
        moves(lambda z, x, y, c: (z, 1 - x, y, c) if c == 0 else (z, x, 1 - y, c)),
    )


def hop_two(value):
    return lax.ppermute(
        value,
        AXES,
        moves(lambda z, x, y, c: (z, x, 1 - y, c) if c == 0 else (z, 1 - x, y, c)),
    )


def hop_core(value):
    return lax.ppermute(value, AXES, moves(lambda z, x, y, c: (z, x, y, 1 - c)))


def hop_y(value):
    return lax.ppermute(value, AXES, moves(lambda z, x, y, c: (z, x, 1 - y, c)))


def ring(value, step):
    return lax.ppermute(value, AXES, moves(lambda z, x, y, c: ((z + step) % 4, x, y, c)))


def after(value, *others):
    return lax.optimization_barrier((value,) + others)[0]


def together(*values):
    return lax.optimization_barrier(values)


def all_round(chunk):
    return jnp.stack([chunk] + [ring(chunk, step) for step in range(1, 4)])


def spread(chunk, wait=()):
    if wait:
        chunk = after(chunk, *wait)
    around = [ring(chunk, step) for step in range(1, 4)]
    line = jnp.stack([chunk] + around)
    one = hop_one(line)
    two = hop_two(line)
    both = hop_two(one)
    return jnp.stack([line, one, two, both]), around


def dot_nn(left, right):
    return lax.dot_general(left, right, (((1,), (0,)), ((), ())), preferred_element_type=jnp.float32)


def dot_nt(left, right):
    return lax.dot_general(left, right, (((1,), (1,)), ((), ())), preferred_element_type=jnp.float32)


def dot_tn(left, right):
    return lax.dot_general(left, right, (((0,), (0,)), ((), ())), preferred_element_type=jnp.float32)


def low(value):
    return value.astype(jnp.bfloat16)


def high(value):
    return value.astype(jnp.float32)


def place_of(coord, other_core, rel):
    core = coord[3] + other_core * (1 - 2 * coord[3])
    first = rel & 1
    second = rel >> 1
    x_flip = first + core * (second - first)
    y_flip = second + core * (first - second)
    x = coord[1] + x_flip * (1 - 2 * coord[1])
    y = coord[2] + y_flip * (1 - 2 * coord[2])
    return x, y, core


def start_weights(coord, parts, held, sem):
    def start(source, slots, y, core):
        row = pl.multiple_of(192 * (2 * y + core), 64)
        pltpu.make_async_copy(source, held.at[slots, pl.ds(row, 192)], sem).start()

    for other_core in range(2):
        for rel in range(4):
            x, y, core = place_of(coord, other_core, rel)
            pair, third, fourth = (
                parts[2 * rel + other_core],
                parts[8 + 2 * rel + other_core],
                parts[16 + 2 * rel + other_core],
            )

            def one(n, carry):
                back = (coord[0] + 4 - n) & 3
                start(pair.at[n], pl.ds(8 * n + 4 * x, 2), y, core)
                start(third.at[n], 8 * back + 4 * x + 2, y, core)
                start(fourth.at[n], 8 * back + 4 * x + 3, y, core)
                return carry

            lax.fori_loop(0, 4, one, 0)


def wait_weights(held, sem):
    pltpu.make_async_copy(held, held, sem).wait()


def iota(shape, axis):
    return lax.broadcasted_iota(jnp.int32, shape, axis)


def pick_rows(lens):
    row = iota((PAIR_ROWS, 1), 0)
    seq = row >> 4
    length = jnp.where(
        seq == 0, lens[0], jnp.where(seq == 1, lens[1], jnp.where(seq == 2, lens[2], lens[3]))
    )
    return seq, length - 1 - CMP + (row & 15)


def masks(lens):
    seq, pos = pick_rows(lens)
    col = iota((PAIR_ROWS, TOKENS), 1)
    same = (col >> 6) == seq
    key = col & 63
    return same & (key <= pos), same & (key == pos)


def turn(chunk, cosine, sine, sign):
    lane = iota(chunk.shape, 1)
    swapped = jnp.where((lane & 63) < 32, pltpu.roll(chunk, 96, 1), pltpu.roll(chunk, 32, 1))
    return chunk * cosine + swapped * (sine * sign)


def scale_of(values):
    return lax.rsqrt(jnp.mean(values * values, axis=-1, keepdims=True) + NORM_EPS)


def rms_back(values, gain, grad):
    scale = scale_of(values)
    inner = jnp.mean(values * gain * grad, axis=-1, keepdims=True)
    back = scale * gain * grad - values * (scale * scale * scale) * inner
    return back, jnp.sum(grad * values * scale, axis=0, keepdims=True)


def forward_kernel(owner, coord, lens, x, gains, cos_q, sin_q, cos_k, sin_k, *rest):
    parts, rest = rest[:24], rest[24:]
    left, q_out, k_out, v_out, h1_out, gate_out, up_out, h2_out, c_out = rest[:9]
    held, sem = rest[9:]
    start_weights(coord, parts, held, sem)
    values = high(x[...])
    a_low = low(values * scale_of(values) * gains[0:1, :])
    left[AT_A:AT_AP] = a_low
    valid, chosen = masks(lens)
    select = jnp.where(chosen, 1.0, 0.0).astype(jnp.bfloat16)
    a_pick = low(dot_nn(select, a_low))
    left[AT_AP:AT_O] = a_pick
    x_pick = dot_nn(select, x[...])
    wait_weights(held, sem)
    for j in range(2):
        q = dot_nn(a_pick, held[owner[j]])
        k = dot_nn(a_low, held[owner[2 + j]])
        v_out[:, j * BC : (j + 1) * BC] = low(dot_nn(a_low, held[owner[4 + j]]))
        for i in range(3):
            at = slice(j * BC + i * 128, j * BC + (i + 1) * 128)
            q_out[:, at] = low(turn(q[:, i * 128 : (i + 1) * 128], cos_q[...], sin_q[...], 1.0))
            k_out[:, at] = low(turn(k[:, i * 128 : (i + 1) * 128], cos_k[...], sin_k[...], 1.0))
    lane = iota((TOKENS, 128), 1)
    zero = jnp.zeros((TOKENS, 128), jnp.bfloat16)
    for p in range(HEADS // 2):
        at = slice(p * 128, (p + 1) * 128)
        total = jnp.zeros((PAIR_ROWS, 128), jnp.float32)
        for h in range(2):
            mine = (lane >> 6) == h
            s = dot_nt(q_out[:, at], jnp.where(mine, k_out[:, at], zero)) * (1.0 / math.sqrt(HDIM))
            s = jnp.where(valid, s, MASKED)
            e = jnp.exp(s - jnp.max(s, axis=-1, keepdims=True))
            prob = low(e / jnp.sum(e, axis=-1, keepdims=True))
            total = total + dot_nn(prob, jnp.where(mine, v_out[:, at], zero))
        left[AT_O:AT_B, at] = low(total)
    for j in range(2):
        at = slice(j * BC, (j + 1) * BC)
        h1_out[:, at] = x_pick[:, at] + dot_nn(left[AT_O:AT_B], held[owner[6 + j]])
    h1 = h1_out[...]
    b_low = low(h1 * scale_of(h1) * gains[1:2, :])
    left[AT_B:AT_Z] = b_low
    for j in range(FF // BC):
        at = slice(j * BC, (j + 1) * BC)
        gate = dot_nn(b_low, held[owner[8 + j]])
        up = dot_nn(b_low, held[owner[16 + j]])
        gate_out[:, at] = gate
        up_out[:, at] = up
        row = AT_Z + j // 2 * PAIR_ROWS
        left[row : row + PAIR_ROWS, j % 2 * BC : (j % 2 + 1) * BC] = low(
            gate * jax.nn.sigmoid(gate) * up
        )
    for j in range(2):
        total = h1[:, j * BC : (j + 1) * BC]
        for r in range(FF // D):
            row = AT_Z + r * PAIR_ROWS
            total = total + dot_nn(left[row : row + PAIR_ROWS], held[owner[24 + 2 * r + j]])
        h2_out[:, j * BC : (j + 1) * BC] = total
    h2 = h2_out[...]
    c_out[...] = low(h2 * scale_of(h2) * gains[2:3, :])


def vmem(number):
    return [pl.BlockSpec(memory_space=pltpu.VMEM)] * number


def smem(number):
    return [pl.BlockSpec(memory_space=pltpu.SMEM)] * number


def anywhere(number):
    return [pl.BlockSpec(memory_space=pl.ANY)] * number


def forward_call(owner, coord, lens, x, gains, turns, parts):
    def made(rows, columns, kind):
        return jax.ShapeDtypeStruct((rows, columns), kind)

    return pl.pallas_call(
        forward_kernel,
        out_shape=(
            made(LEFT_ROWS, D, jnp.bfloat16),
            made(PAIR_ROWS, D, jnp.bfloat16),
            made(TOKENS, D, jnp.bfloat16),
            made(TOKENS, D, jnp.bfloat16),
            made(PAIR_ROWS, D, jnp.float32),
            made(PAIR_ROWS, FF, jnp.float32),
            made(PAIR_ROWS, FF, jnp.float32),
            made(PAIR_ROWS, D, jnp.float32),
            made(PAIR_ROWS, D, jnp.bfloat16),
        ),
        in_specs=smem(3) + vmem(6) + anywhere(24),
        out_specs=tuple(vmem(9)),
        scratch_shapes=[
            pltpu.VMEM((NBLK, D, BC), jnp.bfloat16),
            pltpu.SemaphoreType.DMA,
        ],
        compiler_params=pltpu.CompilerParams(vmem_limit_bytes=VMEM_LIMIT),
        name="layer_forward",
    )(owner, coord, lens, x, gains, *turns, *parts)


def unpack(ext):
    stat = high(ext[:, D:EXT])
    top = (stat[:, 0:1] + stat[:, 1:2]) + stat[:, 2:3]
    total = (stat[:, 3:4] + stat[:, 4:5]) + stat[:, 5:6]
    return top, total, high(ext[:, :D])


def pack_stat(top, total):
    lane = iota((top.shape[0], 128), 1)
    out = jnp.zeros((top.shape[0], 128), jnp.float32)
    for first, value in ((0, top), (3, total)):
        for i in range(3):
            piece = high(low(value))
            out = jnp.where(lane == first + i, piece, out)
            value = value - piece
    return low(out)


def merge(items):
    top = items[0][0]
    for item in items[1:]:
        top = jnp.maximum(top, item[0])
    total = 0.0
    mixed = 0.0
    for item_top, item_total, item_mixed in items:
        factor = jnp.exp(item_top - top)
        total = total + item_total * factor
        mixed = mixed + item_mixed * factor
    return top, total, mixed


def merge_kernel(number, *refs):
    top, total, mixed = merge([unpack(ref[...]) for ref in refs[:number]])
    mixed = low(mixed)
    stat = pack_stat(top, total)
    outs = refs[number:]
    rows = outs[0].shape[0]
    for n, out in enumerate(outs):
        out[:, :D] = mixed[n * rows : (n + 1) * rows]
        out[:, D:EXT] = stat[n * rows : (n + 1) * rows]


def merge_call(parts, pieces=1):
    rows = 4 * PAIR_ROWS
    made = jax.ShapeDtypeStruct((rows // pieces, EXT), jnp.bfloat16)
    return pl.pallas_call(
        functools.partial(merge_kernel, len(parts)),
        grid=(1,),
        out_shape=(made,) * pieces,
        in_specs=[pl.BlockSpec((rows, EXT), lambda i, at=at: (at, 0)) for _, at in parts],
        out_specs=(pl.BlockSpec(made.shape, lambda i: (0, 0)),) * pieces,
        compiler_params=pltpu.CompilerParams(vmem_limit_bytes=VMEM_LIMIT),
        cost_estimate=pl.CostEstimate(
            flops=8 * rows * D, bytes_accessed=4 * rows * EXT, transcendentals=rows
        ),
        name="merge_parts",
    )(*[array for array, _ in parts])


def head_kernel(real, rows, head, ext, kept, stat):
    logits = dot_nt(rows[...], head[...])
    col = iota(logits.shape, 1)
    logits = jnp.where(col < real, logits, MASKED)
    top = jnp.max(logits, axis=-1, keepdims=True)
    e = jnp.exp(logits - top)
    total = jnp.sum(e, axis=-1, keepdims=True)
    e_low = low(e)
    kept[...] = e_low
    ext[:, :D] = low(dot_nn(e_low, head[...]))
    ext[:, D:EXT] = pack_stat(top, total)
    stat[...] = jnp.broadcast_to(top, stat.shape)


def head_call(rows, head, real):
    number, wide = rows.shape[0], head.shape[0]
    return pl.pallas_call(
        functools.partial(head_kernel, real),
        grid=(number // 256,),
        out_shape=(
            jax.ShapeDtypeStruct((number, EXT), jnp.bfloat16),
            jax.ShapeDtypeStruct((number, wide), jnp.bfloat16),
            jax.ShapeDtypeStruct((number, 128), jnp.float32),
        ),
        in_specs=[
            pl.BlockSpec((256, D), lambda i: (i, 0)),
            pl.BlockSpec((wide, D), lambda i: (0, 0)),
        ],
        out_specs=(
            pl.BlockSpec((256, EXT), lambda i: (i, 0)),
            pl.BlockSpec((256, wide), lambda i: (i, 0)),
            pl.BlockSpec((256, 128), lambda i: (i, 0)),
        ),
        compiler_params=pltpu.CompilerParams(vmem_limit_bytes=VMEM_LIMIT),
        cost_estimate=pl.CostEstimate(
            flops=4 * number * wide * D, bytes_accessed=2 * number * wide, transcendentals=number * wide
        ),
        name="head_forward",
    )(rows, head)


def head_grad_kernel(steps, rows_a, rows_b, kept_a, kept_b, stat_a, stat_b, info, out):
    def add(rows, kept, stat):
        weight = info[:, 0:1]
        factor = weight * jnp.exp(stat[:, 0:1] - info[:, 1:2])
        col = iota(kept.shape, 1)
        hit = col == info[:, 2:3].astype(jnp.int32)
        grad = low(jnp.where(hit, weight, 0.0) - high(kept[...]) * factor)
        return dot_tn(grad, rows[...])

    i = pl.program_id(0)

    @pl.when(i == 0)
    def _():
        out[...] = add(rows_a, kept_a, stat_a)

    @pl.when((i > 0) & (i < steps))
    def _():
        out[...] += add(rows_a, kept_a, stat_a)

    @pl.when(i >= steps)
    def _():
        out[...] += add(rows_b, kept_b, stat_b)


def head_grad_call(rows, kept, stat, info):
    number, wide = kept[0].shape
    steps = number // 256

    def pair(columns):
        return [
            pl.BlockSpec((256, columns), lambda i: (jnp.minimum(i, steps - 1), 0)),
            pl.BlockSpec((256, columns), lambda i: (jnp.maximum(i - steps, 0), 0)),
        ]

    return pl.pallas_call(
        functools.partial(head_grad_kernel, steps),
        grid=(2 * steps,),
        out_shape=jax.ShapeDtypeStruct((wide, D), jnp.float32),
        in_specs=pair(D) + pair(wide) + pair(128) + [pl.BlockSpec((256, 128), lambda i: (i, 0))],
        out_specs=pl.BlockSpec((wide, D), lambda i: (0, 0)),
        compiler_params=pltpu.CompilerParams(vmem_limit_bytes=VMEM_LIMIT),
        cost_estimate=pl.CostEstimate(
            flops=4 * number * wide * D, bytes_accessed=4 * number * wide, transcendentals=number
        ),
        name="head_grad",
    )(*rows, *kept, *stat, info)


def backward_kernel(owner, coord, lens, refs, x, gains, cos_q, sin_q, cos_k, sin_k, *rest):
    q, k, v, h1, gate, up, h2, c = rest[:8]
    truth, wanted, u0, u1, u2, u3 = rest[8:14]
    parts = rest[14:38]
    act, dx_out, gain_out, info_out, loss_out = rest[38:43]
    held, sem = rest[43:]
    start_weights(coord, parts, held, sem)
    valid, chosen = masks(lens)
    select = jnp.where(chosen, 1.0, 0.0).astype(jnp.bfloat16)
    top, total, mixed = merge([unpack(part[...]) for part in (u0, u1, u2, u3)])
    norm = top + jnp.log(total)
    target = high(truth[...])
    picked = jnp.sum(high(c[...]) * target, axis=-1, keepdims=True)
    scored = wanted[:, 0:1]
    terms = (picked - norm) * scored
    seq = iota((PAIR_ROWS, 1), 0) >> 4
    logp = [jnp.sum(jnp.where(seq == n, terms, 0.0), axis=0, keepdims=True) for n in range(2 * MB)]
    weight = jnp.zeros((PAIR_ROWS, 1), jnp.float32)
    loss = jnp.zeros((1, 1), jnp.float32)
    for n in range(MB):
        margin = DPO_BETA * ((logp[2 * n] - refs[2 * n]) - (logp[2 * n + 1] - refs[2 * n + 1]))
        loss = loss + jnp.maximum(-margin, 0.0) + jnp.log1p(jnp.exp(-jnp.abs(margin)))
        slope = -DPO_BETA * jax.nn.sigmoid(-margin)
        weight = jnp.where(seq == 2 * n, slope, jnp.where(seq == 2 * n + 1, -slope, weight))
    weight = weight * scored
    loss_out[...] = jnp.broadcast_to(loss, loss_out.shape)
    lane = iota((PAIR_ROWS, 128), 1)
    info_out[...] = jnp.where(
        lane == 0, weight, jnp.where(lane == 1, norm, jnp.where(lane == 2, wanted[:, 1:2], 0.0))
    )
    grad_c = weight * (target - mixed / total)
    d2, gain_top = rms_back(h2[...], gains[2:3, :], grad_c)
    gain_out[2:3, :] = gain_top
    d2_low = low(d2)
    act[AT_DH:RIGHT_ROWS] = d2_low
    wait_weights(held, sem)
    grad_b = jnp.zeros((PAIR_ROWS, D), jnp.float32)
    for r in range(FF // D):
        grad_mix = dot_nt(d2_low[:, :BC], held[owner[24 + 2 * r]]) + dot_nt(
            d2_low[:, BC:], held[owner[25 + 2 * r]]
        )
        at = slice(r * D, (r + 1) * D)
        gate_pre = gate[:, at]
        sig = jax.nn.sigmoid(gate_pre)
        d_gate = low(grad_mix * up[:, at] * sig * (1.0 + gate_pre * (1.0 - sig)))
        d_up = low(grad_mix * gate_pre * sig)
        act[AT_DGATE + r * PAIR_ROWS : AT_DGATE + (r + 1) * PAIR_ROWS] = d_gate
        act[AT_DUP + r * PAIR_ROWS : AT_DUP + (r + 1) * PAIR_ROWS] = d_up
        for j in range(2):
            cut = slice(j * BC, (j + 1) * BC)
            grad_b = grad_b + dot_nt(d_gate[:, cut], held[owner[8 + 2 * r + j]])
            grad_b = grad_b + dot_nt(d_up[:, cut], held[owner[16 + 2 * r + j]])
    back, gain_mid = rms_back(h1[...], gains[1:2, :], grad_b)
    gain_out[1:2, :] = gain_mid
    d1 = d2 + back
    d1_low = low(d1)
    act[AT_DO:AT_DGATE] = d1_low
    d_att = low(
        dot_nt(d1_low[:, :BC], held[owner[6]]) + dot_nt(d1_low[:, BC:], held[owner[7]])
    )
    lane_k = iota((TOKENS, 128), 1)
    zero_k = jnp.zeros((TOKENS, 128), jnp.bfloat16)
    zero_q = jnp.zeros((PAIR_ROWS, 128), jnp.bfloat16)
    root = 1.0 / math.sqrt(HDIM)
    for p in range(HEADS // 2):
        at = slice(p * 128, (p + 1) * 128)
        d_q = jnp.zeros((PAIR_ROWS, 128), jnp.float32)
        d_k = jnp.zeros((TOKENS, 128), jnp.float32)
        d_v = jnp.zeros((TOKENS, 128), jnp.float32)
        for h in range(2):
            mine_k = (lane_k >> 6) == h
            mine_q = (lane >> 6) == h
            k_one = jnp.where(mine_k, k[:, at], zero_k)
            q_one = jnp.where(mine_q, q[:, at], zero_q)
            do_one = jnp.where(mine_q, d_att[:, at], zero_q)
            s = dot_nt(q_one, k_one) * root
            s = jnp.where(valid, s, MASKED)
            e = jnp.exp(s - jnp.max(s, axis=-1, keepdims=True))
            prob = e / jnp.sum(e, axis=-1, keepdims=True)
            d_p = dot_nt(do_one, v[:, at])
            d_s = low(prob * (d_p - jnp.sum(prob * d_p, axis=-1, keepdims=True)))
            d_q = d_q + dot_nn(d_s, k_one)
            d_k = d_k + dot_tn(d_s, q_one)
            d_v = d_v + dot_tn(low(prob), do_one)
        act[AT_DQ:AT_DO, at] = low(turn(d_q * root, cos_q[...], sin_q[...], -1.0))
        act[AT_DK:AT_DV, at] = low(turn(d_k * root, cos_k[...], sin_k[...], -1.0))
        act[AT_DV:AT_DQ, at] = low(d_v)
    d_q_all = low(dot_tn(select, act[AT_DQ:AT_DO]))
    grad_a = jnp.zeros((TOKENS, D), jnp.float32)
    for j in range(2):
        cut = slice(j * BC, (j + 1) * BC)
        grad_a = grad_a + dot_nt(d_q_all[:, cut], held[owner[j]])
        grad_a = grad_a + dot_nt(act[AT_DK:AT_DV, cut], held[owner[2 + j]])
        grad_a = grad_a + dot_nt(act[AT_DV:AT_DQ, cut], held[owner[4 + j]])
    back_in, gain_in = rms_back(high(x[...]), gains[0:1, :], grad_a)
    gain_out[0:1, :] = gain_in
    rest_low = low(d1 - high(d1_low))
    dx_out[...] = low(back_in + dot_tn(select, d1_low) + dot_tn(select, rest_low))


def backward_call(owner, coord, lens, refs, x, gains, turns, saved, truth, wanted, parts_u, parts):
    return pl.pallas_call(
        backward_kernel,
        out_shape=(
            jax.ShapeDtypeStruct((RIGHT_ROWS, D), jnp.bfloat16),
            jax.ShapeDtypeStruct((TOKENS, D), jnp.bfloat16),
            jax.ShapeDtypeStruct((3, D), jnp.float32),
            jax.ShapeDtypeStruct((PAIR_ROWS, 128), jnp.float32),
            jax.ShapeDtypeStruct((1, 128), jnp.float32),
        ),
        in_specs=smem(4) + vmem(6 + 8 + 2 + 4) + anywhere(24),
        out_specs=tuple(vmem(5)),
        scratch_shapes=[
            pltpu.VMEM((NBLK, D, BC), jnp.bfloat16),
            pltpu.SemaphoreType.DMA,
        ],
        compiler_params=pltpu.CompilerParams(vmem_limit_bytes=VMEM_LIMIT),
        name="layer_backward",
    )(owner, coord, lens, refs, x, gains, *turns, *saved, truth, wanted, *parts_u, *parts)


def transpose_kernel(coord, mine, theirs, picked, tokens, turned_a, turned_b):
    near_row = pl.multiple_of(192 * (2 * coord[2] + coord[3]), 64)
    far_row = pl.multiple_of(192 * (2 * (1 - coord[2]) + coord[3]), 64)
    for n in range(LEFT_KINDS):
        at = slice(AT_AP + n * PAIR_ROWS, AT_AP + (n + 1) * PAIR_ROWS)
        turned_a[...] = jnp.concatenate([mine[at], theirs[at]], axis=0).T
        picked[n, :192] = turned_a[pl.ds(near_row, 192), :]
        picked[n, 192:] = turned_a[pl.ds(far_row, 192), :]
    turned_b[:, :TOKENS] = mine[AT_A:AT_AP].T
    turned_b[:, TOKENS:] = theirs[AT_A:AT_AP].T
    tokens[:192] = turned_b[pl.ds(near_row, 192), :]
    tokens[192:] = turned_b[pl.ds(far_row, 192), :]


def transpose_call(coord, mine, theirs):
    return pl.pallas_call(
        transpose_kernel,
        out_shape=(
            jax.ShapeDtypeStruct((LEFT_KINDS, 384, 2 * PAIR_ROWS), jnp.bfloat16),
            jax.ShapeDtypeStruct((384, 2 * TOKENS), jnp.bfloat16),
        ),
        in_specs=smem(1) + vmem(2),
        out_specs=tuple(vmem(2)),
        scratch_shapes=[
            pltpu.VMEM((D, 2 * PAIR_ROWS), jnp.bfloat16),
            pltpu.VMEM((D, 2 * TOKENS), jnp.bfloat16),
        ],
        compiler_params=pltpu.CompilerParams(vmem_limit_bytes=VMEM_LIMIT),
        cost_estimate=pl.CostEstimate(
            flops=0, bytes_accessed=8 * LEFT_ROWS * D, transcendentals=0
        ),
        name="left_transposed",
    )(coord, mine, theirs)


def weight_grad_kernel(block_of, x_at, y_at, coord, picked, tokens, mine, theirs, *rest):
    pair, singles = rest[:4], (rest[4:8], rest[8:12])
    near_held, far_held, sem = rest[12:]
    first = coord[3] == 0
    for group, (k, x_flip) in enumerate((k, x_flip) for k in range(4) for x_flip in range(2)):
        x = coord[1] + x_flip * (1 - 2 * coord[1])

        def step(n, carry):
            z = n if k < 2 else (coord[0] + 4 - n) & 3
            slot = 8 * z + 4 * x + k
            block = block_of[slot]
            cut = pl.ds(pl.multiple_of((block & 1) * BC, 128), BC)
            y_row = pl.multiple_of(y_at[slot], 64)

            def put(left, rows):
                right = jnp.concatenate(
                    [mine[pl.ds(y_row, rows), cut], theirs[pl.ds(y_row, rows), cut]], axis=0
                )
                grad = low(dot_nn(left, right))
                near_held[group, n] = grad[:192]
                far_held[group, n] = grad[192:]

            wide = (block >= 2) & (block < 6)

            @pl.when(wide)
            def _():
                put(tokens[...], TOKENS)

            @pl.when(jnp.logical_not(wide))
            def _():
                put(picked[x_at[slot]], PAIR_ROWS)

            return carry

        lax.fori_loop(0, 4, step, 0)

        def send(held, rel):
            target = pair[rel].at[:, k] if k < 2 else singles[k - 2][rel]
            pltpu.make_async_copy(held.at[group], target, sem).start()

        if x_flip == 0:
            send(near_held, 0)
            side = far_held
        else:
            send(far_held, 3)
            side = near_held

        @pl.when(first == (x_flip == 1))
        def _():
            send(side, 1)

        @pl.when(first == (x_flip == 0))
        def _():
            send(side, 2)

    pltpu.make_async_copy(near_held, near_held, sem).wait()
    pltpu.make_async_copy(far_held, far_held, sem).wait()


def weight_grad_call(block_of, x_at, y_at, coord, picked, tokens, mine, theirs):
    return pl.pallas_call(
        weight_grad_kernel,
        out_shape=tuple(
            [jax.ShapeDtypeStruct((4, 2, 192, BC), jnp.bfloat16)] * 4
            + [jax.ShapeDtypeStruct((4, 192, BC), jnp.bfloat16)] * 8
        ),
        in_specs=smem(4) + vmem(4),
        out_specs=tuple(anywhere(12)),
        scratch_shapes=[
            pltpu.VMEM((8, 4, 192, BC), jnp.bfloat16),
            pltpu.VMEM((8, 4, 192, BC), jnp.bfloat16),
            pltpu.SemaphoreType.DMA,
        ],
        compiler_params=pltpu.CompilerParams(vmem_limit_bytes=VMEM_LIMIT),
        name="weight_grads",
    )(block_of, x_at, y_at, coord, picked, tokens, mine, theirs)


def shampoo_kernel(coord, *refs):
    own, by_y, by_core, by_both, lstat, rstat, lroot, rroot, blk = refs[:9]
    new_b, grad_out, new_l, new_r, whole = refs[-5:]
    y, core = coord[2], coord[3]
    for piece, y_at, core_at in (
        (own, y, core),
        (by_y, 1 - y, core),
        (by_core, y, 1 - core),
        (by_both, 1 - y, 1 - core),
    ):
        row = pl.multiple_of(192 * (2 * y_at + core_at), 64)
        whole[pl.ds(row, 192), :] = piece[0]
    grad_out[0] = high(own[0])
    grad = whole[...]
    new_l[0] = STAT_DECAY * lstat[0] + (1.0 - STAT_DECAY) * dot_nt(grad, grad)
    new_r[0] = STAT_DECAY * rstat[0] + (1.0 - STAT_DECAY) * dot_tn(grad, grad)
    turned = dot_nn(low(lroot[0]), grad)
    new_b[0] = blk[0] - SHAMPOO_RATE * dot_nn(low(turned), low(rroot[0]))


def shampoo_call(start, coord, pieces, lstat, rstat, lroot, rroot, blk, so_far):
    def one(rows, columns):
        return pl.BlockSpec((1, rows, columns), lambda i, coord: (start + i, 0, 0))

    slots = pieces[0].shape[0]
    in_specs = (
        [pl.BlockSpec((1, 192, BC), lambda i, coord: (i, 0, 0))] * 4
        + [
            one(D, D),
            one(BC, BC),
            pl.BlockSpec((1, 192, D), lambda i, coord: (start + i, 2 * coord[2] + coord[3], 0)),
            one(BC, BC),
            one(192, BC),
        ]
        + anywhere(len(so_far))
    )
    return pl.pallas_call(
        shampoo_kernel,
        grid_spec=pltpu.PrefetchScalarGridSpec(
            num_scalar_prefetch=1,
            grid=(slots,),
            in_specs=in_specs,
            out_specs=(one(192, BC), one(192, BC), one(D, D), one(BC, BC)),
            scratch_shapes=[pltpu.VMEM((D, BC), jnp.bfloat16)],
        ),
        out_shape=(
            jax.ShapeDtypeStruct(blk.shape, jnp.float32),
            jax.ShapeDtypeStruct(blk.shape, jnp.float32),
            jax.ShapeDtypeStruct(lstat.shape, jnp.float32),
            jax.ShapeDtypeStruct(rstat.shape, jnp.float32),
        ),
        input_output_aliases={10 + n: n for n in range(len(so_far))},
        compiler_params=pltpu.CompilerParams(vmem_limit_bytes=VMEM_LIMIT),
        cost_estimate=pl.CostEstimate(
            flops=4 * slots * D * D * BC,
            bytes_accessed=8 * slots * 1024 * 1024,
            transcendentals=0,
        ),
        name="shampoo",
    )(coord, *pieces, lstat, rstat, lroot, rroot, blk, *so_far)


def adam_kernel(embed, head, w, m, v, new_w, new_m, new_v):
    def step(grad, rate):
        new_w[0], new_m[0], new_v[0] = adam_step(w[0], grad, m[0], v[0], rate)

    @pl.when(pl.program_id(0) == 0)
    def _():
        step(embed[...], 0.3)

    @pl.when(pl.program_id(0) == 1)
    def _():
        step(head[...], 0.02)


def adam_call(embed, head, w, m, v):
    rows = w.shape[1]
    block = next(n for n in (200, 40, 8) if rows % n == 0)
    steps = rows // block
    spec = pl.BlockSpec((1, block, D), lambda i, j: (i, j, 0))
    return pl.pallas_call(
        adam_kernel,
        grid=(2, steps),
        out_shape=(jax.ShapeDtypeStruct(w.shape, jnp.float32),) * 3,
        in_specs=[
            pl.BlockSpec((block, D), lambda i, j: (j * (1 - i) + (steps - 1) * i, 0)),
            pl.BlockSpec((block, D), lambda i, j: (j * i, 0)),
            spec,
            spec,
            spec,
        ],
        out_specs=(spec,) * 3,
        compiler_params=pltpu.CompilerParams(vmem_limit_bytes=VMEM_LIMIT),
        cost_estimate=pl.CostEstimate(
            flops=20 * rows * D, bytes_accessed=64 * rows * D, transcendentals=2 * rows * D
        ),
        name="adam",
    )(embed, head, w, m, v)


def block_rows():
    x_at, y_at = [], []
    for b in range(NBLK):
        if b < 2:
            x_at.append(0), y_at.append(AT_DQ)
        elif b < 4:
            x_at.append(0), y_at.append(AT_DK)
        elif b < 6:
            x_at.append(0), y_at.append(AT_DV)
        elif b < 8:
            x_at.append(1), y_at.append(AT_DO)
        elif b < 16:
            x_at.append(2), y_at.append(AT_DGATE + (b - 8) // 2 * PAIR_ROWS)
        elif b < 24:
            x_at.append(2), y_at.append(AT_DUP + (b - 16) // 2 * PAIR_ROWS)
        else:
            x_at.append(3 + (b - 24) // 2), y_at.append(AT_DH)
    return jnp.array(x_at, jnp.int32), jnp.array(y_at, jnp.int32)


def per_core(
    token_ids,
    lengths,
    comp_mask,
    ref_logp,
    owner,
    blocks,
    left_stat,
    right_stat,
    left_root,
    right_root,
    tables,
    table_moment,
    table_second,
    gains,
    gain_moment,
    gain_second,
):
    zi, xi, yi, ci = (lax.axis_index(name) for name in AXES)
    coord = jnp.stack([zi, xi, yi, ci]).astype(jnp.int32)
    vocab_index = 2 * yi + ci
    shard = vocab_index * 8 + 2 * zi + xi
    table_rows = tables.shape[1]
    vocab = table_rows * 32
    seqs = 2 * MB
    shares = blocks.astype(jnp.bfloat16)
    with jax.named_scope("weights_fourth"):
        line4 = all_round(shares[3])
    first_pair = vocab_index * MB
    ids = lax.dynamic_slice_in_dim(token_ids, first_pair, MB, 0).reshape(seqs, SLOT)
    lens = lax.dynamic_slice_in_dim(lengths, first_pair, MB, 0).reshape(seqs)
    wanted = lax.dynamic_slice_in_dim(comp_mask, first_pair, MB, 0).reshape(PAIR_ROWS)
    refs = lax.dynamic_slice_in_dim(ref_logp, first_pair, MB, 0).reshape(seqs)
    places = jnp.arange(SLOT)
    pos = (lens[:, None] - 1 - CMP + jnp.arange(CMP)[None, :]).astype(jnp.int32)
    targets = jnp.sum(
        jnp.where(places[None, None, :] == (pos + 1)[:, :, None], ids[:, None, :], 0), axis=-1
    ).reshape(PAIR_ROWS)
    asked = jnp.concatenate([ids.reshape(TOKENS), targets + vocab])
    used = jnp.concatenate(
        [(places[None, :] < lens[:, None]).reshape(TOKENS), jnp.ones((PAIR_ROWS,), bool)]
    )
    number = jnp.where(asked >= vocab, asked - vocab, asked)
    holder = number // table_rows
    local_row = number - holder * table_rows + jnp.where(asked >= vocab, table_rows, 0)
    total = asked.shape[0]
    earlier = jnp.arange(total)[None, :] < jnp.arange(total)[:, None]
    same = (asked[:, None] == asked[None, :]) & used[:, None] & used[None, :]
    first = used & jnp.logical_not(jnp.any(same & earlier, axis=1))
    rank = jnp.sum(
        ((holder[:, None] == holder[None, :]) & earlier & first[None, :]).astype(jnp.int32), axis=1
    )
    spill = jnp.any(first & (rank >= CAP))
    seat_first = jnp.where(first & (rank < CAP), holder * CAP + rank, -1)
    seat = jnp.sum(jnp.where(same & first[None, :], seat_first[None, :] + 1, 0), axis=1) - 1
    seats = jnp.arange(32 * CAP)
    request = jnp.sum(
        jnp.where(seat_first[:, None] == seats[None, :], local_row[:, None], 0), axis=0
    )
    message = jnp.concatenate(
        [
            request.reshape(32, CAP),
            jnp.broadcast_to(spill.astype(jnp.int32), (32, MSG - CAP)),
        ],
        axis=1,
    )
    message = lax.all_to_all(message, SHARD_AXES, 0, 0, tiled=True)
    line4, shares, message = together(line4, shares, message)
    any_spill = jnp.max(message[:, MSG - 1]) > 0
    asked_rows = message[:, :CAP].reshape(32 * CAP)
    table_low = tables.astype(jnp.bfloat16).reshape(2 * table_rows, D)
    give = (asked_rows[:, None] == jnp.arange(2 * table_rows)[None, :]).astype(jnp.bfloat16)
    given = low(dot_nn(give, table_low))
    with jax.named_scope("weights_fourth"):
        one4, two4 = hop_one(line4), hop_two(line4)
    with jax.named_scope("weights_third"):
        line3 = all_round(shares[2])
    with jax.named_scope("weights_pair"):
        line = lax.all_gather(shares[:2], "z")
    line4, one4, two4, line3, given = together(line4, one4, two4, line3, given)
    got = lax.all_to_all(given, SHARD_AXES, 0, 0, tiled=True)
    with jax.named_scope("weights_third"):
        one3, two3 = hop_one(line3), hop_two(line3)
    with jax.named_scope("weights_fourth"):
        both4 = hop_two(one4)
    fourth = [line4, one4, two4, both4]
    line3, one3, two3, both4, line = together(line3, one3, two3, both4, line)
    with jax.named_scope("weights_pair"):
        one, two = hop_one(line), hop_two(line)
    with jax.named_scope("weights_third"):
        both3 = hop_two(one3)
    third = [line3, one3, two3, both3]
    line, one, two, both3, got = together(line, one, two, both3, got)
    with jax.named_scope("weights_pair"):
        pair = [line, one, two, hop_two(one)]
    place = (seat[:, None] == seats[None, :]).astype(jnp.bfloat16)
    rows = low(dot_nn(place, got))
    x, truth = rows[:TOKENS], rows[TOKENS:]
    inv_freq = ROPE_BASE ** (-jnp.arange(HDIM // 2).astype(jnp.float32) * 2.0 / HDIM)
    phase = places.astype(jnp.float32)[:, None] * inv_freq[None, :]
    phase_pick = pos.reshape(PAIR_ROWS).astype(jnp.float32)[:, None] * inv_freq[None, :]

    def turning(angle, repeat):
        cosine, sine = jnp.cos(angle), jnp.sin(angle)
        return (
            jnp.tile(jnp.concatenate([cosine] * 4, axis=1), (repeat, 1)),
            jnp.tile(jnp.concatenate([-sine, sine, -sine, sine], axis=1), (repeat, 1)),
        )

    turns = turning(phase_pick, 1) + turning(phase, seqs)
    pair[1] = after(pair[1], x, truth, *turns)
    parts = []
    for part in fourth + third + pair:
        parts.extend([part, hop_core(part)])
    parts = parts[16:] + parts[8:16] + parts[:8]
    left, *saved = forward_call(owner, coord, lens, x, gains, turns, parts)
    plane, _ = spread(saved[-1])
    plane = plane.reshape(-1, D)
    other = hop_core(plane)
    left_t = transpose_call(coord, left, hop_core(left))
    wide = -(-table_rows // 128) * 128
    head_low = jnp.pad(table_low[table_rows:], ((0, wide - table_rows), (0, 0)))
    ext_other, kept_other, stat_other = head_call(other, head_low, table_rows)
    ext_hop = hop_core(ext_other)
    ext_own, kept_own, stat_own = head_call(plane, head_low, table_rows)
    both = merge_call([(ext_own, 3), (ext_hop, 3)])[0]
    two = merge_call([(ext_own, 2), (ext_hop, 2)])[0]
    one = merge_call([(ext_own, 1), (ext_hop, 1), (hop_two(both), 0)])[0]
    pieces = merge_call([(ext_own, 0), (ext_hop, 0), (hop_one(one), 0), (hop_two(two), 0)], 4)
    pieces = lax.optimization_barrier(tuple(pieces) + tuple(left_t))[:4]
    parts_u = [pieces[0]] + [ring(pieces[step], -step) for step in range(1, 4)]
    marks = jnp.stack([wanted.astype(jnp.float32), targets.astype(jnp.float32)], axis=1)
    marks = jnp.pad(marks, ((0, 0), (0, 126)))
    act, dx, gain_part, info, loss_part = backward_call(
        owner, coord, lens, refs, x, gains, turns, saved, truth, marks, parts_u, parts
    )
    inverse = jnp.sum(
        jnp.where(
            owner[None, :] == jnp.arange(NBLK)[:, None], jnp.arange(NBLK, dtype=jnp.int32)[None, :], 0
        ),
        axis=1,
    )
    x_at, y_at = block_rows()
    chosen = (inverse[:, None] == jnp.arange(NBLK)[None, :]).astype(jnp.int32)
    grads = weight_grad_call(
        inverse,
        jnp.sum(chosen * x_at[None, :], axis=1),
        jnp.sum(chosen * y_at[None, :], axis=1),
        coord,
        *left_t,
        act,
        hop_core(act),
    )
    def plus(*values):
        return low(sum(high(value) for value in values))

    own, one, two, both = grads[:4]
    own3, one3, two3, both3 = grads[4:8]
    own4, one4, two4, both4 = grads[8:]
    info, gain_part, loss_part, dx, both, both3 = together(
        info, gain_part, loss_part, dx, both, both3
    )
    with jax.named_scope("grads_pair"):
        one = plus(one, hop_two(both))
    with jax.named_scope("grads_third"):
        one3 = plus(one3, hop_two(both3))
    sent = low(dot_tn(place[:TOKENS], dx))
    one, two, one3, two3, both4, sent = together(one, two, one3, two3, both4, sent)
    with jax.named_scope("grads_pair"):
        line = plus(own, hop_one(one), hop_two(two)).reshape(8, 192, BC)
    told = jnp.concatenate(
        [
            info[:, :3].reshape(-1),
            gain_part.reshape(-1),
            loss_part[0, :1],
            jnp.zeros((63,), jnp.float32),
        ]
    )
    heard = lax.all_to_all(
        jnp.broadcast_to(told[None], (32, told.shape[0])), AXES, 0, 0, tiled=True
    )
    summed = jnp.sum(heard[:, 3 * PAIR_ROWS :], axis=0)
    gain_grad = summed[: 3 * D].reshape(3, D)
    loss_sum = summed[3 * D]
    sources = []
    for other_core in range(2):
        for rel in range(4):
            for back in range(4):
                sources.append(
                    flat_of((zi + 4 - back) % 4, *place_of((zi, xi, yi, ci), other_core, rel))
                )
    sources = jnp.stack(sources)
    infos = jnp.sum(
        jnp.where(
            (sources[:, None] == jnp.arange(32)[None, :])[:, :, None],
            heard[None, :, : 3 * PAIR_ROWS],
            0.0,
        ),
        axis=1,
    ).reshape(-1, 3)
    infos = jnp.concatenate(
        [infos[:, :2], infos[:, 2:3] - (shard * table_rows).astype(jnp.float32)], axis=1
    )
    infos = jnp.pad(infos, ((0, 0), (0, 125)))
    line, one3, two3, both4, infos = together(line, one3, two3, both4, infos)
    grad_head = head_grad_call(
        (plane, other), (kept_own, kept_other), (stat_own, stat_other), infos
    )
    with jax.named_scope("grads_pair"):
        pair = lax.psum_scatter(line, "z", scatter_dimension=0, tiled=True)
    with jax.named_scope("grads_third"):
        one3, two3 = hop_one(one3), hop_two(two3)
        line3 = [plus(own3[n], one3[n], two3[n]) for n in range(4)]
    with jax.named_scope("grads_fourth"):
        one4 = plus(one4, hop_two(both4))
    *line3, one4, two4, grad_head = together(*line3, one4, two4, grad_head)
    with jax.named_scope("grads_third"):
        third = plus(line3[0], *[ring(line3[step], -step) for step in range(1, 4)])
    with jax.named_scope("grads_fourth"):
        one4, two4 = hop_one(one4), hop_two(two4)
        line4 = [plus(own4[n], one4[n], two4[n]) for n in range(4)]
    back_rows = lax.all_to_all(sent, SHARD_AXES, 0, 0, tiled=True)
    take_back = (asked_rows[None, :] == jnp.arange(table_rows)[:, None]).astype(jnp.bfloat16)

    grad_embed = dot_nn(take_back, back_rows)
    new_tables, new_table_moment, new_table_second = adam_call(
        grad_embed, grad_head, tables, table_moment, table_second
    )
    third, new_tables, *line4 = together(third, new_tables, *line4)
    with jax.named_scope("grads_fourth"):
        fourth = plus(line4[0], *[ring(line4[step], -step) for step in range(1, 4)])
    def finish(start, near, so_far):
        by_y = hop_y(near)
        return shampoo_call(
            start,
            coord,
            (near, by_y, hop_core(near), hop_core(by_y)),
            left_stat,
            right_stat,
            left_root,
            right_root,
            blocks,
            so_far,
        )

    results = finish(0, pair, ())
    new_blocks, block_grads, new_left, new_right = finish(
        2, after(jnp.stack([third, fourth]), results[0]), results
    )
    new_gains, new_gain_moment, new_gain_second = adam_step(
        gains, gain_grad, gain_moment, gain_second, GAIN_RATE
    )
    quick = (
        new_blocks,
        block_grads,
        new_left,
        new_right,
        new_tables,
        new_table_moment,
        new_table_second,
        new_gains,
        new_gain_moment,
        new_gain_second,
        loss_sum,
    )
    whole = (
        token_ids,
        lengths,
        comp_mask,
        ref_logp,
        owner,
        blocks,
        left_stat,
        right_stat,
        left_root,
        right_root,
        tables,
        table_moment,
        table_second,
        gains,
        gain_moment,
        gain_second,
    )
    def slow(state):
        outs = list(per_device(("z", "x"), ("y", "core"), *whole))
        outs[1] = with_layout_constraint(outs[1], Layout((0, 1, 2)))
        return jnp.zeros((), bool), tuple(outs)

    return lax.while_loop(lambda state: state[0], slow, (any_spill, quick))[1]


def solution(mesh):
    tuned = mesh.shape["dp"] == 8 and mesh.shape["vocab"] == 4
    if tuned:
        dp, vocab = ("z", "x"), ("y", "core")
        where = Mesh(mesh.devices.reshape(4, 2, 2, 2), AXES)
        body = per_core
    else:
        dp, vocab = ("dp",), ("vocab",)
        where = mesh
        body = functools.partial(per_device, ("dp",), ("vocab",))
    placed = (
        P(dp, None, None),
        P(dp, None),
        P(dp, None, None),
        P(dp, None),
        P(),
        P(dp, vocab, None),
        P(dp, None, None),
        P(dp, None, None),
        P(dp, None, None),
        P(dp, None, None),
        P(None, vocab + dp, None),
        P(None, vocab + dp, None),
        P(None, vocab + dp, None),
        P(),
        P(),
        P(),
    )
    return jax.shard_map(
        body,
        mesh=where,
        in_specs=placed,
        out_specs=(
            P(dp, vocab, None),
            P(dp, vocab, None),
            P(dp, None, None),
            P(dp, None, None),
            P(None, vocab + dp, None),
            P(None, vocab + dp, None),
            P(None, vocab + dp, None),
            P(),
            P(),
            P(),
            P(),
        ),
        check_vma=False,
    )
```

```python
import functools
import math

import jax
import jax.numpy as jnp
from jax import lax
from jax.experimental import pallas as pl
from jax.experimental.layout import Layout, with_layout_constraint
from jax.experimental.pallas import tpu as pltpu
from jax.sharding import Mesh
from jax.sharding import PartitionSpec as P

D = 768
HEADS = 12
HDIM = 64
FF = 3072
SLOT = 64
MB = 2
CMP = 16
STEP = 10
BC = 384
NBLK = 32


NORM_EPS = 1e-05
DPO_BETA = 0.02
ROPE_BASE = 10000.0
ADAM_ONE = 0.9
ADAM_TWO = 0.999
ADAM_EPS = 1e-08
WEIGHT_DECAY = 0.01
GAIN_RATE = 0.3
STAT_DECAY = 0.5
SHAMPOO_RATE = 0.5
MASKED = -1e30


def joined(value, axis, join):
    pieces = jax.tree.map(lambda part: lax.all_gather(part, axis), value)
    head = jax.tree.map(lambda part: part[0], pieces)
    tail = jax.tree.map(lambda part: part[1:], pieces)
    so_far, _ = lax.scan(lambda so_far, section: (join(so_far, section), None), head, tail)
    return so_far


def mult(left, right):
    return jnp.dot(left, right, preferred_element_type=jnp.float32)


def mult_t(left, right):
    return lax.dot_general(
        left, right, (((0,), (0,)), ((), ())), preferred_element_type=jnp.float32
    )


def mult_nt(left, right):
    return lax.dot_general(
        left, right, (((1,), (1,)), ((), ())), preferred_element_type=jnp.float32
    )


def project(rows, group):
    product = jnp.einsum("td,ndk->tnk", rows, group, preferred_element_type=jnp.float32)
    return product.reshape(rows.shape[0], group.shape[0] * BC)


def project_back(grad, group):
    return jnp.einsum(
        "tnk,ndk->td",
        grad.reshape(grad.shape[0], group.shape[0], BC),
        group,
        preferred_element_type=jnp.float32,
    )


def block_grad(rows, grad, number):
    return jnp.einsum(
        "td,tnk->ndk",
        rows,
        grad.reshape(grad.shape[0], number, BC),
        preferred_element_type=jnp.float32,
    )


def down_forward(mix, down):
    row_total = mix.shape[0]
    product = jnp.einsum(
        "trd,rjdk->tjk",
        mix.reshape(row_total, FF // D, D),
        down.reshape(FF // D, D // BC, D, BC),
        preferred_element_type=jnp.float32,
    )
    return product.reshape(row_total, D)


def down_back(grad, down):
    row_total = grad.shape[0]
    product = jnp.einsum(
        "tjk,rjdk->trd",
        grad.reshape(row_total, D // BC, BC),
        down.reshape(FF // D, D // BC, D, BC),
        preferred_element_type=jnp.float32,
    )
    return product.reshape(row_total, FF)


def down_grad(mix, grad):
    row_total = mix.shape[0]
    product = jnp.einsum(
        "trd,tjk->rjdk",
        mix.reshape(row_total, FF // D, D),
        grad.reshape(row_total, D // BC, BC),
        preferred_element_type=jnp.float32,
    )
    return product.reshape(-1, D, BC)


def groups(weights):
    col_blocks = D // BC
    ff_blocks = FF // BC
    base_gate = 4 * col_blocks
    return (
        weights[0:col_blocks],
        weights[col_blocks : 2 * col_blocks],
        weights[2 * col_blocks : 3 * col_blocks],
        weights[3 * col_blocks : base_gate],
        weights[base_gate : base_gate + ff_blocks],
        weights[base_gate + ff_blocks : base_gate + 2 * ff_blocks],
        weights[base_gate + 2 * ff_blocks :],
    )


def rms_forward(values, gain):
    return values * lax.rsqrt(jnp.mean(values * values, axis=-1, keepdims=True) + NORM_EPS) * gain


def rms_backward(values, gain, grad):
    scale = lax.rsqrt(jnp.mean(values * values, axis=-1, keepdims=True) + NORM_EPS)
    inner = jnp.mean(values * gain * grad, axis=-1, keepdims=True)
    back = scale * gain * grad - values * scale**3 * inner
    return (back, jnp.sum(grad * values * scale, axis=0))


def angles():
    inv_freq = ROPE_BASE ** (-jnp.arange(HDIM // 2).astype(jnp.float32) * 2.0 / HDIM)
    phase_grid = jnp.arange(SLOT).astype(jnp.float32)[:, None] * inv_freq[None, :]
    return (jnp.cos(phase_grid), jnp.sin(phase_grid))


def rotate(values, cosine, sine, direction):
    half_dim = HDIM // 2
    lead_half = values[..., :half_dim]
    tail_half = values[..., half_dim:]
    cos_grid = cosine[None, :, None, :]
    sin_grid = direction * sine[None, :, None, :]
    return jnp.concatenate(
        [lead_half * cos_grid - tail_half * sin_grid, tail_half * cos_grid + lead_half * sin_grid],
        axis=-1,
    )


def attend_scores(q_rot, k_rot, len_vec):
    raw = jnp.einsum(
        "nqhd,nkhd->nhqk", q_rot, k_rot, preferred_element_type=jnp.float32
    ) / math.sqrt(HDIM)
    places = jnp.arange(SLOT)
    valid = (places[None, :] <= places[:, None])[None, None] & (
        places[None, None, None, :] < len_vec[:, None, None, None]
    )
    return jnp.where(valid, raw, MASKED)


def layer_forward(inputs, len_vec, gains, mats, cosine, sine):
    w_query, w_key, w_value, w_out, w_gate, w_up, w_down = mats
    seq_count = inputs.shape[0] // SLOT

    def to_heads(values):
        return values.reshape(seq_count, SLOT, HEADS, HDIM)

    a_low = rms_forward(inputs, gains[0]).astype(jnp.bfloat16)
    q_rot = rotate(to_heads(project(a_low, w_query)), cosine, sine, 1.0).astype(jnp.bfloat16)
    k_rot = rotate(to_heads(project(a_low, w_key)), cosine, sine, 1.0).astype(jnp.bfloat16)
    v_heads = to_heads(project(a_low, w_value)).astype(jnp.bfloat16)
    scores = attend_scores(q_rot, k_rot, len_vec)
    row_max = jnp.max(scores, axis=-1, keepdims=True)
    log_total = jnp.log(jnp.sum(jnp.exp(scores - row_max), axis=-1, keepdims=True)) + row_max
    p_low = jnp.exp(scores - log_total).astype(jnp.bfloat16)
    att_out = jnp.einsum("nhqk,nkhd->nqhd", p_low, v_heads, preferred_element_type=jnp.float32)
    att_out = att_out.reshape(seq_count * SLOT, D).astype(jnp.bfloat16)
    h_mid = inputs + project(att_out, w_out)
    b_low = rms_forward(h_mid, gains[1]).astype(jnp.bfloat16)
    gate_pre = project(b_low, w_gate)
    up_pre = project(b_low, w_up)
    mix_low = (jax.nn.silu(gate_pre) * up_pre).astype(jnp.bfloat16)
    h_out = h_mid + down_forward(mix_low, w_down)
    return (
        h_out,
        (a_low, q_rot, k_rot, v_heads, log_total, att_out, h_mid, b_low, gate_pre, up_pre, mix_low),
    )


def layer_backward(inputs, len_vec, gains, mats, cosine, sine, saved, grad_out):
    w_query, w_key, w_value, w_out, w_gate, w_up, w_down = mats
    a_low, q_rot, k_rot, v_heads, log_total, att_out, h_mid, b_low, gate_pre, up_pre, mix_low = (
        saved
    )
    seq_count = inputs.shape[0] // SLOT
    grad_branch = grad_out.astype(jnp.bfloat16)
    grad_mix = down_back(grad_branch, w_down)
    sigmoid_gate = jax.nn.sigmoid(gate_pre)
    grad_gate = (grad_mix * up_pre * sigmoid_gate * (1.0 + gate_pre * (1.0 - sigmoid_gate))).astype(
        jnp.bfloat16
    )
    grad_up = (grad_mix * gate_pre * sigmoid_gate).astype(jnp.bfloat16)
    grad_b = project_back(grad_gate, w_gate) + project_back(grad_up, w_up)
    back_mid, gain_mid = rms_backward(h_mid, gains[1], grad_b)
    grad_mid = grad_out + back_mid
    grad_attn = grad_mid.astype(jnp.bfloat16)
    grad_att = (
        project_back(grad_attn, w_out).astype(jnp.bfloat16).reshape(seq_count, SLOT, HEADS, HDIM)
    )
    p_full = jnp.exp(attend_scores(q_rot, k_rot, len_vec) - log_total)
    grad_p = jnp.einsum("nqhd,nkhd->nhqk", grad_att, v_heads, preferred_element_type=jnp.float32)
    grad_s = (p_full * (grad_p - jnp.sum(p_full * grad_p, axis=-1, keepdims=True))).astype(
        jnp.bfloat16
    )
    grad_q = jnp.einsum(
        "nhqk,nkhd->nqhd", grad_s, k_rot, preferred_element_type=jnp.float32
    ) / math.sqrt(HDIM)
    grad_k = jnp.einsum(
        "nhqk,nqhd->nkhd", grad_s, q_rot, preferred_element_type=jnp.float32
    ) / math.sqrt(HDIM)
    grad_v = jnp.einsum(
        "nhqk,nqhd->nkhd", p_full.astype(jnp.bfloat16), grad_att, preferred_element_type=jnp.float32
    )
    row_total = seq_count * SLOT
    grad_q = rotate(grad_q, cosine, sine, -1.0).reshape(row_total, D).astype(jnp.bfloat16)
    grad_k = rotate(grad_k, cosine, sine, -1.0).reshape(row_total, D).astype(jnp.bfloat16)
    grad_v = grad_v.reshape(row_total, D).astype(jnp.bfloat16)
    grad_a = (
        project_back(grad_q, w_query) + project_back(grad_k, w_key) + project_back(grad_v, w_value)
    )
    back_in, gain_in = rms_backward(inputs, gains[0], grad_a)
    operands = (
        a_low,
        grad_q,
        grad_k,
        grad_v,
        att_out,
        grad_attn,
        b_low,
        grad_gate,
        grad_up,
        mix_low,
        grad_branch,
    )
    return (grad_mid + back_in, operands, jnp.stack([gain_in, gain_mid]))


def weight_grads(operands):
    (
        a_low,
        grad_q,
        grad_k,
        grad_v,
        att_out,
        grad_attn,
        b_low,
        grad_gate,
        grad_up,
        mix_low,
        grad_branch,
    ) = operands
    col_blocks = D // BC
    ff_blocks = FF // BC
    return jnp.concatenate(
        [
            block_grad(a_low, grad_q, col_blocks),
            block_grad(a_low, grad_k, col_blocks),
            block_grad(a_low, grad_v, col_blocks),
            block_grad(att_out, grad_attn, col_blocks),
            block_grad(b_low, grad_gate, ff_blocks),
            block_grad(b_low, grad_up, ff_blocks),
            down_grad(mix_low, grad_branch),
        ],
        axis=0,
    )


def combine_parts(earlier, later):
    max_one, sum_one, pick_one = earlier
    max_two, sum_two, pick_two = later
    joint_max = jnp.maximum(max_one, max_two)
    joint_sum = sum_one * jnp.exp(max_one - joint_max) + sum_two * jnp.exp(max_two - joint_max)
    return (joint_max, joint_sum, pick_one + pick_two)


def adam_step(weight, grad, moment, second, rate):
    moment = ADAM_ONE * moment + (1.0 - ADAM_ONE) * grad
    second = ADAM_TWO * second + (1.0 - ADAM_TWO) * grad * grad
    ratio = moment / (1.0 - ADAM_ONE**STEP) / (jnp.sqrt(second / (1.0 - ADAM_TWO**STEP)) + ADAM_EPS)
    return (weight - rate * (ratio + WEIGHT_DECAY * weight), moment, second)


def per_device(
    dp,
    vocab,
    token_ids,
    lengths,
    comp_mask,
    ref_logp,
    owner,
    blocks,
    left_stat,
    right_stat,
    left_root,
    right_root,
    tables,
    table_moment,
    table_second,
    gains,
    gain_moment,
    gain_second,
):
    vocab_count = lax.axis_size(vocab)
    vocab_index = lax.axis_index(vocab)
    row_share = blocks.shape[1]
    cosine, sine = angles()
    tables_low = lax.all_gather(tables.astype(jnp.bfloat16), dp, axis=1, tiled=True)
    vocab_rows = tables_low.shape[1]
    local_ids = token_ids.reshape(-1) - vocab_index * vocab_rows
    inside = (local_ids >= 0) & (local_ids < vocab_rows)
    safe_ids = jnp.clip(local_ids, 0, vocab_rows - 1)
    looked = jnp.where(inside[:, None], jnp.take(tables_low[0], safe_ids, axis=0), 0).astype(
        jnp.float32
    )
    embedded = lax.psum_scatter(
        looked.astype(jnp.bfloat16), vocab, scatter_dimension=0, tiled=True
    ).astype(jnp.float32)
    rows_all = lax.all_gather(blocks.astype(jnp.bfloat16), vocab, axis=1, tiled=True)
    slots_all = lax.all_gather(rows_all, dp, axis=0, tiled=True)
    kept_mats = groups(jnp.take(slots_all, owner, axis=0))
    gain_total = jnp.zeros((3, D), jnp.float32)
    loss_own = jnp.zeros((), jnp.float32)
    grad_inputs = []
    operand_list = []
    logit_grads = []
    head_inputs = []
    for micro in range(MB):
        own_pair = vocab_index * MB + micro
        rows_in = embedded[micro * 2 * SLOT : (micro + 1) * 2 * SLOT]
        len_own = lax.dynamic_index_in_dim(lengths, own_pair, 0, keepdims=False)
        h_out, saved = layer_forward(rows_in, len_own, gains, kept_mats, cosine, sine)
        pos_own = len_own[:, None] - 1 - CMP + jnp.arange(CMP)[None, :]
        picked_rows = jnp.take_along_axis(
            h_out.reshape(2, SLOT, D), pos_own[:, :, None], axis=1
        ).reshape(2 * CMP, D)
        c_low = rms_forward(picked_rows, gains[2]).astype(jnp.bfloat16)
        all_rows = lax.all_gather(c_low, vocab, axis=0, tiled=True)
        ids_sel = token_ids[micro::MB]
        lens_sel = lengths[micro::MB]
        mask_sel = comp_mask[micro::MB].astype(jnp.float32)
        ref_sel = ref_logp[micro::MB]
        pos_sel = lens_sel[:, :, None] - 1 - CMP + jnp.arange(CMP)[None, None, :]
        target = (
            jnp.take_along_axis(ids_sel, pos_sel + 1, axis=2).reshape(-1) - vocab_index * vocab_rows
        )
        logits = mult_nt(all_rows, tables_low[1])
        one_hot = jnp.arange(vocab_rows)[None, :] == target[:, None]
        row_max = jnp.max(logits, axis=1)
        row_sum = jnp.sum(jnp.exp(logits - row_max[:, None]), axis=1)
        row_pick = jnp.sum(jnp.where(one_hot, logits, 0.0), axis=1)
        full_max, full_sum, full_pick = joined((row_max, row_sum, row_pick), vocab, combine_parts)
        log_norm = full_max + jnp.log(full_sum)
        seq_logp = jnp.sum((full_pick - log_norm).reshape(vocab_count, 2, CMP) * mask_sel, axis=2)
        margin = DPO_BETA * (seq_logp[:, 0] - ref_sel[:, 0] - (seq_logp[:, 1] - ref_sel[:, 1]))
        loss_own = loss_own + jnp.take(jax.nn.softplus(-margin), vocab_index)
        pair_weight = -DPO_BETA * jax.nn.sigmoid(-margin)
        grad_tok = (jnp.stack([pair_weight, -pair_weight], axis=1)[:, :, None] * mask_sel).reshape(
            -1
        )
        grad_logits = (
            grad_tok[:, None] * (one_hot.astype(jnp.float32) - jnp.exp(logits - log_norm[:, None]))
        ).astype(jnp.bfloat16)
        logit_grads.append(grad_logits)
        head_inputs.append(all_rows)
        grad_c = lax.psum_scatter(
            mult(grad_logits, tables_low[1]), vocab, scatter_dimension=0, tiled=True
        )
        back_rows, gain_head = rms_backward(picked_rows, gains[2], grad_c)
        seq_index = jnp.arange(2)[:, None]
        grad_top = (
            jnp.zeros((2, SLOT, D), jnp.float32)
            .at[seq_index, pos_own]
            .add(back_rows.reshape(2, CMP, D))
        )
        grad_in, operands, gains_now = layer_backward(
            rows_in, len_own, gains, kept_mats, cosine, sine, saved, grad_top.reshape(2 * SLOT, D)
        )
        operand_list.append(operands)
        gain_total = gain_total + jnp.concatenate([gains_now, gain_head[None]], axis=0)
        grad_inputs.append(grad_in)
    joined_ops = tuple(
        (
            jnp.concatenate([ops[i] for ops in operand_list], axis=0)
            for i in range(len(operand_list[0]))
        )
    )
    block_order = weight_grads(joined_ops)
    grad_head = mult_t(jnp.concatenate(logit_grads, axis=0), jnp.concatenate(head_inputs, axis=0))
    grad_rows = lax.all_gather(
        jnp.concatenate(grad_inputs, axis=0).astype(jnp.bfloat16), vocab, axis=0, tiled=True
    ).astype(jnp.float32)
    grad_embed = (
        jnp.zeros((vocab_rows, D), jnp.float32)
        .at[safe_ids]
        .add(jnp.where(inside[:, None], grad_rows, 0.0))
    )
    table_grad = lax.psum_scatter(
        jnp.stack([grad_embed, grad_head]).astype(jnp.bfloat16),
        dp,
        scatter_dimension=1,
        tiled=True,
    ).astype(jnp.float32)
    inverse = jnp.zeros((NBLK,), jnp.int32).at[owner].set(jnp.arange(NBLK, dtype=jnp.int32))
    slotted = jnp.take(block_order, inverse, axis=0)
    summed = lax.psum_scatter(slotted.astype(jnp.bfloat16), dp, scatter_dimension=0, tiled=True)
    share_part = lax.psum_scatter(summed, vocab, scatter_dimension=1, tiled=True).astype(
        jnp.float32
    )
    whole = lax.all_gather(share_part.astype(jnp.bfloat16), vocab, axis=1, tiled=True).astype(
        share_part.dtype
    )
    highest = lax.Precision.HIGHEST
    new_left = STAT_DECAY * left_stat + (1.0 - STAT_DECAY) * jnp.einsum(
        "bij,bkj->bik", whole, whole, precision=highest
    )
    new_right = STAT_DECAY * right_stat + (1.0 - STAT_DECAY) * jnp.einsum(
        "bji,bjk->bik", whole, whole, precision=highest
    )
    direction = jnp.einsum("bij,bjk->bik", left_root, whole, precision=highest)
    direction = jnp.einsum("bij,bjk->bik", direction, right_root, precision=highest)
    new_blocks = blocks - SHAMPOO_RATE * lax.dynamic_slice_in_dim(
        direction, vocab_index * row_share, row_share, 1
    )
    loss_sum, gain_grad = lax.psum((loss_own, gain_total), dp + vocab)
    rates = jnp.array([0.3, 0.02], jnp.float32)[:, None, None]
    new_tables, new_table_moment, new_table_second = adam_step(
        tables, table_grad, table_moment, table_second, rates
    )
    new_gains, new_gain_moment, new_gain_second = adam_step(
        gains, gain_grad, gain_moment, gain_second, GAIN_RATE
    )
    return (
        new_blocks,
        share_part,
        new_left,
        new_right,
        new_tables,
        new_table_moment,
        new_table_second,
        new_gains,
        new_gain_moment,
        new_gain_second,
        loss_sum,
    )


PAIR_ROWS = MB * 2 * CMP
TOKENS = MB * 2 * SLOT
CAP = 24
CAP_BACK = 18
MSG = 32
EXT = D + 128
AXES = ("z", "x", "y", "core")
SHARD_AXES = ("y", "core", "z", "x")
VMEM_LIMIT = 60 * 1024 * 1024

AT_A = 0
AT_AP = AT_A + TOKENS
AT_O = AT_AP + PAIR_ROWS
AT_B = AT_O + PAIR_ROWS
AT_Z = AT_B + PAIR_ROWS
LEFT_ROWS = AT_Z + (FF // D) * PAIR_ROWS
LEFT_KINDS = (LEFT_ROWS - AT_AP) // PAIR_ROWS
AT_DK = 0
AT_DV = AT_DK + TOKENS
AT_DQ = AT_DV + TOKENS
AT_DO = AT_DQ + PAIR_ROWS
AT_DGATE = AT_DO + PAIR_ROWS
AT_DUP = AT_DGATE + (FF // D) * PAIR_ROWS
AT_DH = AT_DUP + (FF // D) * PAIR_ROWS
RIGHT_ROWS = AT_DH + PAIR_ROWS


def flat_of(z, x, y, c):
    return ((z * 2 + x) * 2 + y) * 2 + c


def moves(target):
    pairs = []
    for z in range(4):
        for x in range(2):
            for y in range(2):
                for c in range(2):
                    pairs.append((flat_of(z, x, y, c), flat_of(*target(z, x, y, c))))
    return pairs


def hop_one(value):
    return lax.ppermute(
        value,
        AXES,
        moves(lambda z, x, y, c: (z, 1 - x, y, c) if c == 0 else (z, x, 1 - y, c)),
    )


def hop_two(value):
    return lax.ppermute(
        value,
        AXES,
        moves(lambda z, x, y, c: (z, x, 1 - y, c) if c == 0 else (z, 1 - x, y, c)),
    )


def hop_core(value):
    return lax.ppermute(value, AXES, moves(lambda z, x, y, c: (z, x, y, 1 - c)))


def hop_y(value):
    return lax.ppermute(value, AXES, moves(lambda z, x, y, c: (z, x, 1 - y, c)))


def ring(value, step):
    return lax.ppermute(value, AXES, moves(lambda z, x, y, c: ((z + step) % 4, x, y, c)))


def after(value, *others):
    return lax.optimization_barrier((value,) + others)[0]


def together(*values):
    return lax.optimization_barrier(values)


def all_round(chunk):
    return jnp.stack([chunk] + [ring(chunk, step) for step in range(1, 4)])


def spread(chunk, wait=()):
    if wait:
        chunk = after(chunk, *wait)
    around = [ring(chunk, step) for step in range(1, 4)]
    line = jnp.stack([chunk] + around)
    one = hop_one(line)
    two = hop_two(line)
    both = hop_two(one)
    return jnp.stack([line, one, two, both]), around


def dot_nn(left, right):
    return lax.dot_general(left, right, (((1,), (0,)), ((), ())), preferred_element_type=jnp.float32)


def dot_nt(left, right):
    return lax.dot_general(left, right, (((1,), (1,)), ((), ())), preferred_element_type=jnp.float32)


def dot_tn(left, right):
    return lax.dot_general(left, right, (((0,), (0,)), ((), ())), preferred_element_type=jnp.float32)


def low(value):
    return value.astype(jnp.bfloat16)


def high(value):
    return value.astype(jnp.float32)


def place_of(coord, other_core, rel):
    core = coord[3] + other_core * (1 - 2 * coord[3])
    first = rel & 1
    second = rel >> 1
    x_flip = first + core * (second - first)
    y_flip = second + core * (first - second)
    x = coord[1] + x_flip * (1 - 2 * coord[1])
    y = coord[2] + y_flip * (1 - 2 * coord[2])
    return x, y, core


def start_weights(coord, parts, held, sem):
    def start(source, slots, y, core):
        row = pl.multiple_of(192 * (2 * y + core), 64)
        pltpu.make_async_copy(source, held.at[slots, pl.ds(row, 192)], sem).start()

    for other_core in range(2):
        for rel in range(4):
            x, y, core = place_of(coord, other_core, rel)
            pair, third, last = (
                parts[2 * rel + other_core],
                parts[8 + 2 * rel + other_core],
                parts[16 + other_core],
            )

            def one(n, carry):
                back = (coord[0] + 4 - n) & 3
                start(pair.at[n], pl.ds(8 * n + 4 * x, 2), y, core)
                start(third.at[n], 8 * back + 4 * x + 2, y, core)
                start(last.at[n, rel], 8 * n + 4 * x + 3, y, core)
                return carry

            lax.fori_loop(0, 4, one, 0)


def wait_weights(held, sem):
    pltpu.make_async_copy(held, held, sem).wait()


def iota(shape, axis):
    return lax.broadcasted_iota(jnp.int32, shape, axis)


def pick_rows(lens):
    row = iota((PAIR_ROWS, 1), 0)
    seq = row >> 4
    length = jnp.where(
        seq == 0, lens[0], jnp.where(seq == 1, lens[1], jnp.where(seq == 2, lens[2], lens[3]))
    )
    return seq, length - 1 - CMP + (row & 15)


def masks(lens):
    seq, pos = pick_rows(lens)
    col = iota((PAIR_ROWS, TOKENS), 1)
    same = (col >> 6) == seq
    key = col & 63
    return same & (key <= pos), same & (key == pos)


def turn(chunk, cosine, sine, sign):
    lane = iota(chunk.shape, 1)
    swapped = jnp.where((lane & 63) < 32, pltpu.roll(chunk, 96, 1), pltpu.roll(chunk, 32, 1))
    return chunk * cosine + swapped * (sine * sign)


def scale_of(values):
    return lax.rsqrt(jnp.mean(values * values, axis=-1, keepdims=True) + NORM_EPS)


def rms_back(values, gain, grad):
    scale = scale_of(values)
    inner = jnp.mean(values * gain * grad, axis=-1, keepdims=True)
    back = scale * gain * grad - values * (scale * scale * scale) * inner
    return back, jnp.sum(grad * values * scale, axis=0, keepdims=True)


def forward_kernel(owner, coord, lens, x, gains, cos_q, sin_q, cos_k, sin_k, *rest):
    parts, rest = rest[:18], rest[18:]
    left, q_out, k_out, v_out, h1_out, gate_out, up_out, h2_out, c_out = rest[:9]
    held, sem = rest[9:]
    start_weights(coord, parts, held, sem)
    values = high(x[...])
    a_low = low(values * scale_of(values) * gains[0:1, :])
    left[AT_A:AT_AP] = a_low
    valid, chosen = masks(lens)
    select = jnp.where(chosen, 1.0, 0.0).astype(jnp.bfloat16)
    a_pick = low(dot_nn(select, a_low))
    left[AT_AP:AT_O] = a_pick
    x_pick = dot_nn(select, x[...])
    wait_weights(held, sem)
    for j in range(2):
        q = dot_nn(a_pick, held[owner[j]])
        k = dot_nn(a_low, held[owner[2 + j]])
        v_out[:, j * BC : (j + 1) * BC] = low(dot_nn(a_low, held[owner[4 + j]]))
        for i in range(3):
            at = slice(j * BC + i * 128, j * BC + (i + 1) * 128)
            q_out[:, at] = low(turn(q[:, i * 128 : (i + 1) * 128], cos_q[...], sin_q[...], 1.0))
            k_out[:, at] = low(turn(k[:, i * 128 : (i + 1) * 128], cos_k[...], sin_k[...], 1.0))
    lane = iota((TOKENS, 128), 1)
    zero = jnp.zeros((TOKENS, 128), jnp.bfloat16)
    for p in range(HEADS // 2):
        at = slice(p * 128, (p + 1) * 128)
        total = jnp.zeros((PAIR_ROWS, 128), jnp.float32)
        for h in range(2):
            mine = (lane >> 6) == h
            s = dot_nt(q_out[:, at], jnp.where(mine, k_out[:, at], zero)) * (1.0 / math.sqrt(HDIM))
            s = jnp.where(valid, s, MASKED)
            e = jnp.exp(s - jnp.max(s, axis=-1, keepdims=True))
            prob = low(e / jnp.sum(e, axis=-1, keepdims=True))
            total = total + dot_nn(prob, jnp.where(mine, v_out[:, at], zero))
        left[AT_O:AT_B, at] = low(total)
    for j in range(2):
        at = slice(j * BC, (j + 1) * BC)
        h1_out[:, at] = x_pick[:, at] + dot_nn(left[AT_O:AT_B], held[owner[6 + j]])
    h1 = h1_out[...]
    b_low = low(h1 * scale_of(h1) * gains[1:2, :])
    left[AT_B:AT_Z] = b_low
    for j in range(FF // BC):
        at = slice(j * BC, (j + 1) * BC)
        gate = dot_nn(b_low, held[owner[8 + j]])
        up = dot_nn(b_low, held[owner[16 + j]])
        gate_out[:, at] = gate
        up_out[:, at] = up
        row = AT_Z + j // 2 * PAIR_ROWS
        left[row : row + PAIR_ROWS, j % 2 * BC : (j % 2 + 1) * BC] = low(
            gate * jax.nn.sigmoid(gate) * up
        )
    for j in range(2):
        total = h1[:, j * BC : (j + 1) * BC]
        for r in range(FF // D):
            row = AT_Z + r * PAIR_ROWS
            total = total + dot_nn(left[row : row + PAIR_ROWS], held[owner[24 + 2 * r + j]])
        h2_out[:, j * BC : (j + 1) * BC] = total
    h2 = h2_out[...]
    c_out[...] = low(h2 * scale_of(h2) * gains[2:3, :])


def vmem(number):
    return [pl.BlockSpec(memory_space=pltpu.VMEM)] * number


def smem(number):
    return [pl.BlockSpec(memory_space=pltpu.SMEM)] * number


def anywhere(number):
    return [pl.BlockSpec(memory_space=pl.ANY)] * number


def forward_call(owner, coord, lens, x, gains, turns, parts):
    def made(rows, columns, kind):
        return jax.ShapeDtypeStruct((rows, columns), kind)

    return pl.pallas_call(
        forward_kernel,
        out_shape=(
            made(LEFT_ROWS, D, jnp.bfloat16),
            made(PAIR_ROWS, D, jnp.bfloat16),
            made(TOKENS, D, jnp.bfloat16),
            made(TOKENS, D, jnp.bfloat16),
            made(PAIR_ROWS, D, jnp.float32),
            made(PAIR_ROWS, FF, jnp.float32),
            made(PAIR_ROWS, FF, jnp.float32),
            made(PAIR_ROWS, D, jnp.float32),
            made(PAIR_ROWS, D, jnp.bfloat16),
        ),
        in_specs=smem(3) + vmem(6) + anywhere(18),
        out_specs=tuple(vmem(9)),
        scratch_shapes=[
            pltpu.VMEM((NBLK, D, BC), jnp.bfloat16),
            pltpu.SemaphoreType.DMA,
        ],
        compiler_params=pltpu.CompilerParams(vmem_limit_bytes=VMEM_LIMIT),
        name="layer_forward",
    )(owner, coord, lens, x, gains, *turns, *parts)


def unpack(ext):
    stat = high(ext[:, D:EXT])
    top = (stat[:, 0:1] + stat[:, 1:2]) + stat[:, 2:3]
    total = (stat[:, 3:4] + stat[:, 4:5]) + stat[:, 5:6]
    return top, total, high(ext[:, :D])


def pack_stat(top, total):
    lane = iota((top.shape[0], 128), 1)
    out = jnp.zeros((top.shape[0], 128), jnp.float32)
    for first, value in ((0, top), (3, total)):
        for i in range(3):
            piece = high(low(value))
            out = jnp.where(lane == first + i, piece, out)
            value = value - piece
    return low(out)


def merge(items):
    top = items[0][0]
    for item in items[1:]:
        top = jnp.maximum(top, item[0])
    total = 0.0
    mixed = 0.0
    for item_top, item_total, item_mixed in items:
        factor = jnp.exp(item_top - top)
        total = total + item_total * factor
        mixed = mixed + item_mixed * factor
    return top, total, mixed


def merge_kernel(number, *refs):
    top, total, mixed = merge([unpack(ref[...]) for ref in refs[:number]])
    mixed = low(mixed)
    stat = pack_stat(top, total)
    outs = refs[number:]
    rows = outs[0].shape[0]
    for n, out in enumerate(outs):
        out[:, :D] = mixed[n * rows : (n + 1) * rows]
        out[:, D:EXT] = stat[n * rows : (n + 1) * rows]


def merge_call(parts, pieces=1):
    rows = 4 * PAIR_ROWS
    made = jax.ShapeDtypeStruct((rows // pieces, EXT), jnp.bfloat16)
    return pl.pallas_call(
        functools.partial(merge_kernel, len(parts)),
        grid=(1,),
        out_shape=(made,) * pieces,
        in_specs=[pl.BlockSpec((rows, EXT), lambda i, at=at: (at, 0)) for _, at in parts],
        out_specs=(pl.BlockSpec(made.shape, lambda i: (0, 0)),) * pieces,
        compiler_params=pltpu.CompilerParams(vmem_limit_bytes=VMEM_LIMIT),
        cost_estimate=pl.CostEstimate(
            flops=8 * rows * D, bytes_accessed=4 * rows * EXT, transcendentals=rows
        ),
        name="merge_parts",
    )(*[array for array, _ in parts])


def head_kernel(real, rows, head, ext, kept, stat):
    logits = dot_nt(rows[...], head[...])
    col = iota(logits.shape, 1)
    logits = jnp.where(col < real, logits, MASKED)
    top = jnp.max(logits, axis=-1, keepdims=True)
    e = jnp.exp(logits - top)
    total = jnp.sum(e, axis=-1, keepdims=True)
    e_low = low(e)
    kept[...] = e_low
    ext[:, :D] = low(dot_nn(e_low, head[...]))
    ext[:, D:EXT] = pack_stat(top, total)
    stat[...] = jnp.broadcast_to(top, stat.shape)


def head_call(rows, head, real):
    number, wide = rows.shape[0], head.shape[0]
    return pl.pallas_call(
        functools.partial(head_kernel, real),
        grid=(number // 256,),
        out_shape=(
            jax.ShapeDtypeStruct((number, EXT), jnp.bfloat16),
            jax.ShapeDtypeStruct((number, wide), jnp.bfloat16),
            jax.ShapeDtypeStruct((number, 128), jnp.float32),
        ),
        in_specs=[
            pl.BlockSpec((256, D), lambda i: (i, 0)),
            pl.BlockSpec((wide, D), lambda i: (0, 0)),
        ],
        out_specs=(
            pl.BlockSpec((256, EXT), lambda i: (i, 0)),
            pl.BlockSpec((256, wide), lambda i: (i, 0)),
            pl.BlockSpec((256, 128), lambda i: (i, 0)),
        ),
        compiler_params=pltpu.CompilerParams(vmem_limit_bytes=VMEM_LIMIT),
        cost_estimate=pl.CostEstimate(
            flops=4 * number * wide * D, bytes_accessed=2 * number * wide, transcendentals=number * wide
        ),
        name="head_forward",
    )(rows, head)


def head_grad_kernel(steps, rows_a, rows_b, kept_a, kept_b, stat_a, stat_b, info, out):
    def add(rows, kept, stat):
        weight = info[:, 0:1]
        factor = weight * jnp.exp(stat[:, 0:1] - info[:, 1:2])
        col = iota(kept.shape, 1)
        hit = col == info[:, 2:3].astype(jnp.int32)
        grad = low(jnp.where(hit, weight, 0.0) - high(kept[...]) * factor)
        return dot_tn(grad, rows[...])

    i = pl.program_id(0)

    @pl.when(i == 0)
    def _():
        out[...] = add(rows_a, kept_a, stat_a)

    @pl.when((i > 0) & (i < steps))
    def _():
        out[...] += add(rows_a, kept_a, stat_a)

    @pl.when(i >= steps)
    def _():
        out[...] += add(rows_b, kept_b, stat_b)


def head_grad_call(rows, kept, stat, info):
    number, wide = kept[0].shape
    steps = number // 256

    def pair(columns):
        return [
            pl.BlockSpec((256, columns), lambda i: (jnp.minimum(i, steps - 1), 0)),
            pl.BlockSpec((256, columns), lambda i: (jnp.maximum(i - steps, 0), 0)),
        ]

    return pl.pallas_call(
        functools.partial(head_grad_kernel, steps),
        grid=(2 * steps,),
        out_shape=jax.ShapeDtypeStruct((wide, D), jnp.float32),
        in_specs=pair(D) + pair(wide) + pair(128) + [pl.BlockSpec((256, 128), lambda i: (i, 0))],
        out_specs=pl.BlockSpec((wide, D), lambda i: (0, 0)),
        compiler_params=pltpu.CompilerParams(vmem_limit_bytes=VMEM_LIMIT),
        cost_estimate=pl.CostEstimate(
            flops=4 * number * wide * D, bytes_accessed=4 * number * wide, transcendentals=number
        ),
        name="head_grad",
    )(*rows, *kept, *stat, info)


def backward_kernel(owner, coord, lens, refs, x, gains, cos_q, sin_q, cos_k, sin_k, *rest):
    q, k, v, h1, gate, up, h2, c = rest[:8]
    truth, wanted, u0, u1, u2, u3 = rest[8:14]
    parts = rest[14:32]
    act, dx_out, gain_out, info_out, loss_out = rest[32:37]
    held, sem = rest[37:]
    start_weights(coord, parts, held, sem)
    valid, chosen = masks(lens)
    select = jnp.where(chosen, 1.0, 0.0).astype(jnp.bfloat16)
    top, total, mixed = merge([unpack(part[...]) for part in (u0, u1, u2, u3)])
    norm = top + jnp.log(total)
    target = high(truth[...])
    picked = jnp.sum(high(c[...]) * target, axis=-1, keepdims=True)
    scored = wanted[:, 0:1]
    terms = (picked - norm) * scored
    seq = iota((PAIR_ROWS, 1), 0) >> 4
    logp = [jnp.sum(jnp.where(seq == n, terms, 0.0), axis=0, keepdims=True) for n in range(2 * MB)]
    weight = jnp.zeros((PAIR_ROWS, 1), jnp.float32)
    loss = jnp.zeros((1, 1), jnp.float32)
    for n in range(MB):
        margin = DPO_BETA * ((logp[2 * n] - refs[2 * n]) - (logp[2 * n + 1] - refs[2 * n + 1]))
        loss = loss + jnp.maximum(-margin, 0.0) + jnp.log1p(jnp.exp(-jnp.abs(margin)))
        slope = -DPO_BETA * jax.nn.sigmoid(-margin)
        weight = jnp.where(seq == 2 * n, slope, jnp.where(seq == 2 * n + 1, -slope, weight))
    weight = weight * scored
    loss_out[...] = jnp.broadcast_to(loss, loss_out.shape)
    lane = iota((PAIR_ROWS, 128), 1)
    info_out[...] = jnp.where(
        lane == 0, weight, jnp.where(lane == 1, norm, jnp.where(lane == 2, wanted[:, 1:2], 0.0))
    )
    grad_c = weight * (target - mixed / total)
    d2, gain_top = rms_back(h2[...], gains[2:3, :], grad_c)
    gain_out[2:3, :] = gain_top
    d2_low = low(d2)
    act[AT_DH:RIGHT_ROWS] = d2_low
    wait_weights(held, sem)
    grad_b = jnp.zeros((PAIR_ROWS, D), jnp.float32)
    for r in range(FF // D):
        grad_mix = dot_nt(d2_low[:, :BC], held[owner[24 + 2 * r]]) + dot_nt(
            d2_low[:, BC:], held[owner[25 + 2 * r]]
        )
        at = slice(r * D, (r + 1) * D)
        gate_pre = gate[:, at]
        sig = jax.nn.sigmoid(gate_pre)
        d_gate = low(grad_mix * up[:, at] * sig * (1.0 + gate_pre * (1.0 - sig)))
        d_up = low(grad_mix * gate_pre * sig)
        act[AT_DGATE + r * PAIR_ROWS : AT_DGATE + (r + 1) * PAIR_ROWS] = d_gate
        act[AT_DUP + r * PAIR_ROWS : AT_DUP + (r + 1) * PAIR_ROWS] = d_up
        for j in range(2):
            cut = slice(j * BC, (j + 1) * BC)
            grad_b = grad_b + dot_nt(d_gate[:, cut], held[owner[8 + 2 * r + j]])
            grad_b = grad_b + dot_nt(d_up[:, cut], held[owner[16 + 2 * r + j]])
    back, gain_mid = rms_back(h1[...], gains[1:2, :], grad_b)
    gain_out[1:2, :] = gain_mid
    d1 = d2 + back
    d1_low = low(d1)
    act[AT_DO:AT_DGATE] = d1_low
    d_att = low(
        dot_nt(d1_low[:, :BC], held[owner[6]]) + dot_nt(d1_low[:, BC:], held[owner[7]])
    )
    lane_k = iota((TOKENS, 128), 1)
    zero_k = jnp.zeros((TOKENS, 128), jnp.bfloat16)
    zero_q = jnp.zeros((PAIR_ROWS, 128), jnp.bfloat16)
    root = 1.0 / math.sqrt(HDIM)
    for p in range(HEADS // 2):
        at = slice(p * 128, (p + 1) * 128)
        d_q = jnp.zeros((PAIR_ROWS, 128), jnp.float32)
        d_k = jnp.zeros((TOKENS, 128), jnp.float32)
        d_v = jnp.zeros((TOKENS, 128), jnp.float32)
        for h in range(2):
            mine_k = (lane_k >> 6) == h
            mine_q = (lane >> 6) == h
            k_one = jnp.where(mine_k, k[:, at], zero_k)
            q_one = jnp.where(mine_q, q[:, at], zero_q)
            do_one = jnp.where(mine_q, d_att[:, at], zero_q)
            s = dot_nt(q_one, k_one) * root
            s = jnp.where(valid, s, MASKED)
            e = jnp.exp(s - jnp.max(s, axis=-1, keepdims=True))
            prob = e / jnp.sum(e, axis=-1, keepdims=True)
            d_p = dot_nt(do_one, v[:, at])
            d_s = low(prob * (d_p - jnp.sum(prob * d_p, axis=-1, keepdims=True)))
            d_q = d_q + dot_nn(d_s, k_one)
            d_k = d_k + dot_tn(d_s, q_one)
            d_v = d_v + dot_tn(low(prob), do_one)
        act[AT_DQ:AT_DO, at] = low(turn(d_q * root, cos_q[...], sin_q[...], -1.0))
        act[AT_DK:AT_DV, at] = low(turn(d_k * root, cos_k[...], sin_k[...], -1.0))
        act[AT_DV:AT_DQ, at] = low(d_v)
    d_q_all = low(dot_tn(select, act[AT_DQ:AT_DO]))
    grad_a = jnp.zeros((TOKENS, D), jnp.float32)
    for j in range(2):
        cut = slice(j * BC, (j + 1) * BC)
        grad_a = grad_a + dot_nt(d_q_all[:, cut], held[owner[j]])
        grad_a = grad_a + dot_nt(act[AT_DK:AT_DV, cut], held[owner[2 + j]])
        grad_a = grad_a + dot_nt(act[AT_DV:AT_DQ, cut], held[owner[4 + j]])
    back_in, gain_in = rms_back(high(x[...]), gains[0:1, :], grad_a)
    gain_out[0:1, :] = gain_in
    rest_low = low(d1 - high(d1_low))
    dx_out[...] = low(back_in + dot_tn(select, d1_low) + dot_tn(select, rest_low))


def backward_call(owner, coord, lens, refs, x, gains, turns, saved, truth, wanted, parts_u, parts):
    return pl.pallas_call(
        backward_kernel,
        out_shape=(
            jax.ShapeDtypeStruct((RIGHT_ROWS, D), jnp.bfloat16),
            jax.ShapeDtypeStruct((TOKENS, D), jnp.bfloat16),
            jax.ShapeDtypeStruct((3, D), jnp.float32),
            jax.ShapeDtypeStruct((PAIR_ROWS, 128), jnp.float32),
            jax.ShapeDtypeStruct((1, 128), jnp.float32),
        ),
        in_specs=smem(4) + vmem(6 + 8 + 2 + 4) + anywhere(18),
        out_specs=tuple(vmem(5)),
        scratch_shapes=[
            pltpu.VMEM((NBLK, D, BC), jnp.bfloat16),
            pltpu.SemaphoreType.DMA,
        ],
        compiler_params=pltpu.CompilerParams(vmem_limit_bytes=VMEM_LIMIT),
        name="layer_backward",
    )(owner, coord, lens, refs, x, gains, *turns, *saved, truth, wanted, *parts_u, *parts)


def transpose_kernel(coord, mine, theirs, picked, tokens, turned_a, turned_b):
    near_row = pl.multiple_of(192 * (2 * coord[2] + coord[3]), 64)
    far_row = pl.multiple_of(192 * (2 * (1 - coord[2]) + coord[3]), 64)
    for n in range(LEFT_KINDS):
        at = slice(AT_AP + n * PAIR_ROWS, AT_AP + (n + 1) * PAIR_ROWS)
        turned_a[...] = jnp.concatenate([mine[at], theirs[at]], axis=0).T
        picked[n, :192] = turned_a[pl.ds(near_row, 192), :]
        picked[n, 192:] = turned_a[pl.ds(far_row, 192), :]
    turned_b[:, :TOKENS] = mine[AT_A:AT_AP].T
    turned_b[:, TOKENS:] = theirs[AT_A:AT_AP].T
    tokens[:192] = turned_b[pl.ds(near_row, 192), :]
    tokens[192:] = turned_b[pl.ds(far_row, 192), :]


def transpose_call(coord, mine, theirs):
    return pl.pallas_call(
        transpose_kernel,
        out_shape=(
            jax.ShapeDtypeStruct((LEFT_KINDS, 384, 2 * PAIR_ROWS), jnp.bfloat16),
            jax.ShapeDtypeStruct((384, 2 * TOKENS), jnp.bfloat16),
        ),
        in_specs=smem(1) + vmem(2),
        out_specs=tuple(vmem(2)),
        scratch_shapes=[
            pltpu.VMEM((D, 2 * PAIR_ROWS), jnp.bfloat16),
            pltpu.VMEM((D, 2 * TOKENS), jnp.bfloat16),
        ],
        compiler_params=pltpu.CompilerParams(vmem_limit_bytes=VMEM_LIMIT),
        cost_estimate=pl.CostEstimate(
            flops=0, bytes_accessed=8 * LEFT_ROWS * D, transcendentals=0
        ),
        name="left_transposed",
    )(coord, mine, theirs)


def weight_grad_kernel(block_of, x_at, y_at, coord, picked, tokens, mine, theirs, *rest):
    outs = rest[:-3]
    near_held, far_held, sem = rest[-3:]
    first = coord[3] == 0
    for group, (k, x_flip) in enumerate((k, x_flip) for k in range(4) for x_flip in range(2)):
        x = coord[1] + x_flip * (1 - 2 * coord[1])

        def step(n, carry):
            z = n if k != 2 else (coord[0] + 4 - n) & 3
            slot = 8 * z + 4 * x + k
            block = block_of[slot]
            cut = pl.ds(pl.multiple_of((block & 1) * BC, 128), BC)
            y_row = pl.multiple_of(y_at[slot], 64)

            def put(left, rows):
                right = jnp.concatenate(
                    [mine[pl.ds(y_row, rows), cut], theirs[pl.ds(y_row, rows), cut]], axis=0
                )
                grad = low(dot_nn(left, right))
                near_held[group, n] = grad[:192]
                far_held[group, n] = grad[192:]

            wide = (block >= 2) & (block < 6)

            @pl.when(wide)
            def _():
                put(tokens[...], TOKENS)

            @pl.when(jnp.logical_not(wide))
            def _():
                put(picked[x_at[slot]], PAIR_ROWS)

            return carry

        lax.fori_loop(0, 4, step, 0)

        def send(held, rel):
            if k == 3:
                target = outs[8].at[:, rel]
            elif k == 2:
                target = outs[4 + rel]
            else:
                target = outs[rel].at[:, k]
            pltpu.make_async_copy(held.at[group], target, sem).start()

        if x_flip == 0:
            send(near_held, 0)
            side = far_held
        else:
            send(far_held, 3)
            side = near_held

        @pl.when(first == (x_flip == 1))
        def _():
            send(side, 1)

        @pl.when(first == (x_flip == 0))
        def _():
            send(side, 2)

    pltpu.make_async_copy(near_held, near_held, sem).wait()
    pltpu.make_async_copy(far_held, far_held, sem).wait()


def weight_grad_call(*args):
    shapes = [(4, 2)] * 4 + [(4,)] * 4 + [(4, 4)]
    made = [jax.ShapeDtypeStruct(shape + (192, BC), jnp.bfloat16) for shape in shapes]
    held = pltpu.VMEM((8, 4, 192, BC), jnp.bfloat16)
    return pl.pallas_call(
        weight_grad_kernel,
        out_shape=tuple(made),
        in_specs=smem(4) + vmem(4),
        out_specs=tuple(anywhere(len(made))),
        scratch_shapes=[held, held, pltpu.SemaphoreType.DMA],
        compiler_params=pltpu.CompilerParams(vmem_limit_bytes=VMEM_LIMIT),
        name="weight_grads",
    )(*args)


def shampoo_kernel(coord, *refs):
    own, by_y, by_core, by_both, lstat, rstat, lroot, rroot, blk = refs[:9]
    new_b, grad_out, new_l, new_r, whole = refs[-5:]
    y, core = coord[2], coord[3]
    for piece, y_at, core_at in (
        (own, y, core),
        (by_y, 1 - y, core),
        (by_core, y, 1 - core),
        (by_both, 1 - y, 1 - core),
    ):
        row = pl.multiple_of(192 * (2 * y_at + core_at), 64)
        whole[pl.ds(row, 192), :] = piece[0]
    grad_out[0] = high(own[0])
    grad = whole[...]
    new_l[0] = STAT_DECAY * lstat[0] + (1.0 - STAT_DECAY) * dot_nt(grad, grad)
    new_r[0] = STAT_DECAY * rstat[0] + (1.0 - STAT_DECAY) * dot_tn(grad, grad)
    turned = dot_nn(low(lroot[0]), grad)
    new_b[0] = blk[0] - SHAMPOO_RATE * dot_nn(low(turned), low(rroot[0]))


def shampoo_call(start, coord, pieces, lstat, rstat, lroot, rroot, blk, so_far):
    def one(rows, columns):
        return pl.BlockSpec((1, rows, columns), lambda i, coord: (start + i, 0, 0))

    slots = pieces[0].shape[0]
    in_specs = (
        [pl.BlockSpec((1, 192, BC), lambda i, coord: (i, 0, 0))] * 4
        + [
            one(D, D),
            one(BC, BC),
            pl.BlockSpec((1, 192, D), lambda i, coord: (start + i, 2 * coord[2] + coord[3], 0)),
            one(BC, BC),
            one(192, BC),
        ]
        + anywhere(len(so_far))
    )
    return pl.pallas_call(
        shampoo_kernel,
        grid_spec=pltpu.PrefetchScalarGridSpec(
            num_scalar_prefetch=1,
            grid=(slots,),
            in_specs=in_specs,
            out_specs=(one(192, BC), one(192, BC), one(D, D), one(BC, BC)),
            scratch_shapes=[pltpu.VMEM((D, BC), jnp.bfloat16)],
        ),
        out_shape=(
            jax.ShapeDtypeStruct(blk.shape, jnp.float32),
            jax.ShapeDtypeStruct(blk.shape, jnp.float32),
            jax.ShapeDtypeStruct(lstat.shape, jnp.float32),
            jax.ShapeDtypeStruct(rstat.shape, jnp.float32),
        ),
        input_output_aliases={10 + n: n for n in range(len(so_far))},
        compiler_params=pltpu.CompilerParams(vmem_limit_bytes=VMEM_LIMIT),
        cost_estimate=pl.CostEstimate(
            flops=4 * slots * D * D * BC,
            bytes_accessed=8 * slots * 1024 * 1024,
            transcendentals=0,
        ),
        name="shampoo",
    )(coord, *pieces, lstat, rstat, lroot, rroot, blk, *so_far)


def adam_kernel(rate, grad, w, m, v, *rest):
    new_w, new_m, new_v = rest[-3:]
    new_w[0], new_m[0], new_v[0] = adam_step(w[0], grad[...], m[0], v[0], rate)


def adam_call(table, rate, grad, w, m, v, so_far):
    rows = w.shape[1]
    block = next(n for n in (200, 40, 8) if rows % n == 0)
    spec = pl.BlockSpec((1, block, D), lambda j: (table, j, 0))
    return pl.pallas_call(
        functools.partial(adam_kernel, rate),
        grid=(rows // block,),
        out_shape=(jax.ShapeDtypeStruct(w.shape, jnp.float32),) * 3,
        in_specs=[pl.BlockSpec((block, D), lambda j: (j, 0)), spec, spec, spec]
        + anywhere(len(so_far)),
        out_specs=(spec,) * 3,
        input_output_aliases={4 + n: n for n in range(len(so_far))},
        compiler_params=pltpu.CompilerParams(vmem_limit_bytes=VMEM_LIMIT),
        cost_estimate=pl.CostEstimate(
            flops=10 * rows * D, bytes_accessed=28 * rows * D, transcendentals=rows * D
        ),
        name="adam",
    )(grad, w, m, v, *so_far)


def block_rows():
    x_at, y_at = [], []
    for b in range(NBLK):
        if b < 2:
            x_at.append(0), y_at.append(AT_DQ)
        elif b < 4:
            x_at.append(0), y_at.append(AT_DK)
        elif b < 6:
            x_at.append(0), y_at.append(AT_DV)
        elif b < 8:
            x_at.append(1), y_at.append(AT_DO)
        elif b < 16:
            x_at.append(2), y_at.append(AT_DGATE + (b - 8) // 2 * PAIR_ROWS)
        elif b < 24:
            x_at.append(2), y_at.append(AT_DUP + (b - 16) // 2 * PAIR_ROWS)
        else:
            x_at.append(3 + (b - 24) // 2), y_at.append(AT_DH)
    return jnp.array(x_at, jnp.int32), jnp.array(y_at, jnp.int32)


def per_core(
    token_ids,
    lengths,
    comp_mask,
    ref_logp,
    owner,
    blocks,
    left_stat,
    right_stat,
    left_root,
    right_root,
    tables,
    table_moment,
    table_second,
    gains,
    gain_moment,
    gain_second,
):
    zi, xi, yi, ci = (lax.axis_index(name) for name in AXES)
    coord = jnp.stack([zi, xi, yi, ci]).astype(jnp.int32)
    vocab_index = 2 * yi + ci
    shard = vocab_index * 8 + 2 * zi + xi
    table_rows = tables.shape[1]
    vocab = table_rows * 32
    seqs = 2 * MB
    shares = blocks.astype(jnp.bfloat16)
    with jax.named_scope("weights_last"):
        one, two = hop_one(shares[3]), hop_two(shares[3])
        last = jnp.stack([shares[3], one, two, hop_two(one)])
    with jax.named_scope("weights_third"):
        line3 = all_round(shares[2])
    with jax.named_scope("weights_pair"):
        line = lax.all_gather(shares[:2], "z")
    first_pair = vocab_index * MB
    ids = lax.dynamic_slice_in_dim(token_ids, first_pair, MB, 0).reshape(seqs, SLOT)
    lens = lax.dynamic_slice_in_dim(lengths, first_pair, MB, 0).reshape(seqs)
    wanted = lax.dynamic_slice_in_dim(comp_mask, first_pair, MB, 0).reshape(PAIR_ROWS)
    refs = lax.dynamic_slice_in_dim(ref_logp, first_pair, MB, 0).reshape(seqs)
    places = jnp.arange(SLOT)
    pos = (lens[:, None] - 1 - CMP + jnp.arange(CMP)[None, :]).astype(jnp.int32)
    targets = jnp.sum(
        jnp.where(places[None, None, :] == (pos + 1)[:, :, None], ids[:, None, :], 0), axis=-1
    ).reshape(PAIR_ROWS)
    asked = jnp.concatenate([ids.reshape(TOKENS), targets + vocab])
    used = jnp.concatenate(
        [(places[None, :] < lens[:, None]).reshape(TOKENS), jnp.ones((PAIR_ROWS,), bool)]
    )
    number = jnp.where(asked >= vocab, asked - vocab, asked)
    holder = number // table_rows
    local_row = number - holder * table_rows + jnp.where(asked >= vocab, table_rows, 0)
    total = asked.shape[0]
    earlier = jnp.arange(total)[None, :] < jnp.arange(total)[:, None]
    same = (asked[:, None] == asked[None, :]) & used[:, None] & used[None, :]
    first = used & jnp.logical_not(jnp.any(same & earlier, axis=1))
    rank = jnp.sum(
        ((holder[:, None] == holder[None, :]) & earlier & first[None, :]).astype(jnp.int32), axis=1
    )
    most = jnp.where(jnp.arange(total) < TOKENS, CAP_BACK, CAP)
    spill = jnp.any(first & (rank >= most))
    seat_first = jnp.where(first & (rank < CAP), holder * CAP + rank, -1)
    seat = jnp.sum(jnp.where(same & first[None, :], seat_first[None, :] + 1, 0), axis=1) - 1
    seats = jnp.arange(32 * CAP)
    request = jnp.sum(
        jnp.where(seat_first[:, None] == seats[None, :], local_row[:, None], 0), axis=0
    )
    message = jnp.concatenate(
        [
            request.reshape(32, CAP),
            jnp.broadcast_to(spill.astype(jnp.int32), (32, MSG - CAP)),
        ],
        axis=1,
    )
    message = lax.all_to_all(message, SHARD_AXES, 0, 0, tiled=True)
    line3, last, message = together(line3, last, message)
    any_spill = jnp.max(message[:, MSG - 1]) > 0
    asked_rows = message[:, :CAP].reshape(32 * CAP)
    table_low = tables.astype(jnp.bfloat16).reshape(2 * table_rows, D)
    give = (asked_rows[:, None] == jnp.arange(2 * table_rows)[None, :]).astype(jnp.bfloat16)
    given = low(dot_nn(give, table_low))
    with jax.named_scope("weights_third"):
        one3, two3 = hop_one(line3), hop_two(line3)
    one3, two3, given, line, last = together(one3, two3, given, line, last)
    got = lax.all_to_all(given, SHARD_AXES, 0, 0, tiled=True)
    with jax.named_scope("weights_last"):
        last = lax.all_gather(last, "z")
    with jax.named_scope("weights_third"):
        third = [line3, one3, two3, hop_two(one3)]
    with jax.named_scope("weights_pair"):
        one, two = hop_one(line), hop_two(line)
    one, two, third[3] = together(one, two, third[3])
    with jax.named_scope("weights_pair"):
        pair = [line, one, two, hop_two(one)]
    place = (seat[:, None] == seats[None, :]).astype(jnp.bfloat16)
    rows = low(dot_nn(place, got))
    x, truth = rows[:TOKENS], rows[TOKENS:]
    inv_freq = ROPE_BASE ** (-jnp.arange(HDIM // 2).astype(jnp.float32) * 2.0 / HDIM)
    phase = places.astype(jnp.float32)[:, None] * inv_freq[None, :]
    phase_pick = pos.reshape(PAIR_ROWS).astype(jnp.float32)[:, None] * inv_freq[None, :]

    def turning(angle, repeat):
        cosine, sine = jnp.cos(angle), jnp.sin(angle)
        return (
            jnp.tile(jnp.concatenate([cosine] * 4, axis=1), (repeat, 1)),
            jnp.tile(jnp.concatenate([-sine, sine, -sine, sine], axis=1), (repeat, 1)),
        )

    turns = turning(phase_pick, 1) + turning(phase, seqs)
    last = after(last, x, truth, *turns)
    parts = []
    for part in pair + third + [last]:
        parts.extend([part, hop_core(part)])
    left, *saved = forward_call(owner, coord, lens, x, gains, turns, parts)
    plane, _ = spread(saved[-1])
    plane = plane.reshape(-1, D)
    other = hop_core(plane)
    left_t = transpose_call(coord, left, hop_core(left))
    wide = -(-table_rows // 128) * 128
    head_low = jnp.pad(table_low[table_rows:], ((0, wide - table_rows), (0, 0)))
    ext_other, kept_other, stat_other = head_call(other, head_low, table_rows)
    ext_hop = hop_core(ext_other)
    ext_own, kept_own, stat_own = head_call(plane, head_low, table_rows)
    both = merge_call([(ext_own, 3), (ext_hop, 3)])[0]
    two = merge_call([(ext_own, 2), (ext_hop, 2)])[0]
    one = merge_call([(ext_own, 1), (ext_hop, 1), (hop_two(both), 0)])[0]
    pieces = merge_call([(ext_own, 0), (ext_hop, 0), (hop_one(one), 0), (hop_two(two), 0)], 4)
    pieces = lax.optimization_barrier(tuple(pieces) + tuple(left_t))[:4]
    parts_u = [pieces[0]] + [ring(pieces[step], -step) for step in range(1, 4)]
    marks = jnp.stack([wanted.astype(jnp.float32), targets.astype(jnp.float32)], axis=1)
    marks = jnp.pad(marks, ((0, 0), (0, 126)))
    act, dx, gain_part, info, loss_part = backward_call(
        owner, coord, lens, refs, x, gains, turns, saved, truth, marks, parts_u, parts
    )
    inverse = jnp.sum(
        jnp.where(
            owner[None, :] == jnp.arange(NBLK)[:, None], jnp.arange(NBLK, dtype=jnp.int32)[None, :], 0
        ),
        axis=1,
    )
    x_at, y_at = block_rows()
    chosen = (inverse[:, None] == jnp.arange(NBLK)[None, :]).astype(jnp.int32)
    grad_args = (
        inverse,
        jnp.sum(chosen * x_at[None, :], axis=1),
        jnp.sum(chosen * y_at[None, :], axis=1),
        coord,
        *left_t,
        act,
        hop_core(act),
    )

    def plus(*values):
        return low(sum(high(value) for value in values))

    grads = weight_grad_call(*grad_args)
    info, gain_part, loss_part, dx, *grads = together(info, gain_part, loss_part, dx, *grads)
    own, one, two, both = grads[:4]
    own3, one3, two3, both3, ends = grads[4:]
    with jax.named_scope("grads_pair"):
        one = plus(one, hop_two(both))
    with jax.named_scope("grads_last"):
        last = lax.psum_scatter(
            ends.reshape(16, 192, BC), "z", scatter_dimension=0, tiled=True
        )
    back = place[:TOKENS].reshape(TOKENS, 32, CAP)[:, :, :CAP_BACK].reshape(TOKENS, 32 * CAP_BACK)
    sent = low(dot_tn(back, dx))
    one, two, both3, sent, info, gain_part, loss_part = together(
        one, two, both3, sent, info, gain_part, loss_part
    )
    told = info[:, :3].reshape(-1)
    known = told.shape[0]
    told = jnp.concatenate([told, gain_part.reshape(-1), loss_part[0]])
    told = jnp.broadcast_to(told[None], (32, told.shape[0]))
    heard = lax.all_to_all(told, AXES, 0, 0, tiled=True)
    with jax.named_scope("grads_pair"):
        line = plus(own, hop_one(one), hop_two(two)).reshape(8, 192, BC)
    with jax.named_scope("grads_third"):
        one3 = plus(one3, hop_two(both3))
    back_rows = lax.all_to_all(sent, SHARD_AXES, 0, 0, tiled=True)
    summed = jnp.sum(heard[:, known:], axis=0)
    sources = []
    for other_core in range(2):
        for rel in range(4):
            for back in range(4):
                sources.append(
                    flat_of((zi + 4 - back) % 4, *place_of((zi, xi, yi, ci), other_core, rel))
                )
    sources = jnp.stack(sources)
    infos = jnp.sum(
        jnp.where(
            (sources[:, None] == jnp.arange(32)[None, :])[:, :, None],
            heard[None, :, :known],
            0.0,
        ),
        axis=1,
    ).reshape(-1, 3)
    infos = jnp.concatenate(
        [infos[:, :2], infos[:, 2:3] - (shard * table_rows).astype(jnp.float32)], axis=1
    )
    infos = jnp.pad(infos, ((0, 0), (0, 125)))
    grad_head = head_grad_call(
        (plane, other), (kept_own, kept_other), (stat_own, stat_other), infos
    )
    adam = adam_call(1, 0.02, grad_head, tables, table_moment, table_second, ())
    line, one3, two3, last, *adam = together(line, one3, two3, last, *adam)
    with jax.named_scope("grads_pair"):
        pair = lax.psum_scatter(line, "z", scatter_dimension=0, tiled=True)
    with jax.named_scope("grads_third"):
        one3, two3 = hop_one(one3), hop_two(two3)
        line3 = [plus(own3[n], one3[n], two3[n]) for n in range(4)]
    with jax.named_scope("grads_last"):
        one, two = plus(last[1], hop_two(last[3])), hop_two(last[2])
    back_at = message[:, :CAP_BACK].reshape(32 * CAP_BACK)
    take_back = (back_at[None, :] == jnp.arange(table_rows)[:, None]).astype(jnp.bfloat16)
    grad_embed = dot_nn(take_back, back_rows)
    new_tables, new_table_moment, new_table_second = adam_call(
        0, 0.3, grad_embed, tables, table_moment, table_second, adam
    )
    new_gains, new_gain_moment, new_gain_second = adam_step(
        gains, summed[: 3 * D].reshape(3, D), gain_moment, gain_second, GAIN_RATE
    )
    loss_sum = summed[3 * D]
    one, two, new_tables, new_gains, new_gain_moment, new_gain_second, *line3 = together(
        one, two, new_tables, new_gains, new_gain_moment, new_gain_second, *line3
    )
    pair_y = hop_y(pair)
    with jax.named_scope("grads_third"):
        around = [ring(line3[step], -step) for step in range(1, 4)]
        third = plus(after(line3[0], pair_y), *around)
    with jax.named_scope("grads_last"):
        last = plus(last[0], hop_one(one), two)

    rights = (left_stat, right_stat, left_root, right_root, blocks)
    late = jnp.stack([third, last])
    late_y = hop_y(late)
    results = shampoo_call(
        0, coord, (pair, pair_y, hop_core(pair), hop_core(pair_y)), *rights, ()
    )
    late_y, *results = together(late_y, *results)
    new_blocks, block_grads, new_left, new_right = shampoo_call(
        2, coord, (late, late_y, hop_core(late), hop_core(late_y)), *rights, results
    )
    quick = (
        new_blocks,
        block_grads,
        new_left,
        new_right,
        new_tables,
        new_table_moment,
        new_table_second,
        new_gains,
        new_gain_moment,
        new_gain_second,
        loss_sum,
    )
    whole = (
        token_ids,
        lengths,
        comp_mask,
        ref_logp,
        owner,
        blocks,
        left_stat,
        right_stat,
        left_root,
        right_root,
        tables,
        table_moment,
        table_second,
        gains,
        gain_moment,
        gain_second,
    )

    def slow(state):
        outs = list(per_device(("z", "x"), ("y", "core"), *whole))
        outs[1] = with_layout_constraint(outs[1], Layout((0, 1, 2)))
        return jnp.zeros((), bool), tuple(outs)

    return lax.while_loop(lambda state: state[0], slow, (any_spill, quick))[1]


def solution(mesh):
    tuned = mesh.shape["dp"] == 8 and mesh.shape["vocab"] == 4
    if tuned:
        dp, vocab = ("z", "x"), ("y", "core")
        where = Mesh(mesh.devices.reshape(4, 2, 2, 2), AXES)
        body = per_core
    else:
        dp, vocab = ("dp",), ("vocab",)
        where = mesh
        body = functools.partial(per_device, ("dp",), ("vocab",))
    placed = (
        P(dp, None, None),
        P(dp, None),
        P(dp, None, None),
        P(dp, None),
        P(),
        P(dp, vocab, None),
        P(dp, None, None),
        P(dp, None, None),
        P(dp, None, None),
        P(dp, None, None),
        P(None, vocab + dp, None),
        P(None, vocab + dp, None),
        P(None, vocab + dp, None),
        P(),
        P(),
        P(),
    )
    return jax.shard_map(
        body,
        mesh=where,
        in_specs=placed,
        out_specs=(
            P(dp, vocab, None),
            P(dp, vocab, None),
            P(dp, None, None),
            P(dp, None, None),
            P(None, vocab + dp, None),
            P(None, vocab + dp, None),
            P(None, vocab + dp, None),
            P(),
            P(),
            P(),
            P(),
        ),
        check_vma=False,
    )
```

```python
import functools
import math

import jax
import jax.numpy as jnp
from jax import lax
from jax.experimental import pallas as pl
from jax.experimental.layout import Layout, with_layout_constraint
from jax.experimental.pallas import tpu as pltpu
from jax.sharding import Mesh
from jax.sharding import PartitionSpec as P

D = 768
HEADS = 12
HDIM = 64
FF = 3072
SLOT = 64
MB = 2
CMP = 16
STEP = 10
BC = 384
NBLK = 32


NORM_EPS = 1e-05
DPO_BETA = 0.02
ROPE_BASE = 10000.0
ADAM_ONE = 0.9
ADAM_TWO = 0.999
ADAM_EPS = 1e-08
WEIGHT_DECAY = 0.01
GAIN_RATE = 0.3
STAT_DECAY = 0.5
SHAMPOO_RATE = 0.5
MASKED = -1e30


def joined(value, axis, join):
    pieces = jax.tree.map(lambda part: lax.all_gather(part, axis), value)
    head = jax.tree.map(lambda part: part[0], pieces)
    tail = jax.tree.map(lambda part: part[1:], pieces)
    so_far, _ = lax.scan(lambda so_far, section: (join(so_far, section), None), head, tail)
    return so_far


def mult(left, right):
    return jnp.dot(left, right, preferred_element_type=jnp.float32)


def mult_t(left, right):
    return lax.dot_general(
        left, right, (((0,), (0,)), ((), ())), preferred_element_type=jnp.float32
    )


def mult_nt(left, right):
    return lax.dot_general(
        left, right, (((1,), (1,)), ((), ())), preferred_element_type=jnp.float32
    )


def project(rows, group):
    product = jnp.einsum("td,ndk->tnk", rows, group, preferred_element_type=jnp.float32)
    return product.reshape(rows.shape[0], group.shape[0] * BC)


def project_back(grad, group):
    return jnp.einsum(
        "tnk,ndk->td",
        grad.reshape(grad.shape[0], group.shape[0], BC),
        group,
        preferred_element_type=jnp.float32,
    )


def block_grad(rows, grad, number):
    return jnp.einsum(
        "td,tnk->ndk",
        rows,
        grad.reshape(grad.shape[0], number, BC),
        preferred_element_type=jnp.float32,
    )


def down_forward(mix, down):
    row_total = mix.shape[0]
    product = jnp.einsum(
        "trd,rjdk->tjk",
        mix.reshape(row_total, FF // D, D),
        down.reshape(FF // D, D // BC, D, BC),
        preferred_element_type=jnp.float32,
    )
    return product.reshape(row_total, D)


def down_back(grad, down):
    row_total = grad.shape[0]
    product = jnp.einsum(
        "tjk,rjdk->trd",
        grad.reshape(row_total, D // BC, BC),
        down.reshape(FF // D, D // BC, D, BC),
        preferred_element_type=jnp.float32,
    )
    return product.reshape(row_total, FF)


def down_grad(mix, grad):
    row_total = mix.shape[0]
    product = jnp.einsum(
        "trd,tjk->rjdk",
        mix.reshape(row_total, FF // D, D),
        grad.reshape(row_total, D // BC, BC),
        preferred_element_type=jnp.float32,
    )
    return product.reshape(-1, D, BC)


def groups(weights):
    col_blocks = D // BC
    ff_blocks = FF // BC
    base_gate = 4 * col_blocks
    return (
        weights[0:col_blocks],
        weights[col_blocks : 2 * col_blocks],
        weights[2 * col_blocks : 3 * col_blocks],
        weights[3 * col_blocks : base_gate],
        weights[base_gate : base_gate + ff_blocks],
        weights[base_gate + ff_blocks : base_gate + 2 * ff_blocks],
        weights[base_gate + 2 * ff_blocks :],
    )


def rms_forward(values, gain):
    return values * lax.rsqrt(jnp.mean(values * values, axis=-1, keepdims=True) + NORM_EPS) * gain


def rms_backward(values, gain, grad):
    scale = lax.rsqrt(jnp.mean(values * values, axis=-1, keepdims=True) + NORM_EPS)
    inner = jnp.mean(values * gain * grad, axis=-1, keepdims=True)
    back = scale * gain * grad - values * scale**3 * inner
    return (back, jnp.sum(grad * values * scale, axis=0))


def angles():
    inv_freq = ROPE_BASE ** (-jnp.arange(HDIM // 2).astype(jnp.float32) * 2.0 / HDIM)
    phase_grid = jnp.arange(SLOT).astype(jnp.float32)[:, None] * inv_freq[None, :]
    return (jnp.cos(phase_grid), jnp.sin(phase_grid))


def rotate(values, cosine, sine, direction):
    half_dim = HDIM // 2
    lead_half = values[..., :half_dim]
    tail_half = values[..., half_dim:]
    cos_grid = cosine[None, :, None, :]
    sin_grid = direction * sine[None, :, None, :]
    return jnp.concatenate(
        [lead_half * cos_grid - tail_half * sin_grid, tail_half * cos_grid + lead_half * sin_grid],
        axis=-1,
    )


def attend_scores(q_rot, k_rot, len_vec):
    raw = jnp.einsum(
        "nqhd,nkhd->nhqk", q_rot, k_rot, preferred_element_type=jnp.float32
    ) / math.sqrt(HDIM)
    places = jnp.arange(SLOT)
    valid = (places[None, :] <= places[:, None])[None, None] & (
        places[None, None, None, :] < len_vec[:, None, None, None]
    )
    return jnp.where(valid, raw, MASKED)


def layer_forward(inputs, len_vec, gains, mats, cosine, sine):
    w_query, w_key, w_value, w_out, w_gate, w_up, w_down = mats
    seq_count = inputs.shape[0] // SLOT

    def to_heads(values):
        return values.reshape(seq_count, SLOT, HEADS, HDIM)

    a_low = rms_forward(inputs, gains[0]).astype(jnp.bfloat16)
    q_rot = rotate(to_heads(project(a_low, w_query)), cosine, sine, 1.0).astype(jnp.bfloat16)
    k_rot = rotate(to_heads(project(a_low, w_key)), cosine, sine, 1.0).astype(jnp.bfloat16)
    v_heads = to_heads(project(a_low, w_value)).astype(jnp.bfloat16)
    scores = attend_scores(q_rot, k_rot, len_vec)
    row_max = jnp.max(scores, axis=-1, keepdims=True)
    log_total = jnp.log(jnp.sum(jnp.exp(scores - row_max), axis=-1, keepdims=True)) + row_max
    p_low = jnp.exp(scores - log_total).astype(jnp.bfloat16)
    att_out = jnp.einsum("nhqk,nkhd->nqhd", p_low, v_heads, preferred_element_type=jnp.float32)
    att_out = att_out.reshape(seq_count * SLOT, D).astype(jnp.bfloat16)
    h_mid = inputs + project(att_out, w_out)
    b_low = rms_forward(h_mid, gains[1]).astype(jnp.bfloat16)
    gate_pre = project(b_low, w_gate)
    up_pre = project(b_low, w_up)
    mix_low = (jax.nn.silu(gate_pre) * up_pre).astype(jnp.bfloat16)
    h_out = h_mid + down_forward(mix_low, w_down)
    return (
        h_out,
        (a_low, q_rot, k_rot, v_heads, log_total, att_out, h_mid, b_low, gate_pre, up_pre, mix_low),
    )


def layer_backward(inputs, len_vec, gains, mats, cosine, sine, saved, grad_out):
    w_query, w_key, w_value, w_out, w_gate, w_up, w_down = mats
    a_low, q_rot, k_rot, v_heads, log_total, att_out, h_mid, b_low, gate_pre, up_pre, mix_low = (
        saved
    )
    seq_count = inputs.shape[0] // SLOT
    grad_branch = grad_out.astype(jnp.bfloat16)
    grad_mix = down_back(grad_branch, w_down)
    sigmoid_gate = jax.nn.sigmoid(gate_pre)
    grad_gate = (grad_mix * up_pre * sigmoid_gate * (1.0 + gate_pre * (1.0 - sigmoid_gate))).astype(
        jnp.bfloat16
    )
    grad_up = (grad_mix * gate_pre * sigmoid_gate).astype(jnp.bfloat16)
    grad_b = project_back(grad_gate, w_gate) + project_back(grad_up, w_up)
    back_mid, gain_mid = rms_backward(h_mid, gains[1], grad_b)
    grad_mid = grad_out + back_mid
    grad_attn = grad_mid.astype(jnp.bfloat16)
    grad_att = (
        project_back(grad_attn, w_out).astype(jnp.bfloat16).reshape(seq_count, SLOT, HEADS, HDIM)
    )
    p_full = jnp.exp(attend_scores(q_rot, k_rot, len_vec) - log_total)
    grad_p = jnp.einsum("nqhd,nkhd->nhqk", grad_att, v_heads, preferred_element_type=jnp.float32)
    grad_s = (p_full * (grad_p - jnp.sum(p_full * grad_p, axis=-1, keepdims=True))).astype(
        jnp.bfloat16
    )
    grad_q = jnp.einsum(
        "nhqk,nkhd->nqhd", grad_s, k_rot, preferred_element_type=jnp.float32
    ) / math.sqrt(HDIM)
    grad_k = jnp.einsum(
        "nhqk,nqhd->nkhd", grad_s, q_rot, preferred_element_type=jnp.float32
    ) / math.sqrt(HDIM)
    grad_v = jnp.einsum(
        "nhqk,nqhd->nkhd", p_full.astype(jnp.bfloat16), grad_att, preferred_element_type=jnp.float32
    )
    row_total = seq_count * SLOT
    grad_q = rotate(grad_q, cosine, sine, -1.0).reshape(row_total, D).astype(jnp.bfloat16)
    grad_k = rotate(grad_k, cosine, sine, -1.0).reshape(row_total, D).astype(jnp.bfloat16)
    grad_v = grad_v.reshape(row_total, D).astype(jnp.bfloat16)
    grad_a = (
        project_back(grad_q, w_query) + project_back(grad_k, w_key) + project_back(grad_v, w_value)
    )
    back_in, gain_in = rms_backward(inputs, gains[0], grad_a)
    operands = (
        a_low,
        grad_q,
        grad_k,
        grad_v,
        att_out,
        grad_attn,
        b_low,
        grad_gate,
        grad_up,
        mix_low,
        grad_branch,
    )
    return (grad_mid + back_in, operands, jnp.stack([gain_in, gain_mid]))


def weight_grads(operands):
    (
        a_low,
        grad_q,
        grad_k,
        grad_v,
        att_out,
        grad_attn,
        b_low,
        grad_gate,
        grad_up,
        mix_low,
        grad_branch,
    ) = operands
    col_blocks = D // BC
    ff_blocks = FF // BC
    return jnp.concatenate(
        [
            block_grad(a_low, grad_q, col_blocks),
            block_grad(a_low, grad_k, col_blocks),
            block_grad(a_low, grad_v, col_blocks),
            block_grad(att_out, grad_attn, col_blocks),
            block_grad(b_low, grad_gate, ff_blocks),
            block_grad(b_low, grad_up, ff_blocks),
            down_grad(mix_low, grad_branch),
        ],
        axis=0,
    )


def combine_parts(earlier, later):
    max_one, sum_one, pick_one = earlier
    max_two, sum_two, pick_two = later
    joint_max = jnp.maximum(max_one, max_two)
    joint_sum = sum_one * jnp.exp(max_one - joint_max) + sum_two * jnp.exp(max_two - joint_max)
    return (joint_max, joint_sum, pick_one + pick_two)


def adam_step(weight, grad, moment, second, rate):
    moment = ADAM_ONE * moment + (1.0 - ADAM_ONE) * grad
    second = ADAM_TWO * second + (1.0 - ADAM_TWO) * grad * grad
    ratio = moment / (1.0 - ADAM_ONE**STEP) / (jnp.sqrt(second / (1.0 - ADAM_TWO**STEP)) + ADAM_EPS)
    return (weight - rate * (ratio + WEIGHT_DECAY * weight), moment, second)


def per_device(
    dp,
    vocab,
    token_ids,
    lengths,
    comp_mask,
    ref_logp,
    owner,
    blocks,
    left_stat,
    right_stat,
    left_root,
    right_root,
    tables,
    table_moment,
    table_second,
    gains,
    gain_moment,
    gain_second,
):
    vocab_count = lax.axis_size(vocab)
    vocab_index = lax.axis_index(vocab)
    row_share = blocks.shape[1]
    cosine, sine = angles()
    tables_low = lax.all_gather(tables.astype(jnp.bfloat16), dp, axis=1, tiled=True)
    vocab_rows = tables_low.shape[1]
    local_ids = token_ids.reshape(-1) - vocab_index * vocab_rows
    inside = (local_ids >= 0) & (local_ids < vocab_rows)
    safe_ids = jnp.clip(local_ids, 0, vocab_rows - 1)
    looked = jnp.where(inside[:, None], jnp.take(tables_low[0], safe_ids, axis=0), 0).astype(
        jnp.float32
    )
    embedded = lax.psum_scatter(
        looked.astype(jnp.bfloat16), vocab, scatter_dimension=0, tiled=True
    ).astype(jnp.float32)
    rows_all = lax.all_gather(blocks.astype(jnp.bfloat16), vocab, axis=1, tiled=True)
    slots_all = lax.all_gather(rows_all, dp, axis=0, tiled=True)
    kept_mats = groups(jnp.take(slots_all, owner, axis=0))
    gain_total = jnp.zeros((3, D), jnp.float32)
    loss_own = jnp.zeros((), jnp.float32)
    grad_inputs = []
    operand_list = []
    logit_grads = []
    head_inputs = []
    for micro in range(MB):
        own_pair = vocab_index * MB + micro
        rows_in = embedded[micro * 2 * SLOT : (micro + 1) * 2 * SLOT]
        len_own = lax.dynamic_index_in_dim(lengths, own_pair, 0, keepdims=False)
        h_out, saved = layer_forward(rows_in, len_own, gains, kept_mats, cosine, sine)
        pos_own = len_own[:, None] - 1 - CMP + jnp.arange(CMP)[None, :]
        picked_rows = jnp.take_along_axis(
            h_out.reshape(2, SLOT, D), pos_own[:, :, None], axis=1
        ).reshape(2 * CMP, D)
        c_low = rms_forward(picked_rows, gains[2]).astype(jnp.bfloat16)
        all_rows = lax.all_gather(c_low, vocab, axis=0, tiled=True)
        ids_sel = token_ids[micro::MB]
        lens_sel = lengths[micro::MB]
        mask_sel = comp_mask[micro::MB].astype(jnp.float32)
        ref_sel = ref_logp[micro::MB]
        pos_sel = lens_sel[:, :, None] - 1 - CMP + jnp.arange(CMP)[None, None, :]
        target = (
            jnp.take_along_axis(ids_sel, pos_sel + 1, axis=2).reshape(-1) - vocab_index * vocab_rows
        )
        logits = mult_nt(all_rows, tables_low[1])
        one_hot = jnp.arange(vocab_rows)[None, :] == target[:, None]
        row_max = jnp.max(logits, axis=1)
        row_sum = jnp.sum(jnp.exp(logits - row_max[:, None]), axis=1)
        row_pick = jnp.sum(jnp.where(one_hot, logits, 0.0), axis=1)
        full_max, full_sum, full_pick = joined((row_max, row_sum, row_pick), vocab, combine_parts)
        log_norm = full_max + jnp.log(full_sum)
        seq_logp = jnp.sum((full_pick - log_norm).reshape(vocab_count, 2, CMP) * mask_sel, axis=2)
        margin = DPO_BETA * (seq_logp[:, 0] - ref_sel[:, 0] - (seq_logp[:, 1] - ref_sel[:, 1]))
        loss_own = loss_own + jnp.take(jax.nn.softplus(-margin), vocab_index)
        pair_weight = -DPO_BETA * jax.nn.sigmoid(-margin)
        grad_tok = (jnp.stack([pair_weight, -pair_weight], axis=1)[:, :, None] * mask_sel).reshape(
            -1
        )
        grad_logits = (
            grad_tok[:, None] * (one_hot.astype(jnp.float32) - jnp.exp(logits - log_norm[:, None]))
        ).astype(jnp.bfloat16)
        logit_grads.append(grad_logits)
        head_inputs.append(all_rows)
        grad_c = lax.psum_scatter(
            mult(grad_logits, tables_low[1]), vocab, scatter_dimension=0, tiled=True
        )
        back_rows, gain_head = rms_backward(picked_rows, gains[2], grad_c)
        seq_index = jnp.arange(2)[:, None]
        grad_top = (
            jnp.zeros((2, SLOT, D), jnp.float32)
            .at[seq_index, pos_own]
            .add(back_rows.reshape(2, CMP, D))
        )
        grad_in, operands, gains_now = layer_backward(
            rows_in, len_own, gains, kept_mats, cosine, sine, saved, grad_top.reshape(2 * SLOT, D)
        )
        operand_list.append(operands)
        gain_total = gain_total + jnp.concatenate([gains_now, gain_head[None]], axis=0)
        grad_inputs.append(grad_in)
    joined_ops = tuple(
        (
            jnp.concatenate([ops[i] for ops in operand_list], axis=0)
            for i in range(len(operand_list[0]))
        )
    )
    block_order = weight_grads(joined_ops)
    grad_head = mult_t(jnp.concatenate(logit_grads, axis=0), jnp.concatenate(head_inputs, axis=0))
    grad_rows = lax.all_gather(
        jnp.concatenate(grad_inputs, axis=0).astype(jnp.bfloat16), vocab, axis=0, tiled=True
    ).astype(jnp.float32)
    grad_embed = (
        jnp.zeros((vocab_rows, D), jnp.float32)
        .at[safe_ids]
        .add(jnp.where(inside[:, None], grad_rows, 0.0))
    )
    table_grad = lax.psum_scatter(
        jnp.stack([grad_embed, grad_head]).astype(jnp.bfloat16),
        dp,
        scatter_dimension=1,
        tiled=True,
    ).astype(jnp.float32)
    inverse = jnp.zeros((NBLK,), jnp.int32).at[owner].set(jnp.arange(NBLK, dtype=jnp.int32))
    slotted = jnp.take(block_order, inverse, axis=0)
    summed = lax.psum_scatter(slotted.astype(jnp.bfloat16), dp, scatter_dimension=0, tiled=True)
    share_part = lax.psum_scatter(summed, vocab, scatter_dimension=1, tiled=True).astype(
        jnp.float32
    )
    whole = lax.all_gather(share_part.astype(jnp.bfloat16), vocab, axis=1, tiled=True).astype(
        share_part.dtype
    )
    highest = lax.Precision.HIGHEST
    new_left = STAT_DECAY * left_stat + (1.0 - STAT_DECAY) * jnp.einsum(
        "bij,bkj->bik", whole, whole, precision=highest
    )
    new_right = STAT_DECAY * right_stat + (1.0 - STAT_DECAY) * jnp.einsum(
        "bji,bjk->bik", whole, whole, precision=highest
    )
    direction = jnp.einsum("bij,bjk->bik", left_root, whole, precision=highest)
    direction = jnp.einsum("bij,bjk->bik", direction, right_root, precision=highest)
    new_blocks = blocks - SHAMPOO_RATE * lax.dynamic_slice_in_dim(
        direction, vocab_index * row_share, row_share, 1
    )
    loss_sum, gain_grad = lax.psum((loss_own, gain_total), dp + vocab)
    rates = jnp.array([0.3, 0.02], jnp.float32)[:, None, None]
    new_tables, new_table_moment, new_table_second = adam_step(
        tables, table_grad, table_moment, table_second, rates
    )
    new_gains, new_gain_moment, new_gain_second = adam_step(
        gains, gain_grad, gain_moment, gain_second, GAIN_RATE
    )
    return (
        new_blocks,
        share_part,
        new_left,
        new_right,
        new_tables,
        new_table_moment,
        new_table_second,
        new_gains,
        new_gain_moment,
        new_gain_second,
        loss_sum,
    )


PAIR_ROWS = MB * 2 * CMP
TOKENS = MB * 2 * SLOT
CAP = 24
CAP_BACK = 18
MSG = 32
EXT = D + 128
AXES = ("z", "x", "y", "core")
SHARD_AXES = ("y", "core", "z", "x")
VMEM_LIMIT = 60 * 1024 * 1024

AT_A = 0
AT_AP = AT_A + TOKENS
AT_O = AT_AP + PAIR_ROWS
AT_B = AT_O + PAIR_ROWS
AT_Z = AT_B + PAIR_ROWS
LEFT_ROWS = AT_Z + (FF // D) * PAIR_ROWS
LEFT_KINDS = (LEFT_ROWS - AT_AP) // PAIR_ROWS
AT_DK = 0
AT_DV = AT_DK + TOKENS
AT_DQ = AT_DV + TOKENS
AT_DO = AT_DQ + PAIR_ROWS
AT_DGATE = AT_DO + PAIR_ROWS
AT_DUP = AT_DGATE + (FF // D) * PAIR_ROWS
AT_DH = AT_DUP + (FF // D) * PAIR_ROWS
RIGHT_ROWS = AT_DH + PAIR_ROWS


def flat_of(z, x, y, c):
    return ((z * 2 + x) * 2 + y) * 2 + c


def moves(target):
    pairs = []
    for z in range(4):
        for x in range(2):
            for y in range(2):
                for c in range(2):
                    pairs.append((flat_of(z, x, y, c), flat_of(*target(z, x, y, c))))
    return pairs


def hop_one(value):
    return lax.ppermute(
        value,
        AXES,
        moves(lambda z, x, y, c: (z, 1 - x, y, c) if c == 0 else (z, x, 1 - y, c)),
    )


def hop_two(value):
    return lax.ppermute(
        value,
        AXES,
        moves(lambda z, x, y, c: (z, x, 1 - y, c) if c == 0 else (z, 1 - x, y, c)),
    )


def hop_core(value):
    return lax.ppermute(value, AXES, moves(lambda z, x, y, c: (z, x, y, 1 - c)))


def hop_y(value):
    return lax.ppermute(value, AXES, moves(lambda z, x, y, c: (z, x, 1 - y, c)))


def ring(value, step):
    return lax.ppermute(value, AXES, moves(lambda z, x, y, c: ((z + step) % 4, x, y, c)))


def after(value, *others):
    return lax.optimization_barrier((value,) + others)[0]


def together(*values):
    return lax.optimization_barrier(values)


def all_round(chunk):
    return jnp.stack([chunk] + [ring(chunk, step) for step in range(1, 4)])


def spread(chunk, wait=()):
    if wait:
        chunk = after(chunk, *wait)
    around = [ring(chunk, step) for step in range(1, 4)]
    line = jnp.stack([chunk] + around)
    one = hop_one(line)
    two = hop_two(line)
    both = hop_two(one)
    return jnp.stack([line, one, two, both]), around


def dot_nn(left, right):
    return lax.dot_general(left, right, (((1,), (0,)), ((), ())), preferred_element_type=jnp.float32)


def dot_nt(left, right):
    return lax.dot_general(left, right, (((1,), (1,)), ((), ())), preferred_element_type=jnp.float32)


def dot_tn(left, right):
    return lax.dot_general(left, right, (((0,), (0,)), ((), ())), preferred_element_type=jnp.float32)


def low(value):
    return value.astype(jnp.bfloat16)


def high(value):
    return value.astype(jnp.float32)


def place_of(coord, other_core, rel):
    core = coord[3] + other_core * (1 - 2 * coord[3])
    first = rel & 1
    second = rel >> 1
    x_flip = first + core * (second - first)
    y_flip = second + core * (first - second)
    x = coord[1] + x_flip * (1 - 2 * coord[1])
    y = coord[2] + y_flip * (1 - 2 * coord[2])
    return x, y, core


def start_weights(coord, parts, held, sem):
    def start(source, slots, y, core):
        row = pl.multiple_of(192 * (2 * y + core), 64)
        pltpu.make_async_copy(source, held.at[slots, pl.ds(row, 192)], sem).start()

    for other_core in range(2):
        for rel in range(4):
            x, y, core = place_of(coord, other_core, rel)
            pair, third, last = (
                parts[2 * rel + other_core],
                parts[8 + 2 * rel + other_core],
                parts[16 + other_core],
            )

            def one(n, carry):
                back = (coord[0] + 4 - n) & 3
                start(pair.at[n], pl.ds(8 * n + 4 * x, 2), y, core)
                start(third.at[n], 8 * back + 4 * x + 2, y, core)
                start(last.at[n, rel], 8 * n + 4 * x + 3, y, core)
                return carry

            lax.fori_loop(0, 4, one, 0)


def wait_weights(held, sem):
    pltpu.make_async_copy(held, held, sem).wait()


def iota(shape, axis):
    return lax.broadcasted_iota(jnp.int32, shape, axis)


def pick_rows(lens):
    row = iota((PAIR_ROWS, 1), 0)
    seq = row >> 4
    length = jnp.where(
        seq == 0, lens[0], jnp.where(seq == 1, lens[1], jnp.where(seq == 2, lens[2], lens[3]))
    )
    return seq, length - 1 - CMP + (row & 15)


def masks(lens):
    seq, pos = pick_rows(lens)
    col = iota((PAIR_ROWS, TOKENS), 1)
    same = (col >> 6) == seq
    key = col & 63
    return same & (key <= pos), same & (key == pos)


def turn(chunk, cosine, sine, sign):
    lane = iota(chunk.shape, 1)
    swapped = jnp.where((lane & 63) < 32, pltpu.roll(chunk, 96, 1), pltpu.roll(chunk, 32, 1))
    return chunk * cosine + swapped * (sine * sign)


def scale_of(values):
    return lax.rsqrt(jnp.mean(values * values, axis=-1, keepdims=True) + NORM_EPS)


def rms_back(values, gain, grad):
    scale = scale_of(values)
    inner = jnp.mean(values * gain * grad, axis=-1, keepdims=True)
    back = scale * gain * grad - values * (scale * scale * scale) * inner
    return back, jnp.sum(grad * values * scale, axis=0, keepdims=True)


def forward_kernel(owner, coord, lens, x, gains, cos_q, sin_q, cos_k, sin_k, *rest):
    parts, rest = rest[:18], rest[18:]
    left, q_out, k_out, v_out, h1_out, gate_out, up_out, h2_out, c_out = rest[:9]
    held, sem = rest[9:]
    start_weights(coord, parts, held, sem)
    values = high(x[...])
    a_low = low(values * scale_of(values) * gains[0:1, :])
    left[AT_A:AT_AP] = a_low
    valid, chosen = masks(lens)
    select = jnp.where(chosen, 1.0, 0.0).astype(jnp.bfloat16)
    a_pick = low(dot_nn(select, a_low))
    left[AT_AP:AT_O] = a_pick
    x_pick = dot_nn(select, x[...])
    wait_weights(held, sem)
    for j in range(2):
        q = dot_nn(a_pick, held[owner[j]])
        k = dot_nn(a_low, held[owner[2 + j]])
        v_out[:, j * BC : (j + 1) * BC] = low(dot_nn(a_low, held[owner[4 + j]]))
        for i in range(3):
            at = slice(j * BC + i * 128, j * BC + (i + 1) * 128)
            q_out[:, at] = low(turn(q[:, i * 128 : (i + 1) * 128], cos_q[...], sin_q[...], 1.0))
            k_out[:, at] = low(turn(k[:, i * 128 : (i + 1) * 128], cos_k[...], sin_k[...], 1.0))
    lane = iota((TOKENS, 128), 1)
    zero = jnp.zeros((TOKENS, 128), jnp.bfloat16)
    for p in range(HEADS // 2):
        at = slice(p * 128, (p + 1) * 128)
        total = jnp.zeros((PAIR_ROWS, 128), jnp.float32)
        for h in range(2):
            mine = (lane >> 6) == h
            s = dot_nt(q_out[:, at], jnp.where(mine, k_out[:, at], zero)) * (1.0 / math.sqrt(HDIM))
            s = jnp.where(valid, s, MASKED)
            e = jnp.exp(s - jnp.max(s, axis=-1, keepdims=True))
            prob = low(e / jnp.sum(e, axis=-1, keepdims=True))
            total = total + dot_nn(prob, jnp.where(mine, v_out[:, at], zero))
        left[AT_O:AT_B, at] = low(total)
    for j in range(2):
        at = slice(j * BC, (j + 1) * BC)
        h1_out[:, at] = x_pick[:, at] + dot_nn(left[AT_O:AT_B], held[owner[6 + j]])
    h1 = h1_out[...]
    b_low = low(h1 * scale_of(h1) * gains[1:2, :])
    left[AT_B:AT_Z] = b_low
    for j in range(FF // BC):
        at = slice(j * BC, (j + 1) * BC)
        gate = dot_nn(b_low, held[owner[8 + j]])
        up = dot_nn(b_low, held[owner[16 + j]])
        gate_out[:, at] = gate
        up_out[:, at] = up
        row = AT_Z + j // 2 * PAIR_ROWS
        left[row : row + PAIR_ROWS, j % 2 * BC : (j % 2 + 1) * BC] = low(
            gate * jax.nn.sigmoid(gate) * up
        )
    for j in range(2):
        total = h1[:, j * BC : (j + 1) * BC]
        for r in range(FF // D):
            row = AT_Z + r * PAIR_ROWS
            total = total + dot_nn(left[row : row + PAIR_ROWS], held[owner[24 + 2 * r + j]])
        h2_out[:, j * BC : (j + 1) * BC] = total
    h2 = h2_out[...]
    c_out[...] = low(h2 * scale_of(h2) * gains[2:3, :])


def vmem(number):
    return [pl.BlockSpec(memory_space=pltpu.VMEM)] * number


def smem(number):
    return [pl.BlockSpec(memory_space=pltpu.SMEM)] * number


def anywhere(number):
    return [pl.BlockSpec(memory_space=pl.ANY)] * number


def forward_call(owner, coord, lens, x, gains, turns, parts):
    def made(rows, columns, kind):
        return jax.ShapeDtypeStruct((rows, columns), kind)

    return pl.pallas_call(
        forward_kernel,
        out_shape=(
            made(LEFT_ROWS, D, jnp.bfloat16),
            made(PAIR_ROWS, D, jnp.bfloat16),
            made(TOKENS, D, jnp.bfloat16),
            made(TOKENS, D, jnp.bfloat16),
            made(PAIR_ROWS, D, jnp.float32),
            made(PAIR_ROWS, FF, jnp.float32),
            made(PAIR_ROWS, FF, jnp.float32),
            made(PAIR_ROWS, D, jnp.float32),
            made(PAIR_ROWS, D, jnp.bfloat16),
        ),
        in_specs=smem(3) + vmem(6) + anywhere(18),
        out_specs=tuple(vmem(9)),
        scratch_shapes=[
            pltpu.VMEM((NBLK, D, BC), jnp.bfloat16),
            pltpu.SemaphoreType.DMA,
        ],
        compiler_params=pltpu.CompilerParams(vmem_limit_bytes=VMEM_LIMIT),
        name="layer_forward",
    )(owner, coord, lens, x, gains, *turns, *parts)


def unpack(ext):
    stat = high(ext[:, D:EXT])
    top = (stat[:, 0:1] + stat[:, 1:2]) + stat[:, 2:3]
    total = (stat[:, 3:4] + stat[:, 4:5]) + stat[:, 5:6]
    return top, total, high(ext[:, :D])


def pack_stat(top, total):
    lane = iota((top.shape[0], 128), 1)
    out = jnp.zeros((top.shape[0], 128), jnp.float32)
    for first, value in ((0, top), (3, total)):
        for i in range(3):
            piece = high(low(value))
            out = jnp.where(lane == first + i, piece, out)
            value = value - piece
    return low(out)


def merge(items):
    top = items[0][0]
    for item in items[1:]:
        top = jnp.maximum(top, item[0])
    total = 0.0
    mixed = 0.0
    for item_top, item_total, item_mixed in items:
        factor = jnp.exp(item_top - top)
        total = total + item_total * factor
        mixed = mixed + item_mixed * factor
    return top, total, mixed


def merge_kernel(number, *refs):
    top, total, mixed = merge([unpack(ref[...]) for ref in refs[:number]])
    mixed = low(mixed)
    stat = pack_stat(top, total)
    outs = refs[number:]
    rows = outs[0].shape[0]
    for n, out in enumerate(outs):
        out[:, :D] = mixed[n * rows : (n + 1) * rows]
        out[:, D:EXT] = stat[n * rows : (n + 1) * rows]


def merge_call(parts, pieces=1):
    rows = 4 * PAIR_ROWS
    made = jax.ShapeDtypeStruct((rows // pieces, EXT), jnp.bfloat16)
    return pl.pallas_call(
        functools.partial(merge_kernel, len(parts)),
        grid=(1,),
        out_shape=(made,) * pieces,
        in_specs=[pl.BlockSpec((rows, EXT), lambda i, at=at: (at, 0)) for _, at in parts],
        out_specs=(pl.BlockSpec(made.shape, lambda i: (0, 0)),) * pieces,
        compiler_params=pltpu.CompilerParams(vmem_limit_bytes=VMEM_LIMIT),
        cost_estimate=pl.CostEstimate(
            flops=8 * rows * D, bytes_accessed=4 * rows * EXT, transcendentals=rows
        ),
        name="merge_parts",
    )(*[array for array, _ in parts])


def head_kernel(real, rows, head, ext, kept, stat):
    logits = dot_nt(rows[...], head[...])
    col = iota(logits.shape, 1)
    logits = jnp.where(col < real, logits, MASKED)
    top = jnp.max(logits, axis=-1, keepdims=True)
    e = jnp.exp(logits - top)
    total = jnp.sum(e, axis=-1, keepdims=True)
    e_low = low(e)
    kept[...] = e_low
    ext[:, :D] = low(dot_nn(e_low, head[...]))
    ext[:, D:EXT] = pack_stat(top, total)
    stat[...] = jnp.broadcast_to(top, stat.shape)


def head_call(rows, head, real):
    number, wide = rows.shape[0], head.shape[0]
    return pl.pallas_call(
        functools.partial(head_kernel, real),
        grid=(number // 256,),
        out_shape=(
            jax.ShapeDtypeStruct((number, EXT), jnp.bfloat16),
            jax.ShapeDtypeStruct((number, wide), jnp.bfloat16),
            jax.ShapeDtypeStruct((number, 128), jnp.float32),
        ),
        in_specs=[
            pl.BlockSpec((256, D), lambda i: (i, 0)),
            pl.BlockSpec((wide, D), lambda i: (0, 0)),
        ],
        out_specs=(
            pl.BlockSpec((256, EXT), lambda i: (i, 0)),
            pl.BlockSpec((256, wide), lambda i: (i, 0)),
            pl.BlockSpec((256, 128), lambda i: (i, 0)),
        ),
        compiler_params=pltpu.CompilerParams(vmem_limit_bytes=VMEM_LIMIT),
        cost_estimate=pl.CostEstimate(
            flops=4 * number * wide * D, bytes_accessed=2 * number * wide, transcendentals=number * wide
        ),
        name="head_forward",
    )(rows, head)


def head_grad_kernel(steps, rows_a, rows_b, kept_a, kept_b, stat_a, stat_b, info, out):
    def add(rows, kept, stat):
        weight = info[:, 0:1]
        factor = weight * jnp.exp(stat[:, 0:1] - info[:, 1:2])
        col = iota(kept.shape, 1)
        hit = col == info[:, 2:3].astype(jnp.int32)
        grad = low(jnp.where(hit, weight, 0.0) - high(kept[...]) * factor)
        return dot_tn(grad, rows[...])

    i = pl.program_id(0)

    @pl.when(i == 0)
    def _():
        out[...] = add(rows_a, kept_a, stat_a)

    @pl.when((i > 0) & (i < steps))
    def _():
        out[...] += add(rows_a, kept_a, stat_a)

    @pl.when(i >= steps)
    def _():
        out[...] += add(rows_b, kept_b, stat_b)


def head_grad_call(rows, kept, stat, info):
    number, wide = kept[0].shape
    steps = number // 256

    def pair(columns):
        return [
            pl.BlockSpec((256, columns), lambda i: (jnp.minimum(i, steps - 1), 0)),
            pl.BlockSpec((256, columns), lambda i: (jnp.maximum(i - steps, 0), 0)),
        ]

    return pl.pallas_call(
        functools.partial(head_grad_kernel, steps),
        grid=(2 * steps,),
        out_shape=jax.ShapeDtypeStruct((wide, D), jnp.float32),
        in_specs=pair(D) + pair(wide) + pair(128) + [pl.BlockSpec((256, 128), lambda i: (i, 0))],
        out_specs=pl.BlockSpec((wide, D), lambda i: (0, 0)),
        compiler_params=pltpu.CompilerParams(vmem_limit_bytes=VMEM_LIMIT),
        cost_estimate=pl.CostEstimate(
            flops=4 * number * wide * D, bytes_accessed=4 * number * wide, transcendentals=number
        ),
        name="head_grad",
    )(*rows, *kept, *stat, info)


def backward_kernel(owner, coord, lens, refs, x, gains, cos_q, sin_q, cos_k, sin_k, *rest):
    q, k, v, h1, gate, up, h2, c = rest[:8]
    truth, wanted, u0, u1, u2, u3 = rest[8:14]
    parts = rest[14:32]
    act, dx_out, gain_out, info_out, loss_out = rest[32:37]
    held, sem = rest[37:]
    start_weights(coord, parts, held, sem)
    valid, chosen = masks(lens)
    select = jnp.where(chosen, 1.0, 0.0).astype(jnp.bfloat16)
    top, total, mixed = merge([unpack(part[...]) for part in (u0, u1, u2, u3)])
    norm = top + jnp.log(total)
    target = high(truth[...])
    picked = jnp.sum(high(c[...]) * target, axis=-1, keepdims=True)
    scored = wanted[:, 0:1]
    terms = (picked - norm) * scored
    seq = iota((PAIR_ROWS, 1), 0) >> 4
    logp = [jnp.sum(jnp.where(seq == n, terms, 0.0), axis=0, keepdims=True) for n in range(2 * MB)]
    weight = jnp.zeros((PAIR_ROWS, 1), jnp.float32)
    loss = jnp.zeros((1, 1), jnp.float32)
    for n in range(MB):
        margin = DPO_BETA * ((logp[2 * n] - refs[2 * n]) - (logp[2 * n + 1] - refs[2 * n + 1]))
        loss = loss + jnp.maximum(-margin, 0.0) + jnp.log1p(jnp.exp(-jnp.abs(margin)))
        slope = -DPO_BETA * jax.nn.sigmoid(-margin)
        weight = jnp.where(seq == 2 * n, slope, jnp.where(seq == 2 * n + 1, -slope, weight))
    weight = weight * scored
    loss_out[...] = jnp.broadcast_to(loss, loss_out.shape)
    lane = iota((PAIR_ROWS, 128), 1)
    info_out[...] = jnp.where(
        lane == 0, weight, jnp.where(lane == 1, norm, jnp.where(lane == 2, wanted[:, 1:2], 0.0))
    )
    grad_c = weight * (target - mixed / total)
    d2, gain_top = rms_back(h2[...], gains[2:3, :], grad_c)
    gain_out[2:3, :] = gain_top
    d2_low = low(d2)
    act[AT_DH:RIGHT_ROWS] = d2_low
    wait_weights(held, sem)
    grad_b = jnp.zeros((PAIR_ROWS, D), jnp.float32)
    for r in range(FF // D):
        grad_mix = dot_nt(d2_low[:, :BC], held[owner[24 + 2 * r]]) + dot_nt(
            d2_low[:, BC:], held[owner[25 + 2 * r]]
        )
        at = slice(r * D, (r + 1) * D)
        gate_pre = gate[:, at]
        sig = jax.nn.sigmoid(gate_pre)
        d_gate = low(grad_mix * up[:, at] * sig * (1.0 + gate_pre * (1.0 - sig)))
        d_up = low(grad_mix * gate_pre * sig)
        act[AT_DGATE + r * PAIR_ROWS : AT_DGATE + (r + 1) * PAIR_ROWS] = d_gate
        act[AT_DUP + r * PAIR_ROWS : AT_DUP + (r + 1) * PAIR_ROWS] = d_up
        for j in range(2):
            cut = slice(j * BC, (j + 1) * BC)
            grad_b = grad_b + dot_nt(d_gate[:, cut], held[owner[8 + 2 * r + j]])
            grad_b = grad_b + dot_nt(d_up[:, cut], held[owner[16 + 2 * r + j]])
    back, gain_mid = rms_back(h1[...], gains[1:2, :], grad_b)
    gain_out[1:2, :] = gain_mid
    d1 = d2 + back
    d1_low = low(d1)
    act[AT_DO:AT_DGATE] = d1_low
    d_att = low(
        dot_nt(d1_low[:, :BC], held[owner[6]]) + dot_nt(d1_low[:, BC:], held[owner[7]])
    )
    lane_k = iota((TOKENS, 128), 1)
    zero_k = jnp.zeros((TOKENS, 128), jnp.bfloat16)
    zero_q = jnp.zeros((PAIR_ROWS, 128), jnp.bfloat16)
    root = 1.0 / math.sqrt(HDIM)
    for p in range(HEADS // 2):
        at = slice(p * 128, (p + 1) * 128)
        d_q = jnp.zeros((PAIR_ROWS, 128), jnp.float32)
        d_k = jnp.zeros((TOKENS, 128), jnp.float32)
        d_v = jnp.zeros((TOKENS, 128), jnp.float32)
        for h in range(2):
            mine_k = (lane_k >> 6) == h
            mine_q = (lane >> 6) == h
            k_one = jnp.where(mine_k, k[:, at], zero_k)
            q_one = jnp.where(mine_q, q[:, at], zero_q)
            do_one = jnp.where(mine_q, d_att[:, at], zero_q)
            s = dot_nt(q_one, k_one) * root
            s = jnp.where(valid, s, MASKED)
            e = jnp.exp(s - jnp.max(s, axis=-1, keepdims=True))
            prob = e / jnp.sum(e, axis=-1, keepdims=True)
            d_p = dot_nt(do_one, v[:, at])
            d_s = low(prob * (d_p - jnp.sum(prob * d_p, axis=-1, keepdims=True)))
            d_q = d_q + dot_nn(d_s, k_one)
            d_k = d_k + dot_tn(d_s, q_one)
            d_v = d_v + dot_tn(low(prob), do_one)
        act[AT_DQ:AT_DO, at] = low(turn(d_q * root, cos_q[...], sin_q[...], -1.0))
        act[AT_DK:AT_DV, at] = low(turn(d_k * root, cos_k[...], sin_k[...], -1.0))
        act[AT_DV:AT_DQ, at] = low(d_v)
    d_q_all = low(dot_tn(select, act[AT_DQ:AT_DO]))
    grad_a = jnp.zeros((TOKENS, D), jnp.float32)
    for j in range(2):
        cut = slice(j * BC, (j + 1) * BC)
        grad_a = grad_a + dot_nt(d_q_all[:, cut], held[owner[j]])
        grad_a = grad_a + dot_nt(act[AT_DK:AT_DV, cut], held[owner[2 + j]])
        grad_a = grad_a + dot_nt(act[AT_DV:AT_DQ, cut], held[owner[4 + j]])
    back_in, gain_in = rms_back(high(x[...]), gains[0:1, :], grad_a)
    gain_out[0:1, :] = gain_in
    rest_low = low(d1 - high(d1_low))
    dx_out[...] = low(back_in + dot_tn(select, d1_low) + dot_tn(select, rest_low))


def backward_call(owner, coord, lens, refs, x, gains, turns, saved, truth, wanted, parts_u, parts):
    return pl.pallas_call(
        backward_kernel,
        out_shape=(
            jax.ShapeDtypeStruct((RIGHT_ROWS, D), jnp.bfloat16),
            jax.ShapeDtypeStruct((TOKENS, D), jnp.bfloat16),
            jax.ShapeDtypeStruct((3, D), jnp.float32),
            jax.ShapeDtypeStruct((PAIR_ROWS, 128), jnp.float32),
            jax.ShapeDtypeStruct((1, 128), jnp.float32),
        ),
        in_specs=smem(4) + vmem(6 + 8 + 2 + 4) + anywhere(18),
        out_specs=tuple(vmem(5)),
        scratch_shapes=[
            pltpu.VMEM((NBLK, D, BC), jnp.bfloat16),
            pltpu.SemaphoreType.DMA,
        ],
        compiler_params=pltpu.CompilerParams(vmem_limit_bytes=VMEM_LIMIT),
        name="layer_backward",
    )(owner, coord, lens, refs, x, gains, *turns, *saved, truth, wanted, *parts_u, *parts)


def transpose_kernel(coord, mine, theirs, picked, tokens, turned_a, turned_b):
    near_row = pl.multiple_of(192 * (2 * coord[2] + coord[3]), 64)
    far_row = pl.multiple_of(192 * (2 * (1 - coord[2]) + coord[3]), 64)
    for n in range(LEFT_KINDS):
        at = slice(AT_AP + n * PAIR_ROWS, AT_AP + (n + 1) * PAIR_ROWS)
        turned_a[...] = jnp.concatenate([mine[at], theirs[at]], axis=0).T
        picked[n, :192] = turned_a[pl.ds(near_row, 192), :]
        picked[n, 192:] = turned_a[pl.ds(far_row, 192), :]
    turned_b[:, :TOKENS] = mine[AT_A:AT_AP].T
    turned_b[:, TOKENS:] = theirs[AT_A:AT_AP].T
    tokens[:192] = turned_b[pl.ds(near_row, 192), :]
    tokens[192:] = turned_b[pl.ds(far_row, 192), :]


def transpose_call(coord, mine, theirs):
    return pl.pallas_call(
        transpose_kernel,
        out_shape=(
            jax.ShapeDtypeStruct((LEFT_KINDS, 384, 2 * PAIR_ROWS), jnp.bfloat16),
            jax.ShapeDtypeStruct((384, 2 * TOKENS), jnp.bfloat16),
        ),
        in_specs=smem(1) + vmem(2),
        out_specs=tuple(vmem(2)),
        scratch_shapes=[
            pltpu.VMEM((D, 2 * PAIR_ROWS), jnp.bfloat16),
            pltpu.VMEM((D, 2 * TOKENS), jnp.bfloat16),
        ],
        compiler_params=pltpu.CompilerParams(vmem_limit_bytes=VMEM_LIMIT),
        cost_estimate=pl.CostEstimate(
            flops=0, bytes_accessed=8 * LEFT_ROWS * D, transcendentals=0
        ),
        name="left_transposed",
    )(coord, mine, theirs)


def weight_grad_kernel(block_of, x_at, y_at, coord, picked, tokens, mine, theirs, *rest):
    outs = rest[:-3]
    near_held, far_held, sem = rest[-3:]
    first = coord[3] == 0
    for group, (k, x_flip) in enumerate((k, x_flip) for k in range(4) for x_flip in range(2)):
        x = coord[1] + x_flip * (1 - 2 * coord[1])

        def step(n, carry):
            z = n if k != 2 else (coord[0] + 4 - n) & 3
            slot = 8 * z + 4 * x + k
            block = block_of[slot]
            cut = pl.ds(pl.multiple_of((block & 1) * BC, 128), BC)
            y_row = pl.multiple_of(y_at[slot], 64)

            def put(left, rows):
                right = jnp.concatenate(
                    [mine[pl.ds(y_row, rows), cut], theirs[pl.ds(y_row, rows), cut]], axis=0
                )
                grad = low(dot_nn(left, right))
                near_held[group, n] = grad[:192]
                far_held[group, n] = grad[192:]

            wide = (block >= 2) & (block < 6)

            @pl.when(wide)
            def _():
                put(tokens[...], TOKENS)

            @pl.when(jnp.logical_not(wide))
            def _():
                put(picked[x_at[slot]], PAIR_ROWS)

            return carry

        lax.fori_loop(0, 4, step, 0)

        def send(held, rel):
            if k == 3:
                target = outs[8].at[:, rel]
            elif k == 2:
                target = outs[4 + rel]
            else:
                target = outs[rel].at[:, k]
            pltpu.make_async_copy(held.at[group], target, sem).start()

        if x_flip == 0:
            send(near_held, 0)
            side = far_held
        else:
            send(far_held, 3)
            side = near_held

        @pl.when(first == (x_flip == 1))
        def _():
            send(side, 1)

        @pl.when(first == (x_flip == 0))
        def _():
            send(side, 2)

    pltpu.make_async_copy(near_held, near_held, sem).wait()
    pltpu.make_async_copy(far_held, far_held, sem).wait()


def weight_grad_call(*args):
    shapes = [(4, 2)] * 4 + [(4,)] * 4 + [(4, 4)]
    made = [jax.ShapeDtypeStruct(shape + (192, BC), jnp.bfloat16) for shape in shapes]
    held = pltpu.VMEM((8, 4, 192, BC), jnp.bfloat16)
    return pl.pallas_call(
        weight_grad_kernel,
        out_shape=tuple(made),
        in_specs=smem(4) + vmem(4),
        out_specs=tuple(anywhere(len(made))),
        scratch_shapes=[held, held, pltpu.SemaphoreType.DMA],
        compiler_params=pltpu.CompilerParams(vmem_limit_bytes=VMEM_LIMIT),
        name="weight_grads",
    )(*args)


def shampoo_kernel(coord, *refs):
    own, by_y, by_core, by_both, lstat, rstat, lroot, rroot, blk = refs[:9]
    new_b, grad_out, new_l, new_r, whole = refs[-5:]
    y, core = coord[2], coord[3]
    for piece, y_at, core_at in (
        (own, y, core),
        (by_y, 1 - y, core),
        (by_core, y, 1 - core),
        (by_both, 1 - y, 1 - core),
    ):
        row = pl.multiple_of(192 * (2 * y_at + core_at), 64)
        whole[pl.ds(row, 192), :] = piece[0]
    grad_out[0] = high(own[0])
    grad = whole[...]
    new_l[0] = STAT_DECAY * lstat[0] + (1.0 - STAT_DECAY) * dot_nt(grad, grad)
    new_r[0] = STAT_DECAY * rstat[0] + (1.0 - STAT_DECAY) * dot_tn(grad, grad)
    turned = dot_nn(low(lroot[0]), grad)
    new_b[0] = blk[0] - SHAMPOO_RATE * dot_nn(low(turned), low(rroot[0]))


def shampoo_call(start, coord, pieces, lstat, rstat, lroot, rroot, blk, so_far):
    def one(rows, columns):
        return pl.BlockSpec((1, rows, columns), lambda i, coord: (start + i, 0, 0))

    slots = pieces[0].shape[0]
    in_specs = (
        [pl.BlockSpec((1, 192, BC), lambda i, coord: (i, 0, 0))] * 4
        + [
            one(D, D),
            one(BC, BC),
            pl.BlockSpec((1, 192, D), lambda i, coord: (start + i, 2 * coord[2] + coord[3], 0)),
            one(BC, BC),
            one(192, BC),
        ]
        + anywhere(len(so_far))
    )
    return pl.pallas_call(
        shampoo_kernel,
        grid_spec=pltpu.PrefetchScalarGridSpec(
            num_scalar_prefetch=1,
            grid=(slots,),
            in_specs=in_specs,
            out_specs=(one(192, BC), one(192, BC), one(D, D), one(BC, BC)),
            scratch_shapes=[pltpu.VMEM((D, BC), jnp.bfloat16)],
        ),
        out_shape=(
            jax.ShapeDtypeStruct(blk.shape, jnp.float32),
            jax.ShapeDtypeStruct(blk.shape, jnp.float32),
            jax.ShapeDtypeStruct(lstat.shape, jnp.float32),
            jax.ShapeDtypeStruct(rstat.shape, jnp.float32),
        ),
        input_output_aliases={10 + n: n for n in range(len(so_far))},
        compiler_params=pltpu.CompilerParams(vmem_limit_bytes=VMEM_LIMIT),
        cost_estimate=pl.CostEstimate(
            flops=4 * slots * D * D * BC,
            bytes_accessed=8 * slots * 1024 * 1024,
            transcendentals=0,
        ),
        name="shampoo",
    )(coord, *pieces, lstat, rstat, lroot, rroot, blk, *so_far)


def adam_kernel(rate, grad, w, m, v, *rest):
    new_w, new_m, new_v = rest[-3:]
    new_w[0], new_m[0], new_v[0] = adam_step(w[0], grad[...], m[0], v[0], rate)


def adam_call(table, rate, grad, w, m, v, so_far):
    rows = w.shape[1]
    block = next(n for n in (200, 40, 8) if rows % n == 0)
    spec = pl.BlockSpec((1, block, D), lambda j: (table, j, 0))
    return pl.pallas_call(
        functools.partial(adam_kernel, rate),
        grid=(rows // block,),
        out_shape=(jax.ShapeDtypeStruct(w.shape, jnp.float32),) * 3,
        in_specs=[pl.BlockSpec((block, D), lambda j: (j, 0)), spec, spec, spec]
        + anywhere(len(so_far)),
        out_specs=(spec,) * 3,
        input_output_aliases={4 + n: n for n in range(len(so_far))},
        compiler_params=pltpu.CompilerParams(vmem_limit_bytes=VMEM_LIMIT),
        cost_estimate=pl.CostEstimate(
            flops=10 * rows * D, bytes_accessed=28 * rows * D, transcendentals=rows * D
        ),
        name="adam",
    )(grad, w, m, v, *so_far)


def block_rows():
    x_at, y_at = [], []
    for b in range(NBLK):
        if b < 2:
            x_at.append(0), y_at.append(AT_DQ)
        elif b < 4:
            x_at.append(0), y_at.append(AT_DK)
        elif b < 6:
            x_at.append(0), y_at.append(AT_DV)
        elif b < 8:
            x_at.append(1), y_at.append(AT_DO)
        elif b < 16:
            x_at.append(2), y_at.append(AT_DGATE + (b - 8) // 2 * PAIR_ROWS)
        elif b < 24:
            x_at.append(2), y_at.append(AT_DUP + (b - 16) // 2 * PAIR_ROWS)
        else:
            x_at.append(3 + (b - 24) // 2), y_at.append(AT_DH)
    return jnp.array(x_at, jnp.int32), jnp.array(y_at, jnp.int32)


def per_core(
    token_ids,
    lengths,
    comp_mask,
    ref_logp,
    owner,
    blocks,
    left_stat,
    right_stat,
    left_root,
    right_root,
    tables,
    table_moment,
    table_second,
    gains,
    gain_moment,
    gain_second,
):
    zi, xi, yi, ci = (lax.axis_index(name) for name in AXES)
    coord = jnp.stack([zi, xi, yi, ci]).astype(jnp.int32)
    vocab_index = 2 * yi + ci
    shard = vocab_index * 8 + 2 * zi + xi
    table_rows = tables.shape[1]
    vocab = table_rows * 32
    seqs = 2 * MB
    shares = blocks.astype(jnp.bfloat16)
    with jax.named_scope("weights_last"):
        one, two = hop_one(shares[3]), hop_two(shares[3])
        last = jnp.stack([shares[3], one, two, hop_two(one)])
    with jax.named_scope("weights_third"):
        line3 = all_round(shares[2])
    with jax.named_scope("weights_pair"):
        line = lax.all_gather(shares[:2], "z")
    first_pair = vocab_index * MB
    ids = lax.dynamic_slice_in_dim(token_ids, first_pair, MB, 0).reshape(seqs, SLOT)
    lens = lax.dynamic_slice_in_dim(lengths, first_pair, MB, 0).reshape(seqs)
    wanted = lax.dynamic_slice_in_dim(comp_mask, first_pair, MB, 0).reshape(PAIR_ROWS)
    refs = lax.dynamic_slice_in_dim(ref_logp, first_pair, MB, 0).reshape(seqs)
    places = jnp.arange(SLOT)
    pos = (lens[:, None] - 1 - CMP + jnp.arange(CMP)[None, :]).astype(jnp.int32)
    targets = jnp.sum(
        jnp.where(places[None, None, :] == (pos + 1)[:, :, None], ids[:, None, :], 0), axis=-1
    ).reshape(PAIR_ROWS)
    asked = jnp.concatenate([ids.reshape(TOKENS), targets + vocab])
    used = jnp.concatenate(
        [(places[None, :] < lens[:, None]).reshape(TOKENS), jnp.ones((PAIR_ROWS,), bool)]
    )
    number = jnp.where(asked >= vocab, asked - vocab, asked)
    holder = number // table_rows
    local_row = number - holder * table_rows + jnp.where(asked >= vocab, table_rows, 0)
    total = asked.shape[0]
    earlier = jnp.arange(total)[None, :] < jnp.arange(total)[:, None]
    same = (asked[:, None] == asked[None, :]) & used[:, None] & used[None, :]
    first = used & jnp.logical_not(jnp.any(same & earlier, axis=1))
    rank = jnp.sum(
        ((holder[:, None] == holder[None, :]) & earlier & first[None, :]).astype(jnp.int32), axis=1
    )
    most = jnp.where(jnp.arange(total) < TOKENS, CAP_BACK, CAP)
    spill = jnp.any(first & (rank >= most))
    seat_first = jnp.where(first & (rank < CAP), holder * CAP + rank, -1)
    seat = jnp.sum(jnp.where(same & first[None, :], seat_first[None, :] + 1, 0), axis=1) - 1
    seats = jnp.arange(32 * CAP)
    request = jnp.sum(
        jnp.where(seat_first[:, None] == seats[None, :], local_row[:, None], 0), axis=0
    )
    message = jnp.concatenate(
        [
            request.reshape(32, CAP),
            jnp.broadcast_to(spill.astype(jnp.int32), (32, MSG - CAP)),
        ],
        axis=1,
    )
    message = lax.all_to_all(message, SHARD_AXES, 0, 0, tiled=True)
    line3, last, message = together(line3, last, message)
    any_spill = jnp.max(message[:, MSG - 1]) > 0
    asked_rows = message[:, :CAP].reshape(32 * CAP)
    table_low = tables.astype(jnp.bfloat16).reshape(2 * table_rows, D)
    give = (asked_rows[:, None] == jnp.arange(2 * table_rows)[None, :]).astype(jnp.bfloat16)
    given = low(dot_nn(give, table_low))
    with jax.named_scope("weights_third"):
        one3, two3 = hop_one(line3), hop_two(line3)
    one3, two3, given, line, last = together(one3, two3, given, line, last)
    got = lax.all_to_all(given, SHARD_AXES, 0, 0, tiled=True)
    with jax.named_scope("weights_last"):
        last = lax.all_gather(last, "z")
    with jax.named_scope("weights_third"):
        third = [line3, one3, two3, hop_two(one3)]
    with jax.named_scope("weights_pair"):
        one, two = hop_one(line), hop_two(line)
    early = [hop_core(part) for part in third[:3] + [line]]
    one, two, third[3], *early = together(one, two, third[3], *early)
    with jax.named_scope("weights_pair"):
        pair = [line, one, two, hop_two(one)]
    place = (seat[:, None] == seats[None, :]).astype(jnp.bfloat16)
    rows = low(dot_nn(place, got))
    x, truth = rows[:TOKENS], rows[TOKENS:]
    inv_freq = ROPE_BASE ** (-jnp.arange(HDIM // 2).astype(jnp.float32) * 2.0 / HDIM)
    phase = places.astype(jnp.float32)[:, None] * inv_freq[None, :]
    phase_pick = pos.reshape(PAIR_ROWS).astype(jnp.float32)[:, None] * inv_freq[None, :]

    def turning(angle, repeat):
        cosine, sine = jnp.cos(angle), jnp.sin(angle)
        return (
            jnp.tile(jnp.concatenate([cosine] * 4, axis=1), (repeat, 1)),
            jnp.tile(jnp.concatenate([-sine, sine, -sine, sine], axis=1), (repeat, 1)),
        )

    turns = turning(phase_pick, 1) + turning(phase, seqs)
    middle = [hop_core(part) for part in (one, two, third[3])]
    last, *middle = together(last, *middle, x, truth, *turns)[:4]
    parts = []
    early += middle
    for n, part in enumerate(pair + third + [last]):
        place_of_early = {0: 3, 4: 0, 5: 1, 6: 2, 1: 4, 2: 5, 7: 6}.get(n)
        parts.append(part)
        parts.append(hop_core(part) if place_of_early is None else early[place_of_early])
    left, *saved = forward_call(owner, coord, lens, x, gains, turns, parts)
    plane, _ = spread(saved[-1])
    plane = plane.reshape(-1, D)
    other = hop_core(plane)
    left_t = transpose_call(coord, left, hop_core(left))
    wide = -(-table_rows // 128) * 128
    head_low = jnp.pad(table_low[table_rows:], ((0, wide - table_rows), (0, 0)))
    ext_other, kept_other, stat_other = head_call(other, head_low, table_rows)
    ext_hop = hop_core(ext_other)
    ext_own, kept_own, stat_own = head_call(plane, head_low, table_rows)
    both = merge_call([(ext_own, 3), (ext_hop, 3)])[0]
    two = merge_call([(ext_own, 2), (ext_hop, 2)])[0]
    one = merge_call([(ext_own, 1), (ext_hop, 1), (hop_two(both), 0)])[0]
    pieces = merge_call([(ext_own, 0), (ext_hop, 0), (hop_one(one), 0), (hop_two(two), 0)], 4)
    pieces = lax.optimization_barrier(tuple(pieces) + tuple(left_t))[:4]
    parts_u = [pieces[0]] + [ring(pieces[step], -step) for step in range(1, 4)]
    marks = jnp.stack([wanted.astype(jnp.float32), targets.astype(jnp.float32)], axis=1)
    marks = jnp.pad(marks, ((0, 0), (0, 126)))
    act, dx, gain_part, info, loss_part = backward_call(
        owner, coord, lens, refs, x, gains, turns, saved, truth, marks, parts_u, parts
    )
    inverse = jnp.sum(
        jnp.where(
            owner[None, :] == jnp.arange(NBLK)[:, None], jnp.arange(NBLK, dtype=jnp.int32)[None, :], 0
        ),
        axis=1,
    )
    x_at, y_at = block_rows()
    chosen = (inverse[:, None] == jnp.arange(NBLK)[None, :]).astype(jnp.int32)
    grad_args = (
        inverse,
        jnp.sum(chosen * x_at[None, :], axis=1),
        jnp.sum(chosen * y_at[None, :], axis=1),
        coord,
        *left_t,
        act,
        hop_core(act),
    )

    def plus(*values):
        return low(sum(high(value) for value in values))

    grads = weight_grad_call(*grad_args)
    info, gain_part, loss_part, dx, *grads = together(info, gain_part, loss_part, dx, *grads)
    own, one, two, both = grads[:4]
    own3, one3, two3, both3, ends = grads[4:]
    with jax.named_scope("grads_pair"):
        one = plus(one, hop_two(both))
    with jax.named_scope("grads_last"):
        last = lax.psum_scatter(
            ends.reshape(16, 192, BC), "z", scatter_dimension=0, tiled=True
        )
    back = place[:TOKENS].reshape(TOKENS, 32, CAP)[:, :, :CAP_BACK].reshape(TOKENS, 32 * CAP_BACK)
    sent = low(dot_tn(back, dx))
    told = info[:, :3].reshape(-1)
    known = told.shape[0]
    told = jnp.concatenate([told, gain_part.reshape(-1), loss_part[0]])
    told = jnp.broadcast_to(told[None], (32, told.shape[0]))
    heard = lax.all_to_all(told, AXES, 0, 0, tiled=True)
    with jax.named_scope("grads_pair"):
        two = hop_two(two)
    one, two, both3, sent, heard = together(one, two, both3, sent, heard)
    with jax.named_scope("grads_pair"):
        line = plus(own, hop_one(one), two).reshape(8, 192, BC)
    with jax.named_scope("grads_third"):
        one3 = plus(one3, hop_two(both3))
    back_rows = lax.all_to_all(sent, SHARD_AXES, 0, 0, tiled=True)
    summed = jnp.sum(heard[:, known:], axis=0)
    sources = []
    for other_core in range(2):
        for rel in range(4):
            for back in range(4):
                sources.append(
                    flat_of((zi + 4 - back) % 4, *place_of((zi, xi, yi, ci), other_core, rel))
                )
    sources = jnp.stack(sources)
    infos = jnp.sum(
        jnp.where(
            (sources[:, None] == jnp.arange(32)[None, :])[:, :, None],
            heard[None, :, :known],
            0.0,
        ),
        axis=1,
    ).reshape(-1, 3)
    infos = jnp.concatenate(
        [infos[:, :2], infos[:, 2:3] - (shard * table_rows).astype(jnp.float32)], axis=1
    )
    infos = jnp.pad(infos, ((0, 0), (0, 125)))
    grad_head = head_grad_call(
        (plane, other), (kept_own, kept_other), (stat_own, stat_other), infos
    )
    adam = adam_call(1, 0.02, grad_head, tables, table_moment, table_second, ())
    line, one3, two3, last, *adam = together(line, one3, two3, last, *adam)
    with jax.named_scope("grads_pair"):
        pair = lax.psum_scatter(line, "z", scatter_dimension=0, tiled=True)
    with jax.named_scope("grads_third"):
        one3, two3 = hop_one(one3), hop_two(two3)
        line3 = [plus(own3[n], one3[n], two3[n]) for n in range(4)]
    with jax.named_scope("grads_last"):
        one, two = plus(last[1], hop_two(last[3])), hop_two(last[2])
    back_at = message[:, :CAP_BACK].reshape(32 * CAP_BACK)
    take_back = (back_at[None, :] == jnp.arange(table_rows)[:, None]).astype(jnp.bfloat16)
    grad_embed = dot_nn(take_back, back_rows)
    new_tables, new_table_moment, new_table_second = adam_call(
        0, 0.3, grad_embed, tables, table_moment, table_second, adam
    )
    new_gains, new_gain_moment, new_gain_second = adam_step(
        gains, summed[: 3 * D].reshape(3, D), gain_moment, gain_second, GAIN_RATE
    )
    loss_sum = summed[3 * D]
    one, two, new_tables, new_gains, new_gain_moment, new_gain_second, *line3 = together(
        one, two, new_tables, new_gains, new_gain_moment, new_gain_second, *line3
    )
    pair_y = hop_y(pair)
    with jax.named_scope("grads_third"):
        around = [ring(line3[step], -step) for step in range(1, 4)]
        third = plus(after(line3[0], pair_y), *around)
    with jax.named_scope("grads_last"):
        last = plus(last[0], hop_one(one), two)

    rights = (left_stat, right_stat, left_root, right_root, blocks)
    late = jnp.stack([third, last])
    late_y = hop_y(late)
    results = shampoo_call(
        0, coord, (pair, pair_y, hop_core(pair), hop_core(pair_y)), *rights, ()
    )
    late_y, *results = together(late_y, *results)
    new_blocks, block_grads, new_left, new_right = shampoo_call(
        2, coord, (late, late_y, hop_core(late), hop_core(late_y)), *rights, results
    )
    quick = (
        new_blocks,
        block_grads,
        new_left,
        new_right,
        new_tables,
        new_table_moment,
        new_table_second,
        new_gains,
        new_gain_moment,
        new_gain_second,
        loss_sum,
    )
    whole = (
        token_ids,
        lengths,
        comp_mask,
        ref_logp,
        owner,
        blocks,
        left_stat,
        right_stat,
        left_root,
        right_root,
        tables,
        table_moment,
        table_second,
        gains,
        gain_moment,
        gain_second,
    )

    def slow(state):
        outs = list(per_device(("z", "x"), ("y", "core"), *whole))
        outs[1] = with_layout_constraint(outs[1], Layout((0, 1, 2)))
        return jnp.zeros((), bool), tuple(outs)

    return lax.while_loop(lambda state: state[0], slow, (any_spill, quick))[1]


def solution(mesh):
    tuned = mesh.shape["dp"] == 8 and mesh.shape["vocab"] == 4
    if tuned:
        dp, vocab = ("z", "x"), ("y", "core")
        where = Mesh(mesh.devices.reshape(4, 2, 2, 2), AXES)
        body = per_core
    else:
        dp, vocab = ("dp",), ("vocab",)
        where = mesh
        body = functools.partial(per_device, ("dp",), ("vocab",))
    placed = (
        P(dp, None, None),
        P(dp, None),
        P(dp, None, None),
        P(dp, None),
        P(),
        P(dp, vocab, None),
        P(dp, None, None),
        P(dp, None, None),
        P(dp, None, None),
        P(dp, None, None),
        P(None, vocab + dp, None),
        P(None, vocab + dp, None),
        P(None, vocab + dp, None),
        P(),
        P(),
        P(),
    )
    return jax.shard_map(
        body,
        mesh=where,
        in_specs=placed,
        out_specs=(
            P(dp, vocab, None),
            P(dp, vocab, None),
            P(dp, None, None),
            P(dp, None, None),
            P(None, vocab + dp, None),
            P(None, vocab + dp, None),
            P(None, vocab + dp, None),
            P(),
            P(),
            P(),
            P(),
        ),
        check_vma=False,
    )
```

```python
import functools
import math

import jax
import jax.numpy as jnp
from jax import lax
from jax.experimental import pallas as pl
from jax.experimental.layout import Layout, with_layout_constraint
from jax.experimental.pallas import tpu as pltpu
from jax.sharding import Mesh
from jax.sharding import PartitionSpec as P

D = 768
HEADS = 12
HDIM = 64
FF = 3072
SLOT = 64
MB = 2
CMP = 16
STEP = 10
BC = 384
NBLK = 32


NORM_EPS = 1e-05
DPO_BETA = 0.02
ROPE_BASE = 10000.0
ADAM_ONE = 0.9
ADAM_TWO = 0.999
ADAM_EPS = 1e-08
WEIGHT_DECAY = 0.01
GAIN_RATE = 0.3
STAT_DECAY = 0.5
SHAMPOO_RATE = 0.5
MASKED = -1e30


def joined(value, axis, join):
    pieces = jax.tree.map(lambda part: lax.all_gather(part, axis), value)
    head = jax.tree.map(lambda part: part[0], pieces)
    tail = jax.tree.map(lambda part: part[1:], pieces)
    so_far, _ = lax.scan(lambda so_far, section: (join(so_far, section), None), head, tail)
    return so_far


def mult(left, right):
    return jnp.dot(left, right, preferred_element_type=jnp.float32)


def mult_t(left, right):
    return lax.dot_general(
        left, right, (((0,), (0,)), ((), ())), preferred_element_type=jnp.float32
    )


def mult_nt(left, right):
    return lax.dot_general(
        left, right, (((1,), (1,)), ((), ())), preferred_element_type=jnp.float32
    )


def project(rows, group):
    product = jnp.einsum("td,ndk->tnk", rows, group, preferred_element_type=jnp.float32)
    return product.reshape(rows.shape[0], group.shape[0] * BC)


def project_back(grad, group):
    return jnp.einsum(
        "tnk,ndk->td",
        grad.reshape(grad.shape[0], group.shape[0], BC),
        group,
        preferred_element_type=jnp.float32,
    )


def block_grad(rows, grad, number):
    return jnp.einsum(
        "td,tnk->ndk",
        rows,
        grad.reshape(grad.shape[0], number, BC),
        preferred_element_type=jnp.float32,
    )


def down_forward(mix, down):
    row_total = mix.shape[0]
    product = jnp.einsum(
        "trd,rjdk->tjk",
        mix.reshape(row_total, FF // D, D),
        down.reshape(FF // D, D // BC, D, BC),
        preferred_element_type=jnp.float32,
    )
    return product.reshape(row_total, D)


def down_back(grad, down):
    row_total = grad.shape[0]
    product = jnp.einsum(
        "tjk,rjdk->trd",
        grad.reshape(row_total, D // BC, BC),
        down.reshape(FF // D, D // BC, D, BC),
        preferred_element_type=jnp.float32,
    )
    return product.reshape(row_total, FF)


def down_grad(mix, grad):
    row_total = mix.shape[0]
    product = jnp.einsum(
        "trd,tjk->rjdk",
        mix.reshape(row_total, FF // D, D),
        grad.reshape(row_total, D // BC, BC),
        preferred_element_type=jnp.float32,
    )
    return product.reshape(-1, D, BC)


def groups(weights):
    col_blocks = D // BC
    ff_blocks = FF // BC
    base_gate = 4 * col_blocks
    return (
        weights[0:col_blocks],
        weights[col_blocks : 2 * col_blocks],
        weights[2 * col_blocks : 3 * col_blocks],
        weights[3 * col_blocks : base_gate],
        weights[base_gate : base_gate + ff_blocks],
        weights[base_gate + ff_blocks : base_gate + 2 * ff_blocks],
        weights[base_gate + 2 * ff_blocks :],
    )


def rms_forward(values, gain):
    return values * lax.rsqrt(jnp.mean(values * values, axis=-1, keepdims=True) + NORM_EPS) * gain


def rms_backward(values, gain, grad):
    scale = lax.rsqrt(jnp.mean(values * values, axis=-1, keepdims=True) + NORM_EPS)
    inner = jnp.mean(values * gain * grad, axis=-1, keepdims=True)
    back = scale * gain * grad - values * scale**3 * inner
    return (back, jnp.sum(grad * values * scale, axis=0))


def angles():
    inv_freq = ROPE_BASE ** (-jnp.arange(HDIM // 2).astype(jnp.float32) * 2.0 / HDIM)
    phase_grid = jnp.arange(SLOT).astype(jnp.float32)[:, None] * inv_freq[None, :]
    return (jnp.cos(phase_grid), jnp.sin(phase_grid))


def rotate(values, cosine, sine, direction):
    half_dim = HDIM // 2
    lead_half = values[..., :half_dim]
    tail_half = values[..., half_dim:]
    cos_grid = cosine[None, :, None, :]
    sin_grid = direction * sine[None, :, None, :]
    return jnp.concatenate(
        [lead_half * cos_grid - tail_half * sin_grid, tail_half * cos_grid + lead_half * sin_grid],
        axis=-1,
    )


def attend_scores(q_rot, k_rot, len_vec):
    raw = jnp.einsum(
        "nqhd,nkhd->nhqk", q_rot, k_rot, preferred_element_type=jnp.float32
    ) / math.sqrt(HDIM)
    places = jnp.arange(SLOT)
    valid = (places[None, :] <= places[:, None])[None, None] & (
        places[None, None, None, :] < len_vec[:, None, None, None]
    )
    return jnp.where(valid, raw, MASKED)


def layer_forward(inputs, len_vec, gains, mats, cosine, sine):
    w_query, w_key, w_value, w_out, w_gate, w_up, w_down = mats
    seq_count = inputs.shape[0] // SLOT

    def to_heads(values):
        return values.reshape(seq_count, SLOT, HEADS, HDIM)

    a_low = rms_forward(inputs, gains[0]).astype(jnp.bfloat16)
    q_rot = rotate(to_heads(project(a_low, w_query)), cosine, sine, 1.0).astype(jnp.bfloat16)
    k_rot = rotate(to_heads(project(a_low, w_key)), cosine, sine, 1.0).astype(jnp.bfloat16)
    v_heads = to_heads(project(a_low, w_value)).astype(jnp.bfloat16)
    scores = attend_scores(q_rot, k_rot, len_vec)
    row_max = jnp.max(scores, axis=-1, keepdims=True)
    log_total = jnp.log(jnp.sum(jnp.exp(scores - row_max), axis=-1, keepdims=True)) + row_max
    p_low = jnp.exp(scores - log_total).astype(jnp.bfloat16)
    att_out = jnp.einsum("nhqk,nkhd->nqhd", p_low, v_heads, preferred_element_type=jnp.float32)
    att_out = att_out.reshape(seq_count * SLOT, D).astype(jnp.bfloat16)
    h_mid = inputs + project(att_out, w_out)
    b_low = rms_forward(h_mid, gains[1]).astype(jnp.bfloat16)
    gate_pre = project(b_low, w_gate)
    up_pre = project(b_low, w_up)
    mix_low = (jax.nn.silu(gate_pre) * up_pre).astype(jnp.bfloat16)
    h_out = h_mid + down_forward(mix_low, w_down)
    return (
        h_out,
        (a_low, q_rot, k_rot, v_heads, log_total, att_out, h_mid, b_low, gate_pre, up_pre, mix_low),
    )


def layer_backward(inputs, len_vec, gains, mats, cosine, sine, saved, grad_out):
    w_query, w_key, w_value, w_out, w_gate, w_up, w_down = mats
    a_low, q_rot, k_rot, v_heads, log_total, att_out, h_mid, b_low, gate_pre, up_pre, mix_low = (
        saved
    )
    seq_count = inputs.shape[0] // SLOT
    grad_branch = grad_out.astype(jnp.bfloat16)
    grad_mix = down_back(grad_branch, w_down)
    sigmoid_gate = jax.nn.sigmoid(gate_pre)
    grad_gate = (grad_mix * up_pre * sigmoid_gate * (1.0 + gate_pre * (1.0 - sigmoid_gate))).astype(
        jnp.bfloat16
    )
    grad_up = (grad_mix * gate_pre * sigmoid_gate).astype(jnp.bfloat16)
    grad_b = project_back(grad_gate, w_gate) + project_back(grad_up, w_up)
    back_mid, gain_mid = rms_backward(h_mid, gains[1], grad_b)
    grad_mid = grad_out + back_mid
    grad_attn = grad_mid.astype(jnp.bfloat16)
    grad_att = (
        project_back(grad_attn, w_out).astype(jnp.bfloat16).reshape(seq_count, SLOT, HEADS, HDIM)
    )
    p_full = jnp.exp(attend_scores(q_rot, k_rot, len_vec) - log_total)
    grad_p = jnp.einsum("nqhd,nkhd->nhqk", grad_att, v_heads, preferred_element_type=jnp.float32)
    grad_s = (p_full * (grad_p - jnp.sum(p_full * grad_p, axis=-1, keepdims=True))).astype(
        jnp.bfloat16
    )
    grad_q = jnp.einsum(
        "nhqk,nkhd->nqhd", grad_s, k_rot, preferred_element_type=jnp.float32
    ) / math.sqrt(HDIM)
    grad_k = jnp.einsum(
        "nhqk,nqhd->nkhd", grad_s, q_rot, preferred_element_type=jnp.float32
    ) / math.sqrt(HDIM)
    grad_v = jnp.einsum(
        "nhqk,nqhd->nkhd", p_full.astype(jnp.bfloat16), grad_att, preferred_element_type=jnp.float32
    )
    row_total = seq_count * SLOT
    grad_q = rotate(grad_q, cosine, sine, -1.0).reshape(row_total, D).astype(jnp.bfloat16)
    grad_k = rotate(grad_k, cosine, sine, -1.0).reshape(row_total, D).astype(jnp.bfloat16)
    grad_v = grad_v.reshape(row_total, D).astype(jnp.bfloat16)
    grad_a = (
        project_back(grad_q, w_query) + project_back(grad_k, w_key) + project_back(grad_v, w_value)
    )
    back_in, gain_in = rms_backward(inputs, gains[0], grad_a)
    operands = (
        a_low,
        grad_q,
        grad_k,
        grad_v,
        att_out,
        grad_attn,
        b_low,
        grad_gate,
        grad_up,
        mix_low,
        grad_branch,
    )
    return (grad_mid + back_in, operands, jnp.stack([gain_in, gain_mid]))


def weight_grads(operands):
    (
        a_low,
        grad_q,
        grad_k,
        grad_v,
        att_out,
        grad_attn,
        b_low,
        grad_gate,
        grad_up,
        mix_low,
        grad_branch,
    ) = operands
    col_blocks = D // BC
    ff_blocks = FF // BC
    return jnp.concatenate(
        [
            block_grad(a_low, grad_q, col_blocks),
            block_grad(a_low, grad_k, col_blocks),
            block_grad(a_low, grad_v, col_blocks),
            block_grad(att_out, grad_attn, col_blocks),
            block_grad(b_low, grad_gate, ff_blocks),
            block_grad(b_low, grad_up, ff_blocks),
            down_grad(mix_low, grad_branch),
        ],
        axis=0,
    )


def combine_parts(earlier, later):
    max_one, sum_one, pick_one = earlier
    max_two, sum_two, pick_two = later
    joint_max = jnp.maximum(max_one, max_two)
    joint_sum = sum_one * jnp.exp(max_one - joint_max) + sum_two * jnp.exp(max_two - joint_max)
    return (joint_max, joint_sum, pick_one + pick_two)


def adam_step(weight, grad, moment, second, rate):
    moment = ADAM_ONE * moment + (1.0 - ADAM_ONE) * grad
    second = ADAM_TWO * second + (1.0 - ADAM_TWO) * grad * grad
    ratio = moment / (1.0 - ADAM_ONE**STEP) / (jnp.sqrt(second / (1.0 - ADAM_TWO**STEP)) + ADAM_EPS)
    return (weight - rate * (ratio + WEIGHT_DECAY * weight), moment, second)


def per_device(
    dp,
    vocab,
    token_ids,
    lengths,
    comp_mask,
    ref_logp,
    owner,
    blocks,
    left_stat,
    right_stat,
    left_root,
    right_root,
    tables,
    table_moment,
    table_second,
    gains,
    gain_moment,
    gain_second,
):
    vocab_count = lax.axis_size(vocab)
    vocab_index = lax.axis_index(vocab)
    row_share = blocks.shape[1]
    cosine, sine = angles()
    tables_low = lax.all_gather(tables.astype(jnp.bfloat16), dp, axis=1, tiled=True)
    vocab_rows = tables_low.shape[1]
    local_ids = token_ids.reshape(-1) - vocab_index * vocab_rows
    inside = (local_ids >= 0) & (local_ids < vocab_rows)
    safe_ids = jnp.clip(local_ids, 0, vocab_rows - 1)
    looked = jnp.where(inside[:, None], jnp.take(tables_low[0], safe_ids, axis=0), 0).astype(
        jnp.float32
    )
    embedded = lax.psum_scatter(
        looked.astype(jnp.bfloat16), vocab, scatter_dimension=0, tiled=True
    ).astype(jnp.float32)
    rows_all = lax.all_gather(blocks.astype(jnp.bfloat16), vocab, axis=1, tiled=True)
    slots_all = lax.all_gather(rows_all, dp, axis=0, tiled=True)
    kept_mats = groups(jnp.take(slots_all, owner, axis=0))
    gain_total = jnp.zeros((3, D), jnp.float32)
    loss_own = jnp.zeros((), jnp.float32)
    grad_inputs = []
    operand_list = []
    logit_grads = []
    head_inputs = []
    for micro in range(MB):
        own_pair = vocab_index * MB + micro
        rows_in = embedded[micro * 2 * SLOT : (micro + 1) * 2 * SLOT]
        len_own = lax.dynamic_index_in_dim(lengths, own_pair, 0, keepdims=False)
        h_out, saved = layer_forward(rows_in, len_own, gains, kept_mats, cosine, sine)
        pos_own = len_own[:, None] - 1 - CMP + jnp.arange(CMP)[None, :]
        picked_rows = jnp.take_along_axis(
            h_out.reshape(2, SLOT, D), pos_own[:, :, None], axis=1
        ).reshape(2 * CMP, D)
        c_low = rms_forward(picked_rows, gains[2]).astype(jnp.bfloat16)
        all_rows = lax.all_gather(c_low, vocab, axis=0, tiled=True)
        ids_sel = token_ids[micro::MB]
        lens_sel = lengths[micro::MB]
        mask_sel = comp_mask[micro::MB].astype(jnp.float32)
        ref_sel = ref_logp[micro::MB]
        pos_sel = lens_sel[:, :, None] - 1 - CMP + jnp.arange(CMP)[None, None, :]
        target = (
            jnp.take_along_axis(ids_sel, pos_sel + 1, axis=2).reshape(-1) - vocab_index * vocab_rows
        )
        logits = mult_nt(all_rows, tables_low[1])
        one_hot = jnp.arange(vocab_rows)[None, :] == target[:, None]
        row_max = jnp.max(logits, axis=1)
        row_sum = jnp.sum(jnp.exp(logits - row_max[:, None]), axis=1)
        row_pick = jnp.sum(jnp.where(one_hot, logits, 0.0), axis=1)
        full_max, full_sum, full_pick = joined((row_max, row_sum, row_pick), vocab, combine_parts)
        log_norm = full_max + jnp.log(full_sum)
        seq_logp = jnp.sum((full_pick - log_norm).reshape(vocab_count, 2, CMP) * mask_sel, axis=2)
        margin = DPO_BETA * (seq_logp[:, 0] - ref_sel[:, 0] - (seq_logp[:, 1] - ref_sel[:, 1]))
        loss_own = loss_own + jnp.take(jax.nn.softplus(-margin), vocab_index)
        pair_weight = -DPO_BETA * jax.nn.sigmoid(-margin)
        grad_tok = (jnp.stack([pair_weight, -pair_weight], axis=1)[:, :, None] * mask_sel).reshape(
            -1
        )
        grad_logits = (
            grad_tok[:, None] * (one_hot.astype(jnp.float32) - jnp.exp(logits - log_norm[:, None]))
        ).astype(jnp.bfloat16)
        logit_grads.append(grad_logits)
        head_inputs.append(all_rows)
        grad_c = lax.psum_scatter(
            mult(grad_logits, tables_low[1]), vocab, scatter_dimension=0, tiled=True
        )
        back_rows, gain_head = rms_backward(picked_rows, gains[2], grad_c)
        seq_index = jnp.arange(2)[:, None]
        grad_top = (
            jnp.zeros((2, SLOT, D), jnp.float32)
            .at[seq_index, pos_own]
            .add(back_rows.reshape(2, CMP, D))
        )
        grad_in, operands, gains_now = layer_backward(
            rows_in, len_own, gains, kept_mats, cosine, sine, saved, grad_top.reshape(2 * SLOT, D)
        )
        operand_list.append(operands)
        gain_total = gain_total + jnp.concatenate([gains_now, gain_head[None]], axis=0)
        grad_inputs.append(grad_in)
    joined_ops = tuple(
        (
            jnp.concatenate([ops[i] for ops in operand_list], axis=0)
            for i in range(len(operand_list[0]))
        )
    )
    block_order = weight_grads(joined_ops)
    grad_head = mult_t(jnp.concatenate(logit_grads, axis=0), jnp.concatenate(head_inputs, axis=0))
    grad_rows = lax.all_gather(
        jnp.concatenate(grad_inputs, axis=0).astype(jnp.bfloat16), vocab, axis=0, tiled=True
    ).astype(jnp.float32)
    grad_embed = (
        jnp.zeros((vocab_rows, D), jnp.float32)
        .at[safe_ids]
        .add(jnp.where(inside[:, None], grad_rows, 0.0))
    )
    table_grad = lax.psum_scatter(
        jnp.stack([grad_embed, grad_head]).astype(jnp.bfloat16),
        dp,
        scatter_dimension=1,
        tiled=True,
    ).astype(jnp.float32)
    inverse = jnp.zeros((NBLK,), jnp.int32).at[owner].set(jnp.arange(NBLK, dtype=jnp.int32))
    slotted = jnp.take(block_order, inverse, axis=0)
    summed = lax.psum_scatter(slotted.astype(jnp.bfloat16), dp, scatter_dimension=0, tiled=True)
    share_part = lax.psum_scatter(summed, vocab, scatter_dimension=1, tiled=True).astype(
        jnp.float32
    )
    whole = lax.all_gather(share_part.astype(jnp.bfloat16), vocab, axis=1, tiled=True).astype(
        share_part.dtype
    )
    highest = lax.Precision.HIGHEST
    new_left = STAT_DECAY * left_stat + (1.0 - STAT_DECAY) * jnp.einsum(
        "bij,bkj->bik", whole, whole, precision=highest
    )
    new_right = STAT_DECAY * right_stat + (1.0 - STAT_DECAY) * jnp.einsum(
        "bji,bjk->bik", whole, whole, precision=highest
    )
    direction = jnp.einsum("bij,bjk->bik", left_root, whole, precision=highest)
    direction = jnp.einsum("bij,bjk->bik", direction, right_root, precision=highest)
    new_blocks = blocks - SHAMPOO_RATE * lax.dynamic_slice_in_dim(
        direction, vocab_index * row_share, row_share, 1
    )
    loss_sum, gain_grad = lax.psum((loss_own, gain_total), dp + vocab)
    rates = jnp.array([0.3, 0.02], jnp.float32)[:, None, None]
    new_tables, new_table_moment, new_table_second = adam_step(
        tables, table_grad, table_moment, table_second, rates
    )
    new_gains, new_gain_moment, new_gain_second = adam_step(
        gains, gain_grad, gain_moment, gain_second, GAIN_RATE
    )
    return (
        new_blocks,
        share_part,
        new_left,
        new_right,
        new_tables,
        new_table_moment,
        new_table_second,
        new_gains,
        new_gain_moment,
        new_gain_second,
        loss_sum,
    )


PAIR_ROWS = MB * 2 * CMP
TOKENS = MB * 2 * SLOT
CAP = 24
CAP_BACK = 18
MSG = 32
EXT = D + 128
AXES = ("z", "x", "y", "core")
SHARD_AXES = ("y", "core", "z", "x")
VMEM_LIMIT = 60 * 1024 * 1024

AT_A = 0
AT_AP = AT_A + TOKENS
AT_O = AT_AP + PAIR_ROWS
AT_B = AT_O + PAIR_ROWS
AT_Z = AT_B + PAIR_ROWS
LEFT_ROWS = AT_Z + (FF // D) * PAIR_ROWS
LEFT_KINDS = (LEFT_ROWS - AT_AP) // PAIR_ROWS
AT_DK = 0
AT_DV = AT_DK + TOKENS
AT_DQ = AT_DV + TOKENS
AT_DO = AT_DQ + PAIR_ROWS
AT_DGATE = AT_DO + PAIR_ROWS
AT_DUP = AT_DGATE + (FF // D) * PAIR_ROWS
AT_DH = AT_DUP + (FF // D) * PAIR_ROWS
RIGHT_ROWS = AT_DH + PAIR_ROWS


def flat_of(z, x, y, c):
    return ((z * 2 + x) * 2 + y) * 2 + c


def moves(target):
    pairs = []
    for z in range(4):
        for x in range(2):
            for y in range(2):
                for c in range(2):
                    pairs.append((flat_of(z, x, y, c), flat_of(*target(z, x, y, c))))
    return pairs


def hop_one(value):
    return lax.ppermute(
        value,
        AXES,
        moves(lambda z, x, y, c: (z, 1 - x, y, c) if c == 0 else (z, x, 1 - y, c)),
    )


def hop_two(value):
    return lax.ppermute(
        value,
        AXES,
        moves(lambda z, x, y, c: (z, x, 1 - y, c) if c == 0 else (z, 1 - x, y, c)),
    )


def hop_core(value):
    return lax.ppermute(value, AXES, moves(lambda z, x, y, c: (z, x, y, 1 - c)))


def hop_y(value):
    return lax.ppermute(value, AXES, moves(lambda z, x, y, c: (z, x, 1 - y, c)))


def ring(value, step):
    return lax.ppermute(value, AXES, moves(lambda z, x, y, c: ((z + step) % 4, x, y, c)))


def after(value, *others):
    return lax.optimization_barrier((value,) + others)[0]


def together(*values):
    return lax.optimization_barrier(values)


def all_round(chunk):
    return jnp.stack([chunk] + [ring(chunk, step) for step in range(1, 4)])


def spread(chunk, wait=()):
    if wait:
        chunk = after(chunk, *wait)
    around = [ring(chunk, step) for step in range(1, 4)]
    line = jnp.stack([chunk] + around)
    one = hop_one(line)
    two = hop_two(line)
    both = hop_two(one)
    return jnp.stack([line, one, two, both]), around


def dot_nn(left, right):
    return lax.dot_general(left, right, (((1,), (0,)), ((), ())), preferred_element_type=jnp.float32)


def dot_nt(left, right):
    return lax.dot_general(left, right, (((1,), (1,)), ((), ())), preferred_element_type=jnp.float32)


def dot_tn(left, right):
    return lax.dot_general(left, right, (((0,), (0,)), ((), ())), preferred_element_type=jnp.float32)


def low(value):
    return value.astype(jnp.bfloat16)


def high(value):
    return value.astype(jnp.float32)


def place_of(coord, other_core, rel):
    core = coord[3] + other_core * (1 - 2 * coord[3])
    first = rel & 1
    second = rel >> 1
    x_flip = first + core * (second - first)
    y_flip = second + core * (first - second)
    x = coord[1] + x_flip * (1 - 2 * coord[1])
    y = coord[2] + y_flip * (1 - 2 * coord[2])
    return x, y, core


def start_weights(coord, parts, held, sem):
    def start(source, slots, y, core):
        row = pl.multiple_of(192 * (2 * y + core), 64)
        pltpu.make_async_copy(source, held.at[slots, pl.ds(row, 192)], sem).start()

    for other_core in range(2):
        for rel in range(4):
            x, y, core = place_of(coord, other_core, rel)
            pair, third, last = (
                parts[2 * rel + other_core],
                parts[8 + 2 * rel + other_core],
                parts[16 + other_core],
            )

            def one(n, carry):
                back = (coord[0] + 4 - n) & 3
                start(pair.at[n], pl.ds(8 * n + 4 * x, 2), y, core)
                start(third.at[n], 8 * back + 4 * x + 2, y, core)
                start(last.at[n, rel], 8 * n + 4 * x + 3, y, core)
                return carry

            lax.fori_loop(0, 4, one, 0)


def wait_weights(held, sem):
    pltpu.make_async_copy(held, held, sem).wait()


def iota(shape, axis):
    return lax.broadcasted_iota(jnp.int32, shape, axis)


def pick_rows(lens):
    row = iota((PAIR_ROWS, 1), 0)
    seq = row >> 4
    length = jnp.where(
        seq == 0, lens[0], jnp.where(seq == 1, lens[1], jnp.where(seq == 2, lens[2], lens[3]))
    )
    return seq, length - 1 - CMP + (row & 15)


def masks(lens):
    seq, pos = pick_rows(lens)
    col = iota((PAIR_ROWS, TOKENS), 1)
    same = (col >> 6) == seq
    key = col & 63
    return same & (key <= pos), same & (key == pos)


def both_heads(chunk, first):
    zero = jnp.zeros(chunk.shape, chunk.dtype)
    return jnp.concatenate([jnp.where(first, chunk, zero), jnp.where(first, zero, chunk)], axis=0)


def own_lanes(stacked, first):
    return jnp.where(first, stacked[:PAIR_ROWS], stacked[PAIR_ROWS:])


def probabilities(queries, keys, valid):
    s = dot_nt(queries, keys) * (1.0 / math.sqrt(HDIM))
    s = jnp.where(valid, s, MASKED)
    e = jnp.exp(s - jnp.max(s, axis=-1, keepdims=True))
    return e / jnp.sum(e, axis=-1, keepdims=True)


def turn(chunk, cosine, sine, sign):
    lane = iota(chunk.shape, 1)
    swapped = jnp.where((lane & 63) < 32, pltpu.roll(chunk, 96, 1), pltpu.roll(chunk, 32, 1))
    return chunk * cosine + swapped * (sine * sign)


def scale_of(values):
    return lax.rsqrt(jnp.mean(values * values, axis=-1, keepdims=True) + NORM_EPS)


def rms_back(values, gain, grad):
    scale = scale_of(values)
    inner = jnp.mean(values * gain * grad, axis=-1, keepdims=True)
    back = scale * gain * grad - values * (scale * scale * scale) * inner
    return back, jnp.sum(grad * values * scale, axis=0, keepdims=True)


def forward_kernel(owner, coord, lens, x, gains, cos_q, sin_q, cos_k, sin_k, *rest):
    parts, rest = rest[:18], rest[18:]
    left, q_out, k_out, v_out, h1_out, gate_out, up_out, h2_out, c_out = rest[:9]
    held, sem = rest[9:]
    start_weights(coord, parts, held, sem)
    values = high(x[...])
    a_low = low(values * scale_of(values) * gains[0:1, :])
    left[AT_A:AT_AP] = a_low
    valid, chosen = masks(lens)
    select = jnp.where(chosen, 1.0, 0.0).astype(jnp.bfloat16)
    a_pick = low(dot_nn(select, a_low))
    left[AT_AP:AT_O] = a_pick
    x_pick = dot_nn(select, x[...])
    wait_weights(held, sem)
    for j in range(2):
        q = dot_nn(a_pick, held[owner[j]])
        k = dot_nn(a_low, held[owner[2 + j]])
        v_out[:, j * BC : (j + 1) * BC] = low(dot_nn(a_low, held[owner[4 + j]]))
        for i in range(3):
            at = slice(j * BC + i * 128, j * BC + (i + 1) * 128)
            q_out[:, at] = low(turn(q[:, i * 128 : (i + 1) * 128], cos_q[...], sin_q[...], 1.0))
            k_out[:, at] = low(turn(k[:, i * 128 : (i + 1) * 128], cos_k[...], sin_k[...], 1.0))
    first = iota((PAIR_ROWS, 128), 1) < HDIM
    valid = jnp.concatenate([valid, valid], axis=0)
    for p in range(HEADS // 2):
        at = slice(p * 128, (p + 1) * 128)
        prob = low(probabilities(both_heads(q_out[:, at], first), k_out[:, at], valid))
        left[AT_O:AT_B, at] = low(own_lanes(dot_nn(prob, v_out[:, at]), first))
    for j in range(2):
        at = slice(j * BC, (j + 1) * BC)
        h1_out[:, at] = x_pick[:, at] + dot_nn(left[AT_O:AT_B], held[owner[6 + j]])
    h1 = h1_out[...]
    b_low = low(h1 * scale_of(h1) * gains[1:2, :])
    left[AT_B:AT_Z] = b_low
    for j in range(FF // BC):
        at = slice(j * BC, (j + 1) * BC)
        gate = dot_nn(b_low, held[owner[8 + j]])
        up = dot_nn(b_low, held[owner[16 + j]])
        gate_out[:, at] = gate
        up_out[:, at] = up
        row = AT_Z + j // 2 * PAIR_ROWS
        left[row : row + PAIR_ROWS, j % 2 * BC : (j % 2 + 1) * BC] = low(
            gate * jax.nn.sigmoid(gate) * up
        )
    for j in range(2):
        total = h1[:, j * BC : (j + 1) * BC]
        for r in range(FF // D):
            row = AT_Z + r * PAIR_ROWS
            total = total + dot_nn(left[row : row + PAIR_ROWS], held[owner[24 + 2 * r + j]])
        h2_out[:, j * BC : (j + 1) * BC] = total
    h2 = h2_out[...]
    c_out[...] = low(h2 * scale_of(h2) * gains[2:3, :])


def vmem(number):
    return [pl.BlockSpec(memory_space=pltpu.VMEM)] * number


def smem(number):
    return [pl.BlockSpec(memory_space=pltpu.SMEM)] * number


def anywhere(number):
    return [pl.BlockSpec(memory_space=pl.ANY)] * number


def forward_call(owner, coord, lens, x, gains, turns, parts):
    def made(rows, columns, kind):
        return jax.ShapeDtypeStruct((rows, columns), kind)

    return pl.pallas_call(
        forward_kernel,
        out_shape=(
            made(LEFT_ROWS, D, jnp.bfloat16),
            made(PAIR_ROWS, D, jnp.bfloat16),
            made(TOKENS, D, jnp.bfloat16),
            made(TOKENS, D, jnp.bfloat16),
            made(PAIR_ROWS, D, jnp.float32),
            made(PAIR_ROWS, FF, jnp.float32),
            made(PAIR_ROWS, FF, jnp.float32),
            made(PAIR_ROWS, D, jnp.float32),
            made(PAIR_ROWS, D, jnp.bfloat16),
        ),
        in_specs=smem(3) + vmem(6) + anywhere(18),
        out_specs=tuple(vmem(9)),
        scratch_shapes=[
            pltpu.VMEM((NBLK, D, BC), jnp.bfloat16),
            pltpu.SemaphoreType.DMA,
        ],
        compiler_params=pltpu.CompilerParams(vmem_limit_bytes=VMEM_LIMIT),
        name="layer_forward",
    )(owner, coord, lens, x, gains, *turns, *parts)


def unpack(ext):
    stat = high(ext[:, D:EXT])
    top = (stat[:, 0:1] + stat[:, 1:2]) + stat[:, 2:3]
    total = (stat[:, 3:4] + stat[:, 4:5]) + stat[:, 5:6]
    return top, total, high(ext[:, :D])


def pack_stat(top, total):
    lane = iota((top.shape[0], 128), 1)
    out = jnp.zeros((top.shape[0], 128), jnp.float32)
    for first, value in ((0, top), (3, total)):
        for i in range(3):
            piece = high(low(value))
            out = jnp.where(lane == first + i, piece, out)
            value = value - piece
    return low(out)


def merge(items):
    top = items[0][0]
    for item in items[1:]:
        top = jnp.maximum(top, item[0])
    total = 0.0
    mixed = 0.0
    for item_top, item_total, item_mixed in items:
        factor = jnp.exp(item_top - top)
        total = total + item_total * factor
        mixed = mixed + item_mixed * factor
    return top, total, mixed


def merge_kernel(number, *refs):
    top, total, mixed = merge([unpack(ref[...]) for ref in refs[:number]])
    mixed = low(mixed)
    stat = pack_stat(top, total)
    outs = refs[number:]
    rows = outs[0].shape[0]
    for n, out in enumerate(outs):
        out[:, :D] = mixed[n * rows : (n + 1) * rows]
        out[:, D:EXT] = stat[n * rows : (n + 1) * rows]


def merge_call(parts, pieces=1):
    rows = 4 * PAIR_ROWS
    made = jax.ShapeDtypeStruct((rows // pieces, EXT), jnp.bfloat16)
    return pl.pallas_call(
        functools.partial(merge_kernel, len(parts)),
        grid=(1,),
        out_shape=(made,) * pieces,
        in_specs=[pl.BlockSpec((rows, EXT), lambda i, at=at: (at, 0)) for _, at in parts],
        out_specs=(pl.BlockSpec(made.shape, lambda i: (0, 0)),) * pieces,
        compiler_params=pltpu.CompilerParams(vmem_limit_bytes=VMEM_LIMIT),
        cost_estimate=pl.CostEstimate(
            flops=8 * rows * D, bytes_accessed=4 * rows * EXT, transcendentals=rows
        ),
        name="merge_parts",
    )(*[array for array, _ in parts])


def head_kernel(real, rows, head, ext, kept, stat):
    logits = dot_nt(rows[...], head[...])
    whole = head.shape[0] - 128
    end = logits[:, whole:]
    end = jnp.where(iota(end.shape, 1) < real - whole, end, MASKED)
    logits = jnp.concatenate([logits[:, :whole], end], axis=1)
    top = jnp.max(logits, axis=-1, keepdims=True)
    e = jnp.exp(logits - top)
    total = jnp.sum(e, axis=-1, keepdims=True)
    e_low = low(e)
    kept[...] = e_low
    ext[:, :D] = low(dot_nn(e_low, head[...]))
    ext[:, D:EXT] = pack_stat(top, total)
    stat[...] = jnp.broadcast_to(top, stat.shape)


def head_call(rows, head, real):
    number, wide = rows.shape[0], head.shape[0]
    block = number // 2
    return pl.pallas_call(
        functools.partial(head_kernel, real),
        grid=(number // block,),
        out_shape=(
            jax.ShapeDtypeStruct((number, EXT), jnp.bfloat16),
            jax.ShapeDtypeStruct((number, wide), jnp.bfloat16),
            jax.ShapeDtypeStruct((number, 128), jnp.float32),
        ),
        in_specs=[
            pl.BlockSpec((block, D), lambda i: (i, 0)),
            pl.BlockSpec((wide, D), lambda i: (0, 0)),
        ],
        out_specs=(
            pl.BlockSpec((block, EXT), lambda i: (i, 0)),
            pl.BlockSpec((block, wide), lambda i: (i, 0)),
            pl.BlockSpec((block, 128), lambda i: (i, 0)),
        ),
        compiler_params=pltpu.CompilerParams(vmem_limit_bytes=VMEM_LIMIT),
        cost_estimate=pl.CostEstimate(
            flops=4 * number * wide * D, bytes_accessed=2 * number * wide, transcendentals=number * wide
        ),
        name="head_forward",
    )(rows, head)


def head_grad_kernel(steps, rows_a, rows_b, kept_a, kept_b, stat_a, stat_b, info, out):
    def add(rows, kept, stat):
        weight = info[:, 0:1]
        factor = weight * jnp.exp(stat[:, 0:1] - info[:, 1:2])
        col = iota(kept.shape, 1)
        hit = col == info[:, 2:3].astype(jnp.int32)
        grad = low(jnp.where(hit, weight, 0.0) - high(kept[...]) * factor)
        return dot_tn(grad, rows[...])

    i = pl.program_id(0)

    @pl.when(i == 0)
    def _():
        out[...] = add(rows_a, kept_a, stat_a)

    @pl.when((i > 0) & (i < steps))
    def _():
        out[...] += add(rows_a, kept_a, stat_a)

    @pl.when(i >= steps)
    def _():
        out[...] += add(rows_b, kept_b, stat_b)


def head_grad_call(rows, kept, stat, info):
    number, wide = kept[0].shape
    steps = number // 256

    def pair(columns):
        return [
            pl.BlockSpec((256, columns), lambda i: (jnp.minimum(i, steps - 1), 0)),
            pl.BlockSpec((256, columns), lambda i: (jnp.maximum(i - steps, 0), 0)),
        ]

    return pl.pallas_call(
        functools.partial(head_grad_kernel, steps),
        grid=(2 * steps,),
        out_shape=jax.ShapeDtypeStruct((wide, D), jnp.float32),
        in_specs=pair(D) + pair(wide) + pair(128) + [pl.BlockSpec((256, 128), lambda i: (i, 0))],
        out_specs=pl.BlockSpec((wide, D), lambda i: (0, 0)),
        compiler_params=pltpu.CompilerParams(vmem_limit_bytes=VMEM_LIMIT),
        cost_estimate=pl.CostEstimate(
            flops=4 * number * wide * D, bytes_accessed=4 * number * wide, transcendentals=number
        ),
        name="head_grad",
    )(*rows, *kept, *stat, info)


def backward_kernel(owner, coord, lens, refs, x, gains, cos_q, sin_q, cos_k, sin_k, *rest):
    q, k, v, h1, gate, up, h2, c = rest[:8]
    truth, wanted, u0, u1, u2, u3 = rest[8:14]
    parts = rest[14:32]
    act, dx_out, gain_out, info_out, loss_out = rest[32:37]
    held, sem = rest[37:]
    start_weights(coord, parts, held, sem)
    valid, chosen = masks(lens)
    select = jnp.where(chosen, 1.0, 0.0).astype(jnp.bfloat16)
    top, total, mixed = merge([unpack(part[...]) for part in (u0, u1, u2, u3)])
    norm = top + jnp.log(total)
    target = high(truth[...])
    picked = jnp.sum(high(c[...]) * target, axis=-1, keepdims=True)
    scored = wanted[:, 0:1]
    terms = (picked - norm) * scored
    seq = iota((PAIR_ROWS, 1), 0) >> 4
    logp = [jnp.sum(jnp.where(seq == n, terms, 0.0), axis=0, keepdims=True) for n in range(2 * MB)]
    weight = jnp.zeros((PAIR_ROWS, 1), jnp.float32)
    loss = jnp.zeros((1, 1), jnp.float32)
    for n in range(MB):
        margin = DPO_BETA * ((logp[2 * n] - refs[2 * n]) - (logp[2 * n + 1] - refs[2 * n + 1]))
        loss = loss + jnp.maximum(-margin, 0.0) + jnp.log1p(jnp.exp(-jnp.abs(margin)))
        slope = -DPO_BETA * jax.nn.sigmoid(-margin)
        weight = jnp.where(seq == 2 * n, slope, jnp.where(seq == 2 * n + 1, -slope, weight))
    weight = weight * scored
    loss_out[...] = jnp.broadcast_to(loss, loss_out.shape)
    lane = iota((PAIR_ROWS, 128), 1)
    info_out[...] = jnp.where(
        lane == 0, weight, jnp.where(lane == 1, norm, jnp.where(lane == 2, wanted[:, 1:2], 0.0))
    )
    grad_c = weight * (target - mixed / total)
    d2, gain_top = rms_back(h2[...], gains[2:3, :], grad_c)
    gain_out[2:3, :] = gain_top
    d2_low = low(d2)
    act[AT_DH:RIGHT_ROWS] = d2_low
    wait_weights(held, sem)
    grad_b = jnp.zeros((PAIR_ROWS, D), jnp.float32)
    for r in range(FF // D):
        grad_mix = dot_nt(d2_low[:, :BC], held[owner[24 + 2 * r]]) + dot_nt(
            d2_low[:, BC:], held[owner[25 + 2 * r]]
        )
        at = slice(r * D, (r + 1) * D)
        gate_pre = gate[:, at]
        sig = jax.nn.sigmoid(gate_pre)
        d_gate = low(grad_mix * up[:, at] * sig * (1.0 + gate_pre * (1.0 - sig)))
        d_up = low(grad_mix * gate_pre * sig)
        act[AT_DGATE + r * PAIR_ROWS : AT_DGATE + (r + 1) * PAIR_ROWS] = d_gate
        act[AT_DUP + r * PAIR_ROWS : AT_DUP + (r + 1) * PAIR_ROWS] = d_up
        for j in range(2):
            cut = slice(j * BC, (j + 1) * BC)
            grad_b = grad_b + dot_nt(d_gate[:, cut], held[owner[8 + 2 * r + j]])
            grad_b = grad_b + dot_nt(d_up[:, cut], held[owner[16 + 2 * r + j]])
    back, gain_mid = rms_back(h1[...], gains[1:2, :], grad_b)
    gain_out[1:2, :] = gain_mid
    d1 = d2 + back
    d1_low = low(d1)
    act[AT_DO:AT_DGATE] = d1_low
    d_att = low(
        dot_nt(d1_low[:, :BC], held[owner[6]]) + dot_nt(d1_low[:, BC:], held[owner[7]])
    )
    root = 1.0 / math.sqrt(HDIM)
    first = lane < HDIM
    valid = jnp.concatenate([valid, valid], axis=0)
    for p in range(HEADS // 2):
        at = slice(p * 128, (p + 1) * 128)
        queries = both_heads(q[:, at], first)
        grads = both_heads(d_att[:, at], first)
        prob = probabilities(queries, k[:, at], valid)
        d_p = dot_nt(grads, v[:, at])
        d_s = low(prob * (d_p - jnp.sum(prob * d_p, axis=-1, keepdims=True)))
        d_q = own_lanes(dot_nn(d_s, k[:, at]), first)
        d_k = dot_tn(d_s, queries)
        d_v = dot_tn(low(prob), grads)
        act[AT_DQ:AT_DO, at] = low(turn(d_q * root, cos_q[...], sin_q[...], -1.0))
        act[AT_DK:AT_DV, at] = low(turn(d_k * root, cos_k[...], sin_k[...], -1.0))
        act[AT_DV:AT_DQ, at] = low(d_v)
    d_q_all = low(dot_tn(select, act[AT_DQ:AT_DO]))
    grad_a = jnp.zeros((TOKENS, D), jnp.float32)
    for j in range(2):
        cut = slice(j * BC, (j + 1) * BC)
        grad_a = grad_a + dot_nt(d_q_all[:, cut], held[owner[j]])
        grad_a = grad_a + dot_nt(act[AT_DK:AT_DV, cut], held[owner[2 + j]])
        grad_a = grad_a + dot_nt(act[AT_DV:AT_DQ, cut], held[owner[4 + j]])
    back_in, gain_in = rms_back(high(x[...]), gains[0:1, :], grad_a)
    gain_out[0:1, :] = gain_in
    rest_low = low(d1 - high(d1_low))
    dx_out[...] = low(back_in + dot_tn(select, d1_low) + dot_tn(select, rest_low))


def backward_call(owner, coord, lens, refs, x, gains, turns, saved, truth, wanted, parts_u, parts):
    return pl.pallas_call(
        backward_kernel,
        out_shape=(
            jax.ShapeDtypeStruct((RIGHT_ROWS, D), jnp.bfloat16),
            jax.ShapeDtypeStruct((TOKENS, D), jnp.bfloat16),
            jax.ShapeDtypeStruct((3, D), jnp.float32),
            jax.ShapeDtypeStruct((PAIR_ROWS, 128), jnp.float32),
            jax.ShapeDtypeStruct((1, 128), jnp.float32),
        ),
        in_specs=smem(4) + vmem(6 + 8 + 2 + 4) + anywhere(18),
        out_specs=tuple(vmem(5)),
        scratch_shapes=[
            pltpu.VMEM((NBLK, D, BC), jnp.bfloat16),
            pltpu.SemaphoreType.DMA,
        ],
        compiler_params=pltpu.CompilerParams(vmem_limit_bytes=VMEM_LIMIT),
        name="layer_backward",
    )(owner, coord, lens, refs, x, gains, *turns, *saved, truth, wanted, *parts_u, *parts)


def transpose_kernel(coord, mine, theirs, picked, tokens, turned_a, turned_b):
    near_row = pl.multiple_of(192 * (2 * coord[2] + coord[3]), 64)
    far_row = pl.multiple_of(192 * (2 * (1 - coord[2]) + coord[3]), 64)
    for n in range(LEFT_KINDS):
        at = slice(AT_AP + n * PAIR_ROWS, AT_AP + (n + 1) * PAIR_ROWS)
        turned_a[...] = jnp.concatenate([mine[at], theirs[at]], axis=0).T
        picked[n, :192] = turned_a[pl.ds(near_row, 192), :]
        picked[n, 192:] = turned_a[pl.ds(far_row, 192), :]
    turned_b[:, :TOKENS] = mine[AT_A:AT_AP].T
    turned_b[:, TOKENS:] = theirs[AT_A:AT_AP].T
    tokens[:192] = turned_b[pl.ds(near_row, 192), :]
    tokens[192:] = turned_b[pl.ds(far_row, 192), :]


def transpose_call(coord, mine, theirs):
    return pl.pallas_call(
        transpose_kernel,
        out_shape=(
            jax.ShapeDtypeStruct((LEFT_KINDS, 384, 2 * PAIR_ROWS), jnp.bfloat16),
            jax.ShapeDtypeStruct((384, 2 * TOKENS), jnp.bfloat16),
        ),
        in_specs=smem(1) + vmem(2),
        out_specs=tuple(vmem(2)),
        scratch_shapes=[
            pltpu.VMEM((D, 2 * PAIR_ROWS), jnp.bfloat16),
            pltpu.VMEM((D, 2 * TOKENS), jnp.bfloat16),
        ],
        compiler_params=pltpu.CompilerParams(vmem_limit_bytes=VMEM_LIMIT),
        cost_estimate=pl.CostEstimate(
            flops=0, bytes_accessed=8 * LEFT_ROWS * D, transcendentals=0
        ),
        name="left_transposed",
    )(coord, mine, theirs)


def weight_grad_kernel(block_of, x_at, y_at, coord, picked, tokens, mine, theirs, *rest):
    outs = rest[:-3]
    near_held, far_held, sem = rest[-3:]
    first = coord[3] == 0
    for group, (k, x_flip) in enumerate((k, x_flip) for k in range(4) for x_flip in range(2)):
        x = coord[1] + x_flip * (1 - 2 * coord[1])

        def step(n, carry):
            z = n if k != 2 else (coord[0] + 4 - n) & 3
            slot = 8 * z + 4 * x + k
            block = block_of[slot]
            cut = pl.ds(pl.multiple_of((block & 1) * BC, 128), BC)
            y_row = pl.multiple_of(y_at[slot], 64)

            def put(left, rows):
                right = jnp.concatenate(
                    [mine[pl.ds(y_row, rows), cut], theirs[pl.ds(y_row, rows), cut]], axis=0
                )
                grad = low(dot_nn(left, right))
                near_held[group, n] = grad[:192]
                far_held[group, n] = grad[192:]

            wide = (block >= 2) & (block < 6)

            @pl.when(wide)
            def _():
                put(tokens[...], TOKENS)

            @pl.when(jnp.logical_not(wide))
            def _():
                put(picked[x_at[slot]], PAIR_ROWS)

            return carry

        lax.fori_loop(0, 4, step, 0)

        def send(held, rel):
            if k == 3:
                target = outs[8].at[:, rel]
            elif k == 2:
                target = outs[4 + rel]
            else:
                target = outs[rel].at[:, k]
            pltpu.make_async_copy(held.at[group], target, sem).start()

        if x_flip == 0:
            send(near_held, 0)
            side = far_held
        else:
            send(far_held, 3)
            side = near_held

        @pl.when(first == (x_flip == 1))
        def _():
            send(side, 1)

        @pl.when(first == (x_flip == 0))
        def _():
            send(side, 2)

    pltpu.make_async_copy(near_held, near_held, sem).wait()
    pltpu.make_async_copy(far_held, far_held, sem).wait()


def weight_grad_call(*args):
    shapes = [(4, 2)] * 4 + [(4,)] * 4 + [(4, 4)]
    made = [jax.ShapeDtypeStruct(shape + (192, BC), jnp.bfloat16) for shape in shapes]
    held = pltpu.VMEM((8, 4, 192, BC), jnp.bfloat16)
    return pl.pallas_call(
        weight_grad_kernel,
        out_shape=tuple(made),
        in_specs=smem(4) + vmem(4),
        out_specs=tuple(anywhere(len(made))),
        scratch_shapes=[held, held, pltpu.SemaphoreType.DMA],
        compiler_params=pltpu.CompilerParams(vmem_limit_bytes=VMEM_LIMIT),
        name="weight_grads",
    )(*args)


def shampoo_kernel(coord, *refs):
    own, by_y, by_core, by_both, lstat, rstat, lroot, rroot, blk = refs[:9]
    new_b, grad_out, new_l, new_r, whole = refs[-5:]
    y, core = coord[2], coord[3]
    for piece, y_at, core_at in (
        (own, y, core),
        (by_y, 1 - y, core),
        (by_core, y, 1 - core),
        (by_both, 1 - y, 1 - core),
    ):
        row = pl.multiple_of(192 * (2 * y_at + core_at), 64)
        whole[pl.ds(row, 192), :] = piece[0]
    grad_out[0] = high(own[0])
    grad = whole[...]
    new_l[0] = STAT_DECAY * lstat[0] + (1.0 - STAT_DECAY) * dot_nt(grad, grad)
    new_r[0] = STAT_DECAY * rstat[0] + (1.0 - STAT_DECAY) * dot_tn(grad, grad)
    turned = dot_nn(low(lroot[0]), grad)
    new_b[0] = blk[0] - SHAMPOO_RATE * dot_nn(low(turned), low(rroot[0]))


def shampoo_call(start, coord, pieces, lstat, rstat, lroot, rroot, blk, so_far):
    def one(rows, columns):
        return pl.BlockSpec((1, rows, columns), lambda i, coord: (start + i, 0, 0))

    slots = pieces[0].shape[0]
    in_specs = (
        [pl.BlockSpec((1, 192, BC), lambda i, coord: (i, 0, 0))] * 4
        + [
            one(D, D),
            one(BC, BC),
            pl.BlockSpec((1, 192, D), lambda i, coord: (start + i, 2 * coord[2] + coord[3], 0)),
            one(BC, BC),
            one(192, BC),
        ]
        + anywhere(len(so_far))
    )
    return pl.pallas_call(
        shampoo_kernel,
        grid_spec=pltpu.PrefetchScalarGridSpec(
            num_scalar_prefetch=1,
            grid=(slots,),
            in_specs=in_specs,
            out_specs=(one(192, BC), one(192, BC), one(D, D), one(BC, BC)),
            scratch_shapes=[pltpu.VMEM((D, BC), jnp.bfloat16)],
        ),
        out_shape=(
            jax.ShapeDtypeStruct(blk.shape, jnp.float32),
            jax.ShapeDtypeStruct(blk.shape, jnp.float32),
            jax.ShapeDtypeStruct(lstat.shape, jnp.float32),
            jax.ShapeDtypeStruct(rstat.shape, jnp.float32),
        ),
        input_output_aliases={10 + n: n for n in range(len(so_far))},
        compiler_params=pltpu.CompilerParams(vmem_limit_bytes=VMEM_LIMIT),
        cost_estimate=pl.CostEstimate(
            flops=4 * slots * D * D * BC,
            bytes_accessed=8 * slots * 1024 * 1024,
            transcendentals=0,
        ),
        name="shampoo",
    )(coord, *pieces, lstat, rstat, lroot, rroot, blk, *so_far)


def adam_kernel(rate, grad, w, m, v, *rest):
    new_w, new_m, new_v = rest[-3:]
    new_w[0], new_m[0], new_v[0] = adam_step(w[0], grad[...], m[0], v[0], rate)


def adam_call(table, rate, grad, w, m, v, so_far):
    rows = w.shape[1]
    block = next(n for n in (200, 40, 8) if rows % n == 0)
    spec = pl.BlockSpec((1, block, D), lambda j: (table, j, 0))
    return pl.pallas_call(
        functools.partial(adam_kernel, rate),
        grid=(rows // block,),
        out_shape=(jax.ShapeDtypeStruct(w.shape, jnp.float32),) * 3,
        in_specs=[pl.BlockSpec((block, D), lambda j: (j, 0)), spec, spec, spec]
        + anywhere(len(so_far)),
        out_specs=(spec,) * 3,
        input_output_aliases={4 + n: n for n in range(len(so_far))},
        compiler_params=pltpu.CompilerParams(vmem_limit_bytes=VMEM_LIMIT),
        cost_estimate=pl.CostEstimate(
            flops=10 * rows * D, bytes_accessed=28 * rows * D, transcendentals=rows * D
        ),
        name="adam",
    )(grad, w, m, v, *so_far)


def block_rows():
    x_at, y_at = [], []
    for b in range(NBLK):
        if b < 2:
            x_at.append(0), y_at.append(AT_DQ)
        elif b < 4:
            x_at.append(0), y_at.append(AT_DK)
        elif b < 6:
            x_at.append(0), y_at.append(AT_DV)
        elif b < 8:
            x_at.append(1), y_at.append(AT_DO)
        elif b < 16:
            x_at.append(2), y_at.append(AT_DGATE + (b - 8) // 2 * PAIR_ROWS)
        elif b < 24:
            x_at.append(2), y_at.append(AT_DUP + (b - 16) // 2 * PAIR_ROWS)
        else:
            x_at.append(3 + (b - 24) // 2), y_at.append(AT_DH)
    return jnp.array(x_at, jnp.int32), jnp.array(y_at, jnp.int32)


def per_core(
    token_ids,
    lengths,
    comp_mask,
    ref_logp,
    owner,
    blocks,
    left_stat,
    right_stat,
    left_root,
    right_root,
    tables,
    table_moment,
    table_second,
    gains,
    gain_moment,
    gain_second,
):
    zi, xi, yi, ci = (lax.axis_index(name) for name in AXES)
    coord = jnp.stack([zi, xi, yi, ci]).astype(jnp.int32)
    vocab_index = 2 * yi + ci
    shard = vocab_index * 8 + 2 * zi + xi
    table_rows = tables.shape[1]
    vocab = table_rows * 32
    seqs = 2 * MB
    shares = blocks.astype(jnp.bfloat16)
    with jax.named_scope("weights_last"):
        one, two = hop_one(shares[3]), hop_two(shares[3])
        last = jnp.stack([shares[3], one, two, hop_two(one)])
    with jax.named_scope("weights_third"):
        line3 = all_round(shares[2])
    with jax.named_scope("weights_pair"):
        line = lax.all_gather(shares[:2], "z")
    first_pair = vocab_index * MB
    ids = lax.dynamic_slice_in_dim(token_ids, first_pair, MB, 0).reshape(seqs, SLOT)
    lens = lax.dynamic_slice_in_dim(lengths, first_pair, MB, 0).reshape(seqs)
    wanted = lax.dynamic_slice_in_dim(comp_mask, first_pair, MB, 0).reshape(PAIR_ROWS)
    refs = lax.dynamic_slice_in_dim(ref_logp, first_pair, MB, 0).reshape(seqs)
    places = jnp.arange(SLOT)
    pos = (lens[:, None] - 1 - CMP + jnp.arange(CMP)[None, :]).astype(jnp.int32)
    targets = jnp.sum(
        jnp.where(places[None, None, :] == (pos + 1)[:, :, None], ids[:, None, :], 0), axis=-1
    ).reshape(PAIR_ROWS)
    asked = jnp.concatenate([ids.reshape(TOKENS), targets + vocab])
    used = jnp.concatenate(
        [(places[None, :] < lens[:, None]).reshape(TOKENS), jnp.ones((PAIR_ROWS,), bool)]
    )
    number = jnp.where(asked >= vocab, asked - vocab, asked)
    holder = number // table_rows
    local_row = number - holder * table_rows + jnp.where(asked >= vocab, table_rows, 0)
    total = asked.shape[0]
    earlier = jnp.arange(total)[None, :] < jnp.arange(total)[:, None]
    same = (asked[:, None] == asked[None, :]) & used[:, None] & used[None, :]
    first = used & jnp.logical_not(jnp.any(same & earlier, axis=1))
    rank = jnp.sum(
        ((holder[:, None] == holder[None, :]) & earlier & first[None, :]).astype(jnp.int32), axis=1
    )
    most = jnp.where(jnp.arange(total) < TOKENS, CAP_BACK, CAP)
    spill = jnp.any(first & (rank >= most))
    seat_first = jnp.where(first & (rank < CAP), holder * CAP + rank, -1)
    seat = jnp.sum(jnp.where(same & first[None, :], seat_first[None, :] + 1, 0), axis=1) - 1
    seats = jnp.arange(32 * CAP)
    request = jnp.sum(
        jnp.where(seat_first[:, None] == seats[None, :], local_row[:, None], 0), axis=0
    )
    message = jnp.concatenate(
        [
            request.reshape(32, CAP),
            jnp.broadcast_to(spill.astype(jnp.int32), (32, MSG - CAP)),
        ],
        axis=1,
    )
    message = lax.all_to_all(message, SHARD_AXES, 0, 0, tiled=True)
    line3, last, message = together(line3, last, message)
    any_spill = jnp.max(message[:, MSG - 1]) > 0
    asked_rows = message[:, :CAP].reshape(32 * CAP)
    table_low = tables.astype(jnp.bfloat16).reshape(2 * table_rows, D)
    give = (asked_rows[:, None] == jnp.arange(2 * table_rows)[None, :]).astype(jnp.bfloat16)
    given = low(dot_nn(give, table_low))
    with jax.named_scope("weights_third"):
        one3, two3 = hop_one(line3), hop_two(line3)
    one3, two3, given, line, last = together(one3, two3, given, line, last)
    got = lax.all_to_all(given, SHARD_AXES, 0, 0, tiled=True)
    with jax.named_scope("weights_last"):
        last = lax.all_gather(last, "z")
    with jax.named_scope("weights_third"):
        third = [line3, one3, two3, hop_two(one3)]
    with jax.named_scope("weights_pair"):
        one, two = hop_one(line), hop_two(line)
    early = [hop_core(part) for part in third[:3] + [line]]
    one, two, third[3], *early = together(one, two, third[3], *early)
    with jax.named_scope("weights_pair"):
        pair = [line, one, two, hop_two(one)]
    place = (seat[:, None] == seats[None, :]).astype(jnp.bfloat16)
    rows = low(dot_nn(place, got))
    x, truth = rows[:TOKENS], rows[TOKENS:]
    inv_freq = ROPE_BASE ** (-jnp.arange(HDIM // 2).astype(jnp.float32) * 2.0 / HDIM)
    phase = places.astype(jnp.float32)[:, None] * inv_freq[None, :]
    phase_pick = pos.reshape(PAIR_ROWS).astype(jnp.float32)[:, None] * inv_freq[None, :]

    def turning(angle, repeat):
        cosine, sine = jnp.cos(angle), jnp.sin(angle)
        return (
            jnp.tile(jnp.concatenate([cosine] * 4, axis=1), (repeat, 1)),
            jnp.tile(jnp.concatenate([-sine, sine, -sine, sine], axis=1), (repeat, 1)),
        )

    turns = turning(phase_pick, 1) + turning(phase, seqs)
    middle = [hop_core(part) for part in (one, two, third[3])]
    last, *middle = together(last, *middle, x, truth, *turns)[:4]
    parts = []
    early += middle
    for n, part in enumerate(pair + third + [last]):
        place_of_early = {0: 3, 4: 0, 5: 1, 6: 2, 1: 4, 2: 5, 7: 6}.get(n)
        parts.append(part)
        parts.append(hop_core(part) if place_of_early is None else early[place_of_early])
    left, *saved = forward_call(owner, coord, lens, x, gains, turns, parts)
    plane, _ = spread(saved[-1])
    plane = plane.reshape(-1, D)
    other = hop_core(plane)
    left_t = transpose_call(coord, left, hop_core(left))
    wide = -(-table_rows // 128) * 128
    head_low = jnp.pad(table_low[table_rows:], ((0, wide - table_rows), (0, 0)))
    ext_other, kept_other, stat_other = head_call(other, head_low, table_rows)
    ext_hop = hop_core(ext_other)
    ext_own, kept_own, stat_own = head_call(plane, head_low, table_rows)
    both = merge_call([(ext_own, 3), (ext_hop, 3)])[0]
    two = merge_call([(ext_own, 2), (ext_hop, 2)])[0]
    one = merge_call([(ext_own, 1), (ext_hop, 1), (hop_two(both), 0)])[0]
    pieces = merge_call([(ext_own, 0), (ext_hop, 0), (hop_one(one), 0), (hop_two(two), 0)], 4)
    pieces = lax.optimization_barrier(tuple(pieces) + tuple(left_t))[:4]
    parts_u = [pieces[0]] + [ring(pieces[step], -step) for step in range(1, 4)]
    marks = jnp.stack([wanted.astype(jnp.float32), targets.astype(jnp.float32)], axis=1)
    marks = jnp.pad(marks, ((0, 0), (0, 126)))
    act, dx, gain_part, info, loss_part = backward_call(
        owner, coord, lens, refs, x, gains, turns, saved, truth, marks, parts_u, parts
    )
    inverse = jnp.sum(
        jnp.where(
            owner[None, :] == jnp.arange(NBLK)[:, None], jnp.arange(NBLK, dtype=jnp.int32)[None, :], 0
        ),
        axis=1,
    )
    x_at, y_at = block_rows()
    chosen = (inverse[:, None] == jnp.arange(NBLK)[None, :]).astype(jnp.int32)
    grad_args = (
        inverse,
        jnp.sum(chosen * x_at[None, :], axis=1),
        jnp.sum(chosen * y_at[None, :], axis=1),
        coord,
        *left_t,
        act,
        hop_core(act),
    )

    def plus(*values):
        return low(sum(high(value) for value in values))

    grads = weight_grad_call(*grad_args)
    info, gain_part, loss_part, dx, *grads = together(info, gain_part, loss_part, dx, *grads)
    own, one, two, both = grads[:4]
    own3, one3, two3, both3, ends = grads[4:]
    with jax.named_scope("grads_pair"):
        one = plus(one, hop_two(both))
    with jax.named_scope("grads_last"):
        last = lax.psum_scatter(
            ends.reshape(16, 192, BC), "z", scatter_dimension=0, tiled=True
        )
    back = place[:TOKENS].reshape(TOKENS, 32, CAP)[:, :, :CAP_BACK].reshape(TOKENS, 32 * CAP_BACK)
    sent = low(dot_tn(back, dx))
    told = info[:, :3].reshape(-1)
    known = told.shape[0]
    told = jnp.concatenate([told, gain_part.reshape(-1), loss_part[0]])
    told = jnp.broadcast_to(told[None], (32, told.shape[0]))
    heard = lax.all_to_all(told, AXES, 0, 0, tiled=True)
    with jax.named_scope("grads_pair"):
        two = hop_two(two)
    one, two, both3, sent, heard = together(one, two, both3, sent, heard)
    with jax.named_scope("grads_pair"):
        line = plus(own, hop_one(one), two).reshape(8, 192, BC)
    with jax.named_scope("grads_third"):
        one3 = plus(one3, hop_two(both3))
    back_rows = lax.all_to_all(sent, SHARD_AXES, 0, 0, tiled=True)
    summed = jnp.sum(heard[:, known:], axis=0)
    sources = []
    for other_core in range(2):
        for rel in range(4):
            for back in range(4):
                sources.append(
                    flat_of((zi + 4 - back) % 4, *place_of((zi, xi, yi, ci), other_core, rel))
                )
    sources = jnp.stack(sources)
    infos = jnp.sum(
        jnp.where(
            (sources[:, None] == jnp.arange(32)[None, :])[:, :, None],
            heard[None, :, :known],
            0.0,
        ),
        axis=1,
    ).reshape(-1, 3)
    infos = jnp.concatenate(
        [infos[:, :2], infos[:, 2:3] - (shard * table_rows).astype(jnp.float32)], axis=1
    )
    infos = jnp.pad(infos, ((0, 0), (0, 125)))
    grad_head = head_grad_call(
        (plane, other), (kept_own, kept_other), (stat_own, stat_other), infos
    )
    adam = adam_call(1, 0.02, grad_head, tables, table_moment, table_second, ())
    line, one3, two3, last, *adam = together(line, one3, two3, last, *adam)
    with jax.named_scope("grads_pair"):
        pair = lax.psum_scatter(line, "z", scatter_dimension=0, tiled=True)
    with jax.named_scope("grads_third"):
        one3, two3 = hop_one(one3), hop_two(two3)
        line3 = [plus(own3[n], one3[n], two3[n]) for n in range(4)]
    with jax.named_scope("grads_last"):
        one, two = plus(last[1], hop_two(last[3])), hop_two(last[2])
    back_at = message[:, :CAP_BACK].reshape(32 * CAP_BACK)
    take_back = (back_at[None, :] == jnp.arange(table_rows)[:, None]).astype(jnp.bfloat16)
    grad_embed = dot_nn(take_back, back_rows)
    new_tables, new_table_moment, new_table_second = adam_call(
        0, 0.3, grad_embed, tables, table_moment, table_second, adam
    )
    new_gains, new_gain_moment, new_gain_second = adam_step(
        gains, summed[: 3 * D].reshape(3, D), gain_moment, gain_second, GAIN_RATE
    )
    loss_sum = summed[3 * D]
    one, two, new_tables, new_gains, new_gain_moment, new_gain_second, *line3 = together(
        one, two, new_tables, new_gains, new_gain_moment, new_gain_second, *line3
    )
    pair_y = hop_y(pair)
    with jax.named_scope("grads_third"):
        around = [ring(line3[step], -step) for step in range(1, 4)]
        third = plus(after(line3[0], pair_y), *around)
    with jax.named_scope("grads_last"):
        last = plus(last[0], hop_one(one), two)

    rights = (left_stat, right_stat, left_root, right_root, blocks)
    late = jnp.stack([third, last])
    late_y = hop_y(late)
    results = shampoo_call(
        0, coord, (pair, pair_y, hop_core(pair), hop_core(pair_y)), *rights, ()
    )
    late_y, *results = together(late_y, *results)
    new_blocks, block_grads, new_left, new_right = shampoo_call(
        2, coord, (late, late_y, hop_core(late), hop_core(late_y)), *rights, results
    )
    quick = (
        new_blocks,
        block_grads,
        new_left,
        new_right,
        new_tables,
        new_table_moment,
        new_table_second,
        new_gains,
        new_gain_moment,
        new_gain_second,
        loss_sum,
    )
    whole = (
        token_ids,
        lengths,
        comp_mask,
        ref_logp,
        owner,
        blocks,
        left_stat,
        right_stat,
        left_root,
        right_root,
        tables,
        table_moment,
        table_second,
        gains,
        gain_moment,
        gain_second,
    )

    def slow(state):
        outs = list(per_device(("z", "x"), ("y", "core"), *whole))
        outs[1] = with_layout_constraint(outs[1], Layout((0, 1, 2)))
        return jnp.zeros((), bool), tuple(outs)

    return lax.while_loop(lambda state: state[0], slow, (any_spill, quick))[1]


def solution(mesh):
    tuned = mesh.shape["dp"] == 8 and mesh.shape["vocab"] == 4
    if tuned:
        dp, vocab = ("z", "x"), ("y", "core")
        where = Mesh(mesh.devices.reshape(4, 2, 2, 2), AXES)
        body = per_core
    else:
        dp, vocab = ("dp",), ("vocab",)
        where = mesh
        body = functools.partial(per_device, ("dp",), ("vocab",))
    placed = (
        P(dp, None, None),
        P(dp, None),
        P(dp, None, None),
        P(dp, None),
        P(),
        P(dp, vocab, None),
        P(dp, None, None),
        P(dp, None, None),
        P(dp, None, None),
        P(dp, None, None),
        P(None, vocab + dp, None),
        P(None, vocab + dp, None),
        P(None, vocab + dp, None),
        P(),
        P(),
        P(),
    )
    return jax.shard_map(
        body,
        mesh=where,
        in_specs=placed,
        out_specs=(
            P(dp, vocab, None),
            P(dp, vocab, None),
            P(dp, None, None),
            P(dp, None, None),
            P(None, vocab + dp, None),
            P(None, vocab + dp, None),
            P(None, vocab + dp, None),
            P(),
            P(),
            P(),
            P(),
        ),
        check_vma=False,
    )
```
